128 devices in a mesh: tp: 4 (over y), ep: 8 (over x, core), etp: 4 (over z).
Axes of the slice: x: 4, y: 4, z: 4, core: 2. Of those that a mesh axis runs over, the one named last changes fastest.
Arguments:
- queries: bfloat16 [4096, 6144], P(('ep', 'etp'), 'tp'), may hold values from -128 to 128
- keys: bfloat16 [4096, 1024], P(('ep', 'etp'), 'tp'), may hold values from -4.5 to 4.5
- values: bfloat16 [4096, 1024], P(('ep', 'etp'), 'tp'), may hold values from -6 to 6
- residual: bfloat16 [32, 4, 32, 6144], P(('ep', 'etp'), 'tp'), may hold values from -6 to 6
- norm_gain: float32 [6144], replicated, may hold values from 0.1 to 1.9
- out_weight: bfloat16 [6144, 6144], P('tp', 'etp'), may hold values from -0.078125 to 0.078125
- gate_weight: bfloat16 [8, 6144, 8192], P('ep', None, ('tp', 'etp')), may hold values from -0.078125 to 0.078125
- up_weight: bfloat16 [8, 6144, 8192], P('ep', None, ('tp', 'etp')), may hold values from -0.078125 to 0.078125
- down_weight: bfloat16 [8, 8192, 6144], P('ep', ('tp', 'etp')), may hold values from -0.0625 to 0.0625
- expert_ids: int32 [32, 4, 32, 2], P(('ep', 'etp'), 'tp'), may hold values from 0 to 7, all different within a row; in each aligned block of 32 rows (0 to 31, 32 to 63, ..., all dimensions but the last counted through in order) at most 10 rows name the same one
- route_weights: float32 [32, 4, 32, 2], P(('ep', 'etp'), 'tp'), may hold values from 0.1 to 1
Outputs:
- attention: bfloat16 [4096, 6144], P(('ep', 'etp'), 'tp')
- mixed: bfloat16 [32, 4, 32, 6144], P(('ep', 'etp'), 'tp')
The draws below stay inside these ranges and needn't reach their ends.
Inputs may be any that keep to these rules, and one draw needn't show every extreme that they name: `expert_ids`: the 2 picks of a token differ; in each routing group of 32 tokens (the rows of one device) no expert is named by more than 10 tokens, a bound that some block reaches.
All inputs are finite; a program needn't handle non-finite values.
Results may differ from the reference program's by a relative error of at most 0.013.
Values may be sent and summed in bfloat16 or wider, within the bound.
No kernel may reach another device: no remote copies, remote signals or barrier semaphores. Data moves between devices by JAX's collectives and lax.ppermute only.
A program may use at most 192 MiB of HBM per device.

```python
import math
import jax
import jax.numpy as jnp
import numpy as np
from jax import lax

D = 6144
H = 48
KV = 8
HD = 128
HIDW = 8192
TOP = 2
TOK_DEV = 128
EXPERTS = 8
BLOCKS = 32
TOKENS = 4096
MOE_TOK = 32
CAP = 10
N_TP = 4
N_ETP = 4


def paired_draw(key, boost):
    key_query, key_key = jax.random.split(key, 2)
    base_keys = jax.random.truncated_normal(key_key, -4.5, 4.5, (TOKENS, KV, HD), jnp.float32)
    drawn_queries = 2.0 * jax.random.truncated_normal(key_query, -4.5, 4.5, (TOKENS, H, HD), jnp.float32)
    positions = jnp.arange(TOKENS, dtype=jnp.int32)
    chosen = jnp.where(positions % 61 == 7, boost, 0.0)
    phase = positions // 61 % 3
    level = jnp.where(phase == 0, 9.0, jnp.where(phase == 1, 15.0, 27.0))
    earlier = jnp.roll(base_keys, 1, axis=0)
    aligned = level[:, None, None] * jnp.repeat(earlier, H // KV, axis=1)
    nearby = earlier * (1.0 - 2.0 / (level * math.sqrt(HD)))[:, None, None]
    mixing = chosen[:, None, None]
    queries = drawn_queries + mixing * (aligned - drawn_queries)
    keys = base_keys + mixing * (nearby - base_keys)
    return (queries.reshape(TOKENS, H * HD), keys.reshape(TOKENS, KV * HD))


def draw_queries(key, part):
    boost = 0.0
    return paired_draw(key, boost)[0].astype(jnp.bfloat16)


def draw_keys(key, part):
    boost = 0.0
    return paired_draw(key, boost)[1].astype(jnp.bfloat16)


def block_levels(key, extent, cuts, low, high):
    def one(dim, shards_of):
        heights = jax.random.uniform(jax.random.fold_in(jax.random.fold_in(key, 6), dim), (shards_of,), jnp.float32, low / len(cuts), high / len(cuts))
        return jnp.repeat(jnp.exp(heights), extent[dim] // shards_of).reshape((-1,) + (1,) * (len(extent) - dim - 1))

    loudness = one(*cuts[0])
    for cut in cuts[1:]:
        loudness = loudness * one(*cut)
    return loudness


def routed_block(key, own, number, rows, count, top, reach, skew):
    ranking = jax.random.permutation(key, count)
    heavy_load, ordinary = shares(count, rows * top, reach, skew, True), shares(count, rows * top, reach, skew, False)
    places = jnp.arange(count)

    def named(tallies, offset_by):
        used = int((tallies > 0).sum())
        fixed = max(1, used // 4)
        passed = fixed + (places - fixed + offset_by * (used - fixed)) % max(1, count - fixed)
        return jnp.zeros((count,), jnp.int32).at[ranking[jnp.where(places < fixed, places, passed)]].set(jnp.asarray(tallies, jnp.int32))

    tallies = jnp.where(number % 4 == 0, named(heavy_load, number // 4), named(ordinary, number - number // 4 - 1))
    mixed = jax.random.permutation(jax.random.fold_in(own, 3), count)
    source_of, sink = mixed[0:count // 2 * 2:2], mixed[1:count // 2 * 2:2]
    room = jnp.minimum(tallies[source_of] - 1, reach - tallies[sink]) // 2
    room = jnp.where((source_of == ranking[0]) | (sink == ranking[0]) | (tallies[sink] == 0), 0, jnp.maximum(room, 0))
    passed = jax.random.randint(jax.random.fold_in(own, 4), (count // 2,), 0, 1 << 20) % (room + 1)
    tallies = tallies.at[source_of].add(-passed).at[sink].add(passed)
    labels = jnp.searchsorted(jnp.cumsum(tallies), jnp.arange(rows * top), side="right").astype(jnp.int32)
    table = labels.reshape(top, rows).T
    table = table[jax.random.permutation(jax.random.fold_in(own, 1), rows)]
    offset_by = jax.random.randint(jax.random.fold_in(own, 2), (rows, 1), 0, top)
    return jnp.take_along_axis(table, (jnp.arange(top)[None, :] + offset_by) % top, axis=1)


def shares(number_of, total, bound, slope, full):
    portions = [(1 << 20) // math.isqrt(grade ** slope) + 1 for grade in range(1, number_of + 1)]
    largest = bound if full else min(bound, max(-(-total // number_of), total * portions[0] // sum(portions)))
    least = 1 if total - largest >= number_of - 1 else 0
    counts, spare = [largest] + [least] * (number_of - 1), total - largest - least * (number_of - 1)
    while spare > 0:
        movable = [i for i in range(1, number_of) if counts[i] < largest] or [i for i in range(1, number_of) if counts[i] < bound]
        whole, budget = sum([portions[i] for i in movable]), spare
        for i in movable:
            more = min(bound - counts[i], max(1, budget * portions[i] // whole), spare)
            counts[i] = counts[i] + more
            spare = spare - more
    return np.array(counts)


def gaussian(rng, dims, spread, bound, cuts=(), held_as=jnp.bfloat16):
    factor_of = block_levels(rng, dims, cuts, -0.22, 0.18) if cuts else 1.0
    values = jax.random.normal(rng, dims, jnp.float32) * spread * factor_of
    return jnp.minimum(jnp.maximum(values, -bound), bound).astype(held_as)


def setup_inputs(seed: int = 0) -> dict:
    seeds = jax.random.split(jax.random.key(seed), 12)
    queries = draw_queries(jax.random.fold_in(seeds[11], 71), 0)
    keys = draw_keys(jax.random.fold_in(seeds[11], 71), 0)
    values = gaussian(seeds[2], (TOKENS, KV * HD), 1.0, 6.0, ((0, 32), (1, 4)))
    residual = gaussian(seeds[3], (BLOCKS, N_TP, MOE_TOK, D), 1.0, 6.0, ((0, 32), (1, 4)))
    norm_gain = jnp.clip(1.0 + 0.18 * jax.random.normal(seeds[4], (D,), jnp.float32), 0.1, 1.9)
    out_weight = gaussian(seeds[5], (H * HD, D), (H * HD) ** -0.5, 0.078125, ((0, 4), (1, 4)))
    gate_weight = gaussian(seeds[6], (EXPERTS, D, HIDW), D ** -0.5, 0.078125, ((0, 8), (2, 16)))
    up_weight = gaussian(seeds[7], (EXPERTS, D, HIDW), D ** -0.5, 0.078125, ((0, 8), (2, 16)))
    down_weight = gaussian(seeds[8], (EXPERTS, HIDW, D), HIDW ** -0.5, 0.0625, ((0, 8), (1, 16)))
    expert_ids_keys = jax.random.split(jax.random.fold_in(seeds[9], 1), BLOCKS * N_TP * MOE_TOK // MOE_TOK)
    expert_ids_turns = jax.random.permutation(jax.random.fold_in(seeds[9], 3), BLOCKS * N_TP * MOE_TOK // MOE_TOK)
    expert_ids = jax.vmap(lambda own, number: routed_block(jax.random.fold_in(seeds[9], 2), own, number, MOE_TOK, EXPERTS, TOP, CAP, 1))(expert_ids_keys, expert_ids_turns).reshape((BLOCKS, N_TP, MOE_TOK, TOP))
    route_weights = jnp.clip(jnp.exp(math.log(1.0) - 2.3025851 * jax.random.uniform(seeds[10], (BLOCKS, N_TP, MOE_TOK, TOP), jnp.float32) ** block_levels(seeds[10], (BLOCKS, N_TP, MOE_TOK, TOP), ((0, 32), (1, 4)), -0.2, 0.2)), 0.1, 1.0)
    return {"queries": queries, "keys": keys, "values": values, "residual": residual, "norm_gain": norm_gain, "out_weight": out_weight, "gate_weight": gate_weight, "up_weight": up_weight, "down_weight": down_weight, "expert_ids": expert_ids, "route_weights": route_weights}


def route_tables(ids, weights, experts, cap):
    tokens, top = ids.shape
    flat = ids.reshape(-1)
    hot = (flat[:, None] == jnp.arange(experts, dtype=jnp.int32)[None, :]).astype(jnp.int32)
    rank = jnp.cumsum(hot, axis=0) - hot
    slot = lax.optimization_barrier(jnp.sum(rank * hot, axis=1)).reshape(tokens, top)
    same_expert = ids[None, None, :, :] == jnp.arange(experts, dtype=jnp.int32)[:, None, None, None]
    same_slot = slot[None, None, :, :] == jnp.arange(cap, dtype=jnp.int32)[None, :, None, None]
    match = jnp.where(same_expert & same_slot, 1.0, 0.0).astype(jnp.float32)
    dispatch = lax.optimization_barrier(jnp.sum(match, axis=3))
    combine = jnp.transpose(lax.optimization_barrier(jnp.sum(match * weights[None, None, :, :], axis=3)), (2, 0, 1))
    return (dispatch, combine)

def reference(queries, keys, values, residual, norm_gain, out_weight, gate_weight, up_weight, down_weight, expert_ids, route_weights):
    group = H // KV
    block = math.gcd(TOKENS, 512)
    key_all = keys.reshape(TOKENS, KV, HD).astype(jnp.float32)
    value_all = values.reshape(TOKENS, KV, HD).astype(jnp.float32)
    key_pos = jnp.arange(TOKENS, dtype=jnp.int32)

    def attend(start):
        query_block = lax.dynamic_slice_in_dim(queries, start, block, 0)
        query_block = query_block.reshape(block, KV, group, HD).astype(jnp.float32)
        scores = jnp.einsum('qkgd,skd->qkgs', query_block, key_all) / math.sqrt(HD)
        query_pos = start + jnp.arange(block, dtype=jnp.int32)
        visible = (key_pos[None, :] <= query_pos[:, None])[:, None, None, :]
        scores = jnp.where(visible, scores, -1e+30)
        highest = lax.optimization_barrier(jnp.max(scores, axis=-1, keepdims=True))
        probs = jnp.where(visible, jnp.exp(scores - highest), 0.0)
        total = lax.optimization_barrier(jnp.sum(probs, axis=-1))
        rounded = lax.optimization_barrier(probs.astype(jnp.bfloat16)).astype(jnp.float32)
        weighted = jnp.einsum('qkgs,skd->qkgd', rounded, value_all)
        return (weighted / total[..., None]).astype(jnp.bfloat16).reshape(block, H * HD)
    starts = jnp.arange(0, TOKENS, block, dtype=jnp.int32)
    attention = lax.map(attend, starts).reshape(TOKENS, H * HD)
    projected = jnp.dot(attention, out_weight, preferred_element_type=jnp.float32)
    state = residual.reshape(TOKENS, D).astype(jnp.float32) + projected
    scale_rows = lax.rsqrt(lax.optimization_barrier(jnp.mean(state * state, axis=-1, keepdims=True)) + 1e-05)
    normed = (state * scale_rows * norm_gain).astype(jnp.bfloat16)
    groups = TOKENS // MOE_TOK
    tokens_f = normed.reshape(groups, MOE_TOK, D).astype(jnp.float32)
    dispatch, combine = jax.vmap(lambda ids, wts: route_tables(ids, wts, EXPERTS, CAP))(expert_ids.reshape(groups, MOE_TOK, TOP), route_weights.reshape(groups, MOE_TOK, TOP))
    pieces = N_TP * N_ETP
    width = HIDW // pieces

    def one_expert(carry, inputs):
        gate_e, up_e, down_e, dispatch_e, combine_e = inputs
        rows_in = jnp.einsum('gcm,gmd->gcd', dispatch_e, tokens_f).astype(jnp.bfloat16).reshape(groups * CAP, D)
        gate_v = jnp.dot(rows_in, gate_e, preferred_element_type=jnp.float32)
        up_v = jnp.dot(rows_in, up_e, preferred_element_type=jnp.float32)
        inner = (jax.nn.silu(gate_v) * up_v).astype(jnp.bfloat16)

        def add_piece(total, index):
            part_in = lax.dynamic_slice_in_dim(inner, index * width, width, 1)
            part_w = lax.dynamic_slice_in_dim(down_e, index * width, width, 0)
            term = lax.optimization_barrier(jnp.dot(part_in, part_w, preferred_element_type=jnp.float32).astype(jnp.bfloat16))
            return (total + term.astype(jnp.float32), None)
        out_e, _ = lax.scan(add_piece, jnp.zeros((groups * CAP, D), jnp.float32), jnp.arange(pieces, dtype=jnp.int32))
        out_e = out_e.reshape(groups, CAP, D)
        return (carry + jnp.einsum('gmc,gcd->gmd', combine_e, out_e), None)
    moe, _ = lax.scan(one_expert, jnp.zeros((groups, MOE_TOK, D), jnp.float32), (gate_weight, up_weight, down_weight, jnp.transpose(dispatch, (1, 0, 2, 3)), jnp.transpose(combine, (2, 0, 1, 3))))
    mixed = (state.reshape(groups, MOE_TOK, D) + moe).astype(jnp.bfloat16)
    return (attention, mixed.reshape(TOKENS // TOK_DEV, N_TP, MOE_TOK, D))
```

```python
import math

import jax
import jax.numpy as jnp
from jax import lax
from jax.sharding import PartitionSpec as P

HD = 128


def route_slots(ids, experts):
    tokens, top = ids.shape
    flat = ids.reshape(-1)
    hot = (flat[:, None] == jnp.arange(experts, dtype=jnp.int32)[None, :]).astype(jnp.int32)
    rank = jnp.cumsum(hot, axis=0) - hot
    return jnp.sum(rank * hot, axis=1).reshape(tokens, top)


def split_bf16(x):
    hi = x.astype(jnp.bfloat16)
    lo = (x - hi.astype(jnp.float32)).astype(jnp.bfloat16)
    return hi, lo


def shards(
    queries,
    keys,
    values,
    residual,
    norm_gain,
    out_weight,
    gate_weight,
    up_weight,
    down_weight,
    expert_ids,
    route_weights,
):
    n_tp = lax.axis_size("tp")
    n_ep = lax.axis_size("ep")
    n_etp = lax.axis_size("etp")
    rows = queries.shape[0]
    heads_dev = queries.shape[1] // HD
    kv_dev = keys.shape[1] // HD
    group = heads_dev // kv_dev
    query_pos = lax.axis_index(("ep", "etp")) * rows + jnp.arange(rows, dtype=jnp.int32)
    grouped = queries.reshape(rows, kv_dev, group, HD)
    kv = lax.all_gather(
        jnp.concatenate([keys, values], axis=1), ("ep", "etp"), axis=0, tiled=True
    )
    count = kv.shape[0]
    key_heads = kv[:, : kv_dev * HD].reshape(count, kv_dev, HD)
    value_heads = kv[:, kv_dev * HD :].reshape(count, kv_dev, HD)
    scores = jnp.einsum(
        "qkgd,skd->qkgs", grouped, key_heads, preferred_element_type=jnp.float32
    ) / math.sqrt(HD)
    key_pos = jnp.arange(count, dtype=jnp.int32)
    visible = (key_pos[None, :] <= query_pos[:, None])[:, None, None, :]
    scores = jnp.where(visible, scores, -1e30)
    newest = jnp.max(scores, axis=-1)
    probs = jnp.where(visible, jnp.exp(scores - newest[..., None]), 0.0)
    total = jnp.sum(probs, axis=-1)
    weighted = jnp.einsum(
        "qkgs,skd->qkgd",
        probs.astype(jnp.bfloat16),
        value_heads,
        preferred_element_type=jnp.float32,
    )
    attention = (weighted / total[..., None]).astype(jnp.bfloat16).reshape(rows, heads_dev * HD)
    moe_rows = rows // n_tp
    stacked = attention.reshape(n_tp, moe_rows, heads_dev * HD)
    partial_proj = jnp.einsum(
        "tmf,fc->tmc",
        lax.all_gather(stacked, "etp", axis=1, tiled=True),
        out_weight,
        preferred_element_type=jnp.float32,
    )
    cols = out_weight.shape[1]
    parts = lax.all_to_all(
        partial_proj.reshape(n_tp * n_etp, moe_rows, cols).astype(jnp.bfloat16),
        ("tp", "etp"),
        split_axis=0,
        concat_axis=0,
        tiled=True,
    ).astype(jnp.float32)
    projected = jnp.sum(parts.reshape(n_tp, n_etp, moe_rows, cols), axis=0)
    projected = jnp.transpose(projected, (1, 0, 2)).reshape(moe_rows, n_etp * cols)
    model = n_etp * cols
    state = residual.reshape(moe_rows, model).astype(jnp.float32) + projected
    scale_rows = lax.rsqrt(jnp.mean(state * state, axis=-1, keepdims=True) + 1e-05)
    normed = (state * scale_rows * norm_gain).astype(jnp.bfloat16)
    experts = n_ep * gate_weight.shape[0]
    top = expert_ids.shape[-1]
    cap = max(2, min(moe_rows, 5 * moe_rows * top // (4 * experts)))
    ids = expert_ids.reshape(moe_rows, top)
    weights = route_weights.reshape(moe_rows, top)
    place = ids * cap + route_slots(ids, experts)
    match = place[:, :, None] == jnp.arange(experts * cap, dtype=jnp.int32)[None, None, :]
    dispatch = jnp.sum(match.astype(jnp.float32), axis=1)
    combine = jnp.sum(jnp.where(match, weights[:, :, None], 0.0), axis=1)
    send = lax.dot_general(
        dispatch.astype(jnp.bfloat16),
        normed,
        (((0,), (0,)), ((), ())),
        preferred_element_type=jnp.float32,
    ).astype(jnp.bfloat16)
    gate_local = gate_weight[0]
    up_local = up_weight[0]
    down_local = down_weight[0]
    own = lax.all_to_all(send, "ep", split_axis=0, concat_axis=0, tiled=True)
    piece = lax.all_gather(own, ("tp", "etp"), axis=0, tiled=True)
    gate_v = jnp.dot(piece, gate_local, preferred_element_type=jnp.float32)
    up_v = jnp.dot(piece, up_local, preferred_element_type=jnp.float32)
    inner = (jax.nn.silu(gate_v) * up_v).astype(jnp.bfloat16)
    terms = jnp.dot(inner, down_local, preferred_element_type=jnp.float32).astype(jnp.bfloat16)
    summed = lax.psum_scatter(terms, ("tp", "etp"), scatter_dimension=0, tiled=True)
    expert_out = lax.all_to_all(summed, "ep", split_axis=0, concat_axis=0, tiled=True)
    hi, lo = split_bf16(combine)
    moe = jnp.dot(hi, expert_out, preferred_element_type=jnp.float32) + jnp.dot(
        lo, expert_out, preferred_element_type=jnp.float32
    )
    mixed = (state + moe).astype(jnp.bfloat16).reshape(1, 1, moe_rows, model)
    return (attention, mixed)


def solution(mesh):
    return jax.shard_map(
        shards,
        mesh=mesh,
        in_specs=(
            P(("ep", "etp"), "tp"),
            P(("ep", "etp"), "tp"),
            P(("ep", "etp"), "tp"),
            P(("ep", "etp"), "tp", None, None),
            P(),
            P("tp", "etp"),
            P("ep", None, ("tp", "etp")),
            P("ep", None, ("tp", "etp")),
            P("ep", ("tp", "etp"), None),
            P(("ep", "etp"), "tp", None, None),
            P(("ep", "etp"), "tp", None, None),
        ),
        out_specs=(P(("ep", "etp"), "tp"), P(("ep", "etp"), "tp", None, None)),
        check_vma=False,
    )
```

```python
import math

import jax
import jax.numpy as jnp
from jax import lax
from jax.sharding import PartitionSpec as P

HD = 128


def route_slots(ids, experts):
    tokens, top = ids.shape
    flat = ids.reshape(-1)
    hot = (flat[:, None] == jnp.arange(experts, dtype=jnp.int32)[None, :]).astype(jnp.int32)
    rank = jnp.cumsum(hot, axis=0) - hot
    return jnp.sum(rank * hot, axis=1).reshape(tokens, top)


def split_bf16(x):
    hi = x.astype(jnp.bfloat16)
    lo = (x - hi.astype(jnp.float32)).astype(jnp.bfloat16)
    return hi, lo


def shift(x, axis, by):
    n = lax.axis_size(axis)
    return lax.ppermute(x, axis, [(i, (i + by) % n) for i in range(n)])


def swap_core(x):
    n = lax.axis_size("ep")
    return lax.ppermute(x, "ep", [(i, i ^ 1) for i in range(n)])


def pair_places(ids, side, cap, experts):
    me = lax.axis_index("ep")
    chip = (ids // 2 - me // 2) % (experts // 2)
    place = chip * (2 * cap) + side * cap + route_slots(ids, experts)
    return jnp.where(ids % 2 == me % 2, place, -1)


def ring_gather(halves, axis):
    lo, hi = halves
    left_lo, right_hi = shift(lo, axis, 1), shift(hi, axis, -1)
    left_hi, right_lo = shift(hi, axis, 1), shift(lo, axis, -1)
    return (
        (lo, left_lo, right_lo, shift(left_lo, axis, 1)),
        (hi, left_hi, right_hi, shift(right_hi, axis, -1)),
    )


def ring_scatter(halves, axis):
    (own_lo, left_lo, right_lo, far_lo), (own_hi, left_hi, right_hi, far_hi) = halves
    over_lo, over_hi = shift(far_lo, axis, 1), shift(far_hi, axis, -1)
    got_lo, got_hi = shift(left_lo, axis, -1), shift(right_hi, axis, 1)
    last_lo = shift(add(right_lo, over_lo), axis, 1)
    last_hi = shift(add(left_hi, over_hi), axis, -1)
    return add(own_lo, got_lo, last_lo), add(own_hi, got_hi, last_hi)


def add(*terms):
    return sum(t.astype(jnp.float32) for t in terms).astype(jnp.bfloat16)


def shards(
    queries,
    keys,
    values,
    residual,
    norm_gain,
    out_weight,
    gate_weight,
    up_weight,
    down_weight,
    expert_ids,
    route_weights,
):
    n_tp = lax.axis_size("tp")
    n_ep = lax.axis_size("ep")
    n_etp = lax.axis_size("etp")
    rows = queries.shape[0]
    heads_dev = queries.shape[1] // HD
    kv_dev = keys.shape[1] // HD
    group = heads_dev // kv_dev
    query_pos = lax.axis_index(("ep", "etp")) * rows + jnp.arange(rows, dtype=jnp.int32)
    grouped = queries.reshape(rows, kv_dev, group, HD)
    kv = lax.all_gather(
        jnp.concatenate([keys, values], axis=1), ("ep", "etp"), axis=0, tiled=True
    )
    count = kv.shape[0]
    key_heads = kv[:, : kv_dev * HD].reshape(count, kv_dev, HD)
    value_heads = kv[:, kv_dev * HD :].reshape(count, kv_dev, HD)
    scores = jnp.einsum(
        "qkgd,skd->qkgs", grouped, key_heads, preferred_element_type=jnp.float32
    ) / math.sqrt(HD)
    key_pos = jnp.arange(count, dtype=jnp.int32)
    visible = (key_pos[None, :] <= query_pos[:, None])[:, None, None, :]
    scores = jnp.where(visible, scores, -1e30)
    newest = jnp.max(scores, axis=-1)
    probs = jnp.where(visible, jnp.exp(scores - newest[..., None]), 0.0)
    total = jnp.sum(probs, axis=-1)
    weighted = jnp.einsum(
        "qkgs,skd->qkgd",
        probs.astype(jnp.bfloat16),
        value_heads,
        preferred_element_type=jnp.float32,
    )
    attention = (weighted / total[..., None]).astype(jnp.bfloat16).reshape(rows, heads_dev * HD)
    moe_rows = rows // n_tp
    stacked = attention.reshape(n_tp, moe_rows, heads_dev * HD)
    partial_proj = jnp.einsum(
        "tmf,fc->tmc",
        lax.all_gather(stacked, "etp", axis=1, tiled=True),
        out_weight,
        preferred_element_type=jnp.float32,
    )
    cols = out_weight.shape[1]
    parts = lax.all_to_all(
        partial_proj.reshape(n_tp * n_etp, moe_rows, cols).astype(jnp.bfloat16),
        ("tp", "etp"),
        split_axis=0,
        concat_axis=0,
        tiled=True,
    ).astype(jnp.float32)
    projected = jnp.sum(parts.reshape(n_tp, n_etp, moe_rows, cols), axis=0)
    projected = jnp.transpose(projected, (1, 0, 2)).reshape(moe_rows, n_etp * cols)
    model = n_etp * cols
    state = residual.reshape(moe_rows, model).astype(jnp.float32) + projected
    scale_rows = lax.rsqrt(jnp.mean(state * state, axis=-1, keepdims=True) + 1e-05)
    normed = (state * scale_rows * norm_gain).astype(jnp.bfloat16)
    top = expert_ids.shape[-1]
    experts = n_ep * gate_weight.shape[0]
    cap = max(2, min(moe_rows, 5 * moe_rows * top // (4 * experts)))
    ids = expert_ids.reshape(moe_rows, top)
    weights = route_weights.reshape(moe_rows, top)
    other_ids, other_weights = swap_core(ids), swap_core(weights)
    place = jnp.concatenate(
        [pair_places(ids, 0, cap, experts), pair_places(other_ids, 1, cap, experts)], axis=0
    )
    match = place[:, :, None] == jnp.arange(experts * cap, dtype=jnp.int32)[None, None, :]
    dispatch = jnp.sum(match.astype(jnp.float32), axis=1).astype(jnp.bfloat16)
    pair_weights = jnp.concatenate([weights, other_weights], axis=0)
    combine = jnp.sum(jnp.where(match, pair_weights[:, :, None], 0.0), axis=1)
    hi, lo = split_bf16(combine)

    width = model // 4
    steps = n_ep // 2
    rows_step = 2 * cap
    pair = jnp.concatenate([normed, swap_core(normed)], axis=0)
    quarters = []
    for q in range(4):
        send = lax.dot_general(
            dispatch,
            pair[:, q * width : (q + 1) * width],
            (((0,), (0,)), ((), ())),
            preferred_element_type=jnp.float32,
        ).astype(jnp.bfloat16)
        pieces = [send[d * rows_step : (d + 1) * rows_step] for d in range(steps)]
        pieces = [pieces[0]] + [shift(pieces[d], "ep", 2 * d) for d in range(1, steps)]
        quarters.append(jnp.concatenate(pieces, axis=0))

    gate_local = gate_weight[0]
    up_local = up_weight[0]
    down_local = down_weight[0]
    sums = []
    for half, (first, second) in enumerate((("tp", "etp"), ("etp", "tp"))):
        near = ring_gather(quarters[2 * half : 2 * half + 2], first)
        near = [jnp.concatenate(blocks, axis=0) for blocks in near]
        far = ring_gather(near, second)
        gates, ups = [], []
        for j in range(4):
            gate_v = up_v = 0.0
            for k in range(2):
                span = slice((2 * half + k) * width, (2 * half + k + 1) * width)
                gate_v += jnp.dot(far[k][j], gate_local[span], preferred_element_type=jnp.float32)
                up_v += jnp.dot(far[k][j], up_local[span], preferred_element_type=jnp.float32)
            gates.append(gate_v)
            ups.append(up_v)
        sums.append((jnp.stack(gates), jnp.stack(ups)))
    slots = experts * cap
    hidden = gate_local.shape[1]

    def crossed(v):
        return jnp.swapaxes(v.reshape(4, 4, slots, hidden), 0, 1).reshape(4, 4 * slots, hidden)

    gate_v = sums[0][0] + crossed(sums[1][0])
    up_v = sums[0][1] + crossed(sums[1][1])
    inner = (jax.nn.silu(gate_v) * up_v).astype(jnp.bfloat16)
    returned = []
    for half, (first, second) in enumerate((("tp", "etp"), ("etp", "tp"))):
        inner_h = inner if half == 0 else crossed(inner)
        terms = []
        for k in range(2):
            span = slice((2 * half + k) * width, (2 * half + k + 1) * width)
            terms.append(
                [
                    jnp.dot(
                        inner_h[j], down_local[:, span], preferred_element_type=jnp.float32
                    ).astype(jnp.bfloat16)
                    for j in range(4)
                ]
            )
        near = ring_scatter(terms, second)
        near = [[v[j * slots : (j + 1) * slots] for j in range(4)] for v in near]
        returned += ring_scatter(near, first)
    moe = []
    for v in returned:
        pieces = [v[d * rows_step : (d + 1) * rows_step] for d in range(steps)]
        pieces = [pieces[0]] + [shift(pieces[d], "ep", -2 * d) for d in range(1, steps)]
        rows_q = jnp.concatenate(pieces, axis=0)
        both = jnp.dot(hi, rows_q, preferred_element_type=jnp.float32) + jnp.dot(
            lo, rows_q, preferred_element_type=jnp.float32
        )
        theirs = swap_core(both[moe_rows:].astype(jnp.bfloat16))
        moe.append(both[:moe_rows] + theirs.astype(jnp.float32))
    mixed = (state + jnp.concatenate(moe, axis=1)).astype(jnp.bfloat16)
    return (attention, mixed.reshape(1, 1, moe_rows, model))


def solution(mesh):
    return jax.shard_map(
        shards,
        mesh=mesh,
        in_specs=(
            P(("ep", "etp"), "tp"),
            P(("ep", "etp"), "tp"),
            P(("ep", "etp"), "tp"),
            P(("ep", "etp"), "tp", None, None),
            P(),
            P("tp", "etp"),
            P("ep", None, ("tp", "etp")),
            P("ep", None, ("tp", "etp")),
            P("ep", ("tp", "etp"), None),
            P(("ep", "etp"), "tp", None, None),
            P(("ep", "etp"), "tp", None, None),
        ),
        out_specs=(P(("ep", "etp"), "tp"), P(("ep", "etp"), "tp", None, None)),
        check_vma=False,
    )
```

```python
import functools
import math

import jax
import jax.numpy as jnp
from jax import lax
from jax.experimental import pallas as pl
from jax.experimental.pallas import tpu as pltpu
from jax.sharding import PartitionSpec as P

HD = 128


def route_slots(ids, experts):
    tokens, top = ids.shape
    flat = ids.reshape(-1)
    hot = (flat[:, None] == jnp.arange(experts, dtype=jnp.int32)[None, :]).astype(jnp.int32)
    rank = jnp.cumsum(hot, axis=0) - hot
    return jnp.sum(rank * hot, axis=1).reshape(tokens, top)


def split_bf16(x):
    hi = x.astype(jnp.bfloat16)
    lo = (x - hi.astype(jnp.float32)).astype(jnp.bfloat16)
    return hi, lo


def shift(x, axis, by):
    n = lax.axis_size(axis)
    return lax.ppermute(x, axis, [(i, (i + by) % n) for i in range(n)])


def swap_core(x):
    n = lax.axis_size("ep")
    return lax.ppermute(x, "ep", [(i, i ^ 1) for i in range(n)])


def pair_places(ids, side, cap, experts):
    me = lax.axis_index("ep")
    chip = (ids // 2 - me // 2) % (experts // 2)
    place = chip * (2 * cap) + side * cap + route_slots(ids, experts)
    return jnp.where(ids % 2 == me % 2, place, -1)


def ring_gather(halves, axis):
    lo, hi = halves
    left_lo, right_hi = shift(lo, axis, 1), shift(hi, axis, -1)
    left_hi, right_lo = shift(hi, axis, 1), shift(lo, axis, -1)
    return (
        (lo, left_lo, right_lo, shift(left_lo, axis, 1)),
        (hi, left_hi, right_hi, shift(right_hi, axis, -1)),
    )


def ring_scatter(halves, axis):
    (own_lo, left_lo, right_lo, far_lo), (own_hi, left_hi, right_hi, far_hi) = halves
    over_lo, over_hi = shift(far_lo, axis, 1), shift(far_hi, axis, -1)
    got_lo, got_hi = shift(left_lo, axis, -1), shift(right_hi, axis, 1)
    last_lo = shift(add(right_lo, over_lo), axis, 1)
    last_hi = shift(add(left_hi, over_hi), axis, -1)
    return add(own_lo, got_lo, last_lo), add(own_hi, got_hi, last_hi)


def add(*terms):
    return sum(t.astype(jnp.float32) for t in terms).astype(jnp.bfloat16)


def gather_direct(x, axis, step=1):
    return (
        x,
        shift(x, axis, step),
        shift(x, axis, -step),
        shift(x, axis, 2 * step),
    )


OFFSETS = (0, -1, 1, 2)


def attend_kernel(scale, head_dim, places_ref, q_ref, *refs):
    keys, vals = refs[:4], refs[4:8]
    out_ref, top_ref, sum_ref, acc_ref = refs[8:]
    rows = q_ref.shape[0]
    heads = q_ref.shape[1] // head_dim
    me = places_ref[32]
    top_ref[...] = jnp.full_like(top_ref, -1e30)
    sum_ref[...] = jnp.zeros_like(sum_ref)
    acc_ref[...] = jnp.zeros_like(acc_ref)
    row = lax.broadcasted_iota(jnp.int32, (rows, 4 * rows), 0)
    col = lax.broadcasted_iota(jnp.int32, (rows, 4 * rows), 1)
    within, block = col % rows, col // rows
    for i in range(4):
        for j in range(0, 4, 2):
            at = [places_ref[(i * 4 + j) * 2 + n] for n in range(4)]
            first = jnp.minimum(jnp.minimum(at[0], at[1]), jnp.minimum(at[2], at[3]))

            @pl.when(first <= me)
            def _(i=i, j=j, at=at):
                k = keys[i][j * 2 * rows : (j + 2) * 2 * rows, :]
                v = jnp.concatenate(
                    [vals[n][i * 2 * rows : (i + 1) * 2 * rows, :] for n in (j, j + 1)], axis=0
                )
                base = jnp.where(
                    block < 2,
                    jnp.where(block == 0, at[0], at[1]),
                    jnp.where(block == 2, at[2], at[3]),
                )
                visible = (base - me) * rows + within <= row
                for h in range(heads):
                    span = slice(h * head_dim, (h + 1) * head_dim)
                    s = lax.dot_general(
                        q_ref[:, span],
                        k,
                        (((1,), (1,)), ((), ())),
                        preferred_element_type=jnp.float32,
                    )
                    s = jnp.where(visible, s * scale, -1e30)
                    old = top_ref[h]
                    new = jnp.maximum(old, jnp.max(s, axis=1, keepdims=True))
                    p = jnp.where(visible, jnp.exp(s - new), 0.0)
                    carry = jnp.exp(old - new)
                    top_ref[h] = new
                    sum_ref[h] = sum_ref[h] * carry + jnp.sum(p, axis=1, keepdims=True)
                    acc_ref[h] = acc_ref[h] * carry + jnp.dot(
                        p.astype(jnp.bfloat16), v, preferred_element_type=jnp.float32
                    )

    for h in range(heads):
        out_ref[:, h * head_dim : (h + 1) * head_dim] = (acc_ref[h] / sum_ref[h]).astype(
            out_ref.dtype
        )


def attend(places, q, keys, vals):
    rows, cols = q.shape
    heads = cols // HD
    vmem = pl.BlockSpec(memory_space=pltpu.VMEM)
    return pl.pallas_call(
        functools.partial(attend_kernel, 1.0 / math.sqrt(HD), HD),
        out_shape=jax.ShapeDtypeStruct(q.shape, q.dtype),
        in_specs=[pl.BlockSpec(memory_space=pltpu.SMEM)] + [vmem] * 9,
        out_specs=vmem,
        scratch_shapes=[
            pltpu.VMEM((heads, rows, 1), jnp.float32),
            pltpu.VMEM((heads, rows, 1), jnp.float32),
            pltpu.VMEM((heads, rows, HD), jnp.float32),
        ],
        compiler_params=pltpu.CompilerParams(vmem_limit_bytes=24 * 2**20),
        cost_estimate=pl.CostEstimate(
            flops=4 * heads * rows * 32 * rows * HD,
            bytes_accessed=4 * 32 * rows * HD,
            transcendentals=heads * rows * 32 * rows,
        ),
    )(places, q, *keys, *vals)


def stack_kernel(*refs):
    ins, outs, sems = refs[:8], refs[8:12], refs[12]
    rows, cols = ins[0].shape
    copies = []
    for half in range(2):
        for j in range(4):
            for k in range(2):
                copies.append(
                    pltpu.make_async_copy(
                        ins[4 * half + j].at[:, pl.ds(k * (cols // 2), cols // 2)],
                        outs[2 * half + k].at[pl.ds(j * rows, rows)],
                        sems.at[len(copies)],
                    )
                )
    for copy in copies:
        copy.start()
    for copy in copies:
        copy.wait()


def stack_blocks(blocks):
    rows, cols = blocks[0].shape
    whole = pl.BlockSpec(memory_space=pl.ANY)
    return pl.pallas_call(
        stack_kernel,
        out_shape=[jax.ShapeDtypeStruct((4 * rows, cols // 2), blocks[0].dtype)] * 4,
        in_specs=[whole] * 8,
        out_specs=[whole] * 4,
        scratch_shapes=[pltpu.SemaphoreType.DMA((16,))],
    )(*blocks)


def shards(
    queries,
    keys,
    values,
    residual,
    norm_gain,
    out_weight,
    gate_weight,
    up_weight,
    down_weight,
    expert_ids,
    route_weights,
):
    n_tp = lax.axis_size("tp")
    n_ep = lax.axis_size("ep")
    n_etp = lax.axis_size("etp")
    tp, ep, etp = (lax.axis_index(name) for name in ("tp", "ep", "etp"))
    rows = queries.shape[0]
    chip, core = ep // 2, ep % 2
    half_q = queries.shape[1] // 2

    def mine_theirs(x):
        w = x.shape[1] // 2
        mine = jnp.where(core == 0, x[:, :w], x[:, w:])
        theirs = jnp.where(core == 0, x[:, w:], x[:, :w])
        return mine, swap_core(theirs)

    key_pair = jnp.concatenate(mine_theirs(keys), axis=0)
    value_pair = jnp.concatenate(mine_theirs(values), axis=0)
    own_q, other_q = mine_theirs(queries)
    key_line = jnp.concatenate(gather_direct(key_pair, "etp"), axis=0)
    value_line = jnp.concatenate(gather_direct(value_pair, "ep", 2), axis=0)
    all_keys = gather_direct(key_line, "ep", 2)
    all_values = gather_direct(value_line, "etp")
    order = jnp.array(OFFSETS, jnp.int32)
    chips = (chip + order) % (n_ep // 2)
    depths = (etp + order) % n_etp
    cores = jnp.stack([core, 1 - core])
    places = (
        (2 * chips[:, None, None] + cores[None, None, :]) * n_etp + depths[None, :, None]
    ).reshape(-1)

    def for_block(block):
        return jnp.concatenate([places, block[None]]).astype(jnp.int32)

    me = ep * n_etp + etp
    far_block = (ep + 1 - 2 * core) * n_etp + etp
    lent = attend(for_block(far_block), other_q, all_keys, all_values)
    back = swap_core(lent)
    kept = attend(for_block(me), own_q, all_keys, all_values)
    attention = jnp.concatenate(
        [jnp.where(core == 0, kept, back), jnp.where(core == 0, back, kept)], axis=1
    )
    near_weight = lax.dynamic_slice_in_dim(out_weight, core * half_q, half_q, 0)
    far_weight = lax.dynamic_slice_in_dim(out_weight, (1 - core) * half_q, half_q, 0)
    back_all = gather_direct(back, "etp")
    kept_all = gather_direct(kept, "etp")
    moe_rows = rows // n_tp
    cols = out_weight.shape[1]
    partial_proj = jnp.stack(
        [
            (
                jnp.dot(b, far_weight, preferred_element_type=jnp.float32)
                + jnp.dot(k, near_weight, preferred_element_type=jnp.float32)
            )
            .astype(jnp.bfloat16)
            .reshape(n_tp, moe_rows, cols)
            for b, k in zip(back_all, kept_all)
        ],
        axis=1,
    )

    def for_tp(by):
        at = (tp + by) % n_tp
        return lax.dynamic_slice_in_dim(partial_proj, at, 1, 0).reshape(n_etp * moe_rows, cols)

    summed = for_tp(0).astype(jnp.float32)
    for by in (1, -1, 2):
        summed = summed + shift(for_tp(by), "tp", by).astype(jnp.float32)
    summed = summed.astype(jnp.bfloat16).reshape(n_etp, moe_rows, cols)
    column_blocks = [summed[0]] + [
        shift(summed[j], "etp", OFFSETS[j]) for j in range(1, n_etp)
    ]
    sources = [(etp - OFFSETS[j]) % n_etp for j in range(n_etp)]
    projected = jnp.concatenate(
        [
            sum(
                jnp.where(sources[j] == q, column_blocks[j].astype(jnp.float32), 0.0)
                for j in range(n_etp)
            )
            for q in range(n_etp)
        ],
        axis=1,
    )
    model = n_etp * cols
    state = residual.reshape(moe_rows, model).astype(jnp.float32) + projected
    scale_rows = lax.rsqrt(jnp.mean(state * state, axis=-1, keepdims=True) + 1e-05)
    normed = (state * scale_rows * norm_gain).astype(jnp.bfloat16)
    top = expert_ids.shape[-1]
    experts = n_ep * gate_weight.shape[0]
    cap = max(2, min(moe_rows, 5 * moe_rows * top // (4 * experts)))
    ids = expert_ids.reshape(moe_rows, top)
    weights = route_weights.reshape(moe_rows, top)
    other_ids, other_weights = swap_core(ids), swap_core(weights)
    place = jnp.concatenate(
        [pair_places(ids, 0, cap, experts), pair_places(other_ids, 1, cap, experts)], axis=0
    )
    match = place[:, :, None] == jnp.arange(experts * cap, dtype=jnp.int32)[None, None, :]
    dispatch = jnp.sum(match.astype(jnp.float32), axis=1).astype(jnp.bfloat16)
    pair_weights = jnp.concatenate([weights, other_weights], axis=0)
    combine = jnp.sum(jnp.where(match, pair_weights[:, :, None], 0.0), axis=1)
    hi, lo = split_bf16(combine)

    width = model // 4
    steps = n_ep // 2
    rows_step = 2 * cap
    pair = jnp.concatenate([normed, swap_core(normed)], axis=0)
    send = lax.dot_general(
        dispatch, pair, (((0,), (0,)), ((), ())), preferred_element_type=jnp.float32
    ).astype(jnp.bfloat16)
    pieces = [send[d * rows_step : (d + 1) * rows_step] for d in range(steps)]
    pieces = [pieces[0]] + [shift(pieces[d], "ep", 2 * d) for d in range(1, steps)]
    arrived = jnp.concatenate(pieces, axis=0)
    stacked = stack_blocks(
        gather_direct(arrived[:, : 2 * width], "tp")
        + gather_direct(arrived[:, 2 * width :], "etp")
    )

    gate_local = gate_weight[0]
    up_local = up_weight[0]
    down_local = down_weight[0]
    sums = []
    for half, (first, second) in enumerate((("tp", "etp"), ("etp", "tp"))):
        near = stacked[2 * half : 2 * half + 2]
        far = ring_gather(near, second)
        gates, ups = [], []
        for j in range(4):
            gate_v = up_v = 0.0
            for k in range(2):
                span = slice((2 * half + k) * width, (2 * half + k + 1) * width)
                gate_v += jnp.dot(far[k][j], gate_local[span], preferred_element_type=jnp.float32)
                up_v += jnp.dot(far[k][j], up_local[span], preferred_element_type=jnp.float32)
            gates.append(gate_v)
            ups.append(up_v)
        sums.append((jnp.stack(gates), jnp.stack(ups)))
    slots = experts * cap
    hidden = gate_local.shape[1]

    def crossed(v):
        return jnp.swapaxes(v.reshape(4, 4, slots, hidden), 0, 1).reshape(4, 4 * slots, hidden)

    gate_v = sums[0][0] + crossed(sums[1][0])
    up_v = sums[0][1] + crossed(sums[1][1])
    inner = (jax.nn.silu(gate_v) * up_v).astype(jnp.bfloat16)
    returned = []
    for half, (first, second) in enumerate((("tp", "etp"), ("etp", "tp"))):
        inner_h = inner if half == 0 else crossed(inner)
        terms = []
        for k in range(2):
            span = slice((2 * half + k) * width, (2 * half + k + 1) * width)
            terms.append(
                [
                    jnp.dot(
                        inner_h[j], down_local[:, span], preferred_element_type=jnp.float32
                    ).astype(jnp.bfloat16)
                    for j in range(4)
                ]
            )
        near = ring_scatter(terms, second)
        near = [[v[j * slots : (j + 1) * slots] for j in range(4)] for v in near]
        returned += ring_scatter(near, first)
    outs = jnp.concatenate(returned, axis=1)
    pieces = [outs[d * rows_step : (d + 1) * rows_step] for d in range(steps)]
    pieces = [pieces[0]] + [shift(pieces[d], "ep", -2 * d) for d in range(1, steps)]
    expert_rows = jnp.concatenate(pieces, axis=0)
    both = jnp.dot(hi, expert_rows, preferred_element_type=jnp.float32) + jnp.dot(
        lo, expert_rows, preferred_element_type=jnp.float32
    )
    theirs = swap_core(both[moe_rows:].astype(jnp.bfloat16))
    mixed = (state + both[:moe_rows] + theirs.astype(jnp.float32)).astype(jnp.bfloat16)
    return (attention, mixed.reshape(1, 1, moe_rows, model))


def solution(mesh):
    return jax.shard_map(
        shards,
        mesh=mesh,
        in_specs=(
            P(("ep", "etp"), "tp"),
            P(("ep", "etp"), "tp"),
            P(("ep", "etp"), "tp"),
            P(("ep", "etp"), "tp", None, None),
            P(),
            P("tp", "etp"),
            P("ep", None, ("tp", "etp")),
            P("ep", None, ("tp", "etp")),
            P("ep", ("tp", "etp"), None),
            P(("ep", "etp"), "tp", None, None),
            P(("ep", "etp"), "tp", None, None),
        ),
        out_specs=(P(("ep", "etp"), "tp"), P(("ep", "etp"), "tp", None, None)),
        check_vma=False,
    )
```

```python
import functools
import math

import jax
import jax.numpy as jnp
from jax import lax
from jax.experimental import pallas as pl
from jax.experimental.pallas import tpu as pltpu
from jax.sharding import PartitionSpec as P

HD = 128


def route_slots(ids, experts):
    tokens, top = ids.shape
    flat = ids.reshape(-1)
    hot = (flat[:, None] == jnp.arange(experts, dtype=jnp.int32)[None, :]).astype(jnp.int32)
    rank = jnp.cumsum(hot, axis=0) - hot
    return jnp.sum(rank * hot, axis=1).reshape(tokens, top)


def split_bf16(x):
    hi = x.astype(jnp.bfloat16)
    lo = (x - hi.astype(jnp.float32)).astype(jnp.bfloat16)
    return hi, lo


def shift(x, axis, by):
    n = lax.axis_size(axis)
    return lax.ppermute(x, axis, [(i, (i + by) % n) for i in range(n)])


def swap_core(x):
    n = lax.axis_size("ep")
    return lax.ppermute(x, "ep", [(i, i ^ 1) for i in range(n)])


def pair_places(ids, side, cap, experts):
    me = lax.axis_index("ep")
    chip = (ids // 2 - me // 2) % (experts // 2)
    place = chip * (2 * cap) + side * cap + route_slots(ids, experts)
    return jnp.where(ids % 2 == me % 2, place, -1)


def ring_gather(halves, axis):
    lo, hi = halves
    left_lo, right_hi = shift(lo, axis, 1), shift(hi, axis, -1)
    left_hi, right_lo = shift(hi, axis, 1), shift(lo, axis, -1)
    return (
        (lo, left_lo, right_lo, shift(left_lo, axis, 1)),
        (hi, left_hi, right_hi, shift(right_hi, axis, -1)),
    )


def add(*terms):
    return sum(t.astype(jnp.float32) for t in terms).astype(jnp.bfloat16)


def gather_direct(x, axis, step=1):
    return (
        x,
        shift(x, axis, step),
        shift(x, axis, -step),
        shift(x, axis, 2 * step),
    )


OFFSETS = (0, -1, 1, 2)


LIMIT = 48 * 2**20


def attend_kernel(scale, places_ref, q_ref, *refs):
    keys, vals = refs[:4], refs[4:8]
    out_ref, diff_ref, top_ref, sum_ref, acc_ref = refs[8:]
    depth, width = q_ref.shape
    rows = out_ref.shape[0]
    me = places_ref[32]
    top_ref[...] = jnp.full_like(top_ref, -1e20)
    sum_ref[...] = jnp.zeros_like(sum_ref)
    acc_ref[...] = jnp.zeros_like(acc_ref)
    diff_ref[...] = lax.broadcasted_iota(jnp.int32, (rows, width), 0) - (
        lax.broadcasted_iota(jnp.int32, (rows, width), 1) % rows
    )
    for i in range(4):
        for j in range(4):
            at = [places_ref[(i * 4 + j) * 2 + n] for n in range(2)]

            @pl.when(jnp.minimum(at[0], at[1]) <= me)
            def _(i=i, j=j, at=at):
                k = keys[i][j * 2 * rows : (j + 1) * 2 * rows, :]
                v = vals[j][i * depth : (i + 1) * depth, :]
                s = jnp.dot(k, q_ref[...], preferred_element_type=jnp.float32) * scale
                s = jnp.concatenate(
                    [
                        jnp.where(
                            diff_ref[...] <= (me - at[n]) * rows,
                            s[n * rows : (n + 1) * rows],
                            -1e30,
                        )
                        for n in range(2)
                    ],
                    axis=0,
                )
                old = top_ref[...]
                new = jnp.maximum(old, jnp.max(s, axis=0, keepdims=True))
                p = jnp.exp2(s - new)
                carry = jnp.exp2(old - new)
                top_ref[...] = new
                sum_ref[...] = sum_ref[...] * carry + jnp.sum(p, axis=0, keepdims=True)
                acc_ref[...] = acc_ref[...] * carry + jnp.dot(
                    v, p.astype(jnp.bfloat16), preferred_element_type=jnp.float32
                )

    done = acc_ref[...] / sum_ref[...]
    for h in range(width // rows):
        out_ref[:, h * depth : (h + 1) * depth] = (
            done[:, h * rows : (h + 1) * rows].T.astype(out_ref.dtype)
        )


def attend(places, q, keys, vals):
    depth = keys[0].shape[1]
    heads = q.shape[1] // depth
    rows = q.shape[0]
    turned = jnp.transpose(q.reshape(rows, heads, depth), (2, 1, 0)).reshape(depth, heads * rows)
    vmem = pl.BlockSpec(memory_space=pltpu.VMEM)
    return pl.pallas_call(
        functools.partial(attend_kernel, math.log2(math.e) / math.sqrt(depth)),
        out_shape=jax.ShapeDtypeStruct(q.shape, q.dtype),
        in_specs=[pl.BlockSpec(memory_space=pltpu.SMEM)] + [vmem] * 9,
        out_specs=vmem,
        scratch_shapes=[
            pltpu.VMEM((rows, heads * rows), jnp.int32),
            pltpu.VMEM((1, heads * rows), jnp.float32),
            pltpu.VMEM((1, heads * rows), jnp.float32),
            pltpu.VMEM((depth, heads * rows), jnp.float32),
        ],
        compiler_params=pltpu.CompilerParams(vmem_limit_bytes=LIMIT),
        cost_estimate=pl.CostEstimate(
            flops=4 * heads * rows * 32 * rows * depth,
            bytes_accessed=4 * 32 * rows * depth,
            transcendentals=heads * rows * 32 * rows,
        ),
    )(places, turned, *keys, *vals)


def stack_kernel(*refs):
    ins, outs = refs[:8], refs[8:]
    rows, cols = ins[0].shape
    for half in range(2):
        for j in range(4):
            for k in range(2):
                outs[2 * half + k][j * rows : (j + 1) * rows, :] = ins[4 * half + j][
                    :, k * (cols // 2) : (k + 1) * (cols // 2)
                ]


def stack_blocks(blocks):
    rows, cols = blocks[0].shape
    vmem = pl.BlockSpec(memory_space=pltpu.VMEM)
    return pl.pallas_call(
        stack_kernel,
        out_shape=[jax.ShapeDtypeStruct((4 * rows, cols // 2), blocks[0].dtype)] * 4,
        in_specs=[vmem] * 8,
        out_specs=[vmem] * 4,
        compiler_params=pltpu.CompilerParams(vmem_limit_bytes=LIMIT),
    )(*blocks)


def first_sums_kernel(*refs):
    blocks, (gate_ref, up_ref, out_ref) = refs[:12], refs[12:]
    step = pl.program_id(0)
    rows, hidden = blocks[0].shape[0], gate_ref.shape[-1]

    @pl.when(step % 4 == 0)
    def _():
        out_ref[...] = jnp.zeros_like(out_ref)

    for part in range(4):

        @pl.when(step // 2 == part)
        def _(part=part):
            for j in range(3):
                x = blocks[3 * part + j][...]
                span = slice(j * rows, (j + 1) * rows)
                out_ref[0, span, :hidden] += jnp.dot(
                    x, gate_ref[0], preferred_element_type=jnp.float32
                )
                out_ref[0, span, hidden:] += jnp.dot(
                    x, up_ref[0], preferred_element_type=jnp.float32
                )


def first_sums(blocks, gate, up):
    rows, width = blocks[0][0].shape
    hidden = gate.shape[2]
    sub = width // 2

    def spec(part):
        return pl.BlockSpec((rows, sub), lambda g: (0, jnp.clip(g - 2 * part, 0, 1)))

    weight = pl.BlockSpec((1, sub, hidden), lambda g: (0, g, 0))
    return pl.pallas_call(
        first_sums_kernel,
        grid=(8,),
        out_shape=jax.ShapeDtypeStruct((2, 3 * rows, 2 * hidden), jnp.float32),
        in_specs=[spec(part) for part in range(4) for _ in range(3)] + [weight, weight],
        out_specs=pl.BlockSpec((1, 3 * rows, 2 * hidden), lambda g: (g // 4, 0, 0)),
        compiler_params=pltpu.CompilerParams(vmem_limit_bytes=LIMIT),
    )(*[x for part in blocks for x in part], gate, up)


def down_kernel(*refs):
    xs, down_ref, outs = refs[:4], refs[4], refs[5:]
    for part in range(4):

        @pl.when(pl.program_id(0) == part)
        def _(part=part):
            outs[part][...] = jnp.dot(
                xs[part][...], down_ref[0], preferred_element_type=jnp.float32
            ).astype(outs[part].dtype)


def down_terms(xs, down):
    rows, hidden = xs[0].shape
    width = down.shape[2] // 4
    return pl.pallas_call(
        down_kernel,
        grid=(4,),
        out_shape=[jax.ShapeDtypeStruct((rows, width), jnp.bfloat16)] * 4,
        in_specs=[pl.BlockSpec((rows, hidden), lambda g: (0, 0))] * 4
        + [pl.BlockSpec((1, hidden, width), lambda g: (0, 0, g))],
        out_specs=[pl.BlockSpec((rows, width), lambda g: (0, 0))] * 4,
        compiler_params=pltpu.CompilerParams(vmem_limit_bytes=LIMIT),
    )(*xs, down)


def merge_kernel(*refs):
    terms, outs = refs[:6], refs[6:]
    rows, cols = outs[0].shape
    for k in range(2):
        for j in range(4):
            span = slice(j * rows, (j + 1) * rows)
            a, b, c = (terms[3 * k + n][span, :].astype(jnp.float32) for n in range(3))
            outs[j][:, k * (cols // 2) : (k + 1) * (cols // 2)] = (a + b + c).astype(
                outs[j].dtype
            )


def merge_terms(lo, hi):
    rows, width = lo[0].shape
    vmem = pl.BlockSpec(memory_space=pltpu.VMEM)
    return pl.pallas_call(
        merge_kernel,
        out_shape=[jax.ShapeDtypeStruct((rows // 4, 2 * width), jnp.bfloat16)] * 4,
        in_specs=[vmem] * 6,
        out_specs=[vmem] * 4,
        compiler_params=pltpu.CompilerParams(vmem_limit_bytes=LIMIT),
    )(*lo, *hi)


def shards(
    queries,
    keys,
    values,
    residual,
    norm_gain,
    out_weight,
    gate_weight,
    up_weight,
    down_weight,
    expert_ids,
    route_weights,
):
    n_tp = lax.axis_size("tp")
    n_ep = lax.axis_size("ep")
    n_etp = lax.axis_size("etp")
    tp, ep, etp = (lax.axis_index(name) for name in ("tp", "ep", "etp"))
    rows = queries.shape[0]
    chip, core = ep // 2, ep % 2
    half_q = queries.shape[1] // 2

    def mine_theirs(x):
        w = x.shape[1] // 2
        mine = jnp.where(core == 0, x[:, :w], x[:, w:])
        theirs = jnp.where(core == 0, x[:, w:], x[:, :w])
        return mine, swap_core(theirs)

    key_pair = jnp.concatenate(mine_theirs(keys), axis=0)
    value_pair = jnp.concatenate(mine_theirs(values), axis=0).T
    own_q, other_q = mine_theirs(queries)
    key_line = jnp.concatenate(gather_direct(key_pair, "etp"), axis=0)
    value_line = jnp.concatenate(gather_direct(value_pair, "ep", 2), axis=0)
    all_keys = gather_direct(key_line, "ep", 2)
    all_values = gather_direct(value_line, "etp")
    order = jnp.array(OFFSETS, jnp.int32)
    chips = (chip + order) % (n_ep // 2)
    depths = (etp + order) % n_etp
    cores = jnp.stack([core, 1 - core])
    places = (
        (2 * chips[:, None, None] + cores[None, None, :]) * n_etp + depths[None, :, None]
    ).reshape(-1)

    def for_block(block):
        return jnp.concatenate([places, block[None]]).astype(jnp.int32)

    me = ep * n_etp + etp
    far_block = (ep + 1 - 2 * core) * n_etp + etp
    lent = attend(for_block(far_block), other_q, all_keys, all_values)
    back = swap_core(lent)
    kept = attend(for_block(me), own_q, all_keys, all_values)
    attention = jnp.concatenate(
        [jnp.where(core == 0, kept, back), jnp.where(core == 0, back, kept)], axis=1
    )
    near_weight = lax.dynamic_slice_in_dim(out_weight, core * half_q, half_q, 0)
    far_weight = lax.dynamic_slice_in_dim(out_weight, (1 - core) * half_q, half_q, 0)
    back_all = gather_direct(back, "etp")
    kept_all = gather_direct(kept, "etp")
    moe_rows = rows // n_tp
    cols = out_weight.shape[1]
    partial_proj = jnp.stack(
        [
            (
                jnp.dot(b, far_weight, preferred_element_type=jnp.float32)
                + jnp.dot(k, near_weight, preferred_element_type=jnp.float32)
            )
            .astype(jnp.bfloat16)
            .reshape(n_tp, moe_rows, cols)
            for b, k in zip(back_all, kept_all)
        ],
        axis=1,
    )

    def for_tp(by):
        at = (tp + by) % n_tp
        return lax.dynamic_slice_in_dim(partial_proj, at, 1, 0).reshape(n_etp * moe_rows, cols)

    summed = for_tp(0).astype(jnp.float32)
    for by in (1, -1, 2):
        summed = summed + shift(for_tp(by), "tp", by).astype(jnp.float32)
    summed = summed.astype(jnp.bfloat16).reshape(n_etp, moe_rows, cols)
    column_blocks = [summed[0]] + [
        shift(summed[j], "etp", OFFSETS[j]) for j in range(1, n_etp)
    ]
    sources = [(etp - OFFSETS[j]) % n_etp for j in range(n_etp)]
    projected = jnp.concatenate(
        [
            sum(
                jnp.where(sources[j] == q, column_blocks[j].astype(jnp.float32), 0.0)
                for j in range(n_etp)
            )
            for q in range(n_etp)
        ],
        axis=1,
    )
    model = n_etp * cols
    state = residual.reshape(moe_rows, model).astype(jnp.float32) + projected
    scale_rows = lax.rsqrt(jnp.mean(state * state, axis=-1, keepdims=True) + 1e-05)
    normed = (state * scale_rows * norm_gain).astype(jnp.bfloat16)
    top = expert_ids.shape[-1]
    experts = n_ep * gate_weight.shape[0]
    cap = max(2, min(moe_rows, 5 * moe_rows * top // (4 * experts)))
    ids = expert_ids.reshape(moe_rows, top)
    weights = route_weights.reshape(moe_rows, top)
    other_ids, other_weights = swap_core(ids), swap_core(weights)
    place = jnp.concatenate(
        [pair_places(ids, 0, cap, experts), pair_places(other_ids, 1, cap, experts)], axis=0
    )
    match = place[:, :, None] == jnp.arange(experts * cap, dtype=jnp.int32)[None, None, :]
    dispatch = jnp.sum(match.astype(jnp.float32), axis=1).astype(jnp.bfloat16)
    pair_weights = jnp.concatenate([weights, other_weights], axis=0)
    combine = jnp.sum(jnp.where(match, pair_weights[:, :, None], 0.0), axis=1)
    hi, lo = split_bf16(combine)

    width = model // 4
    steps = n_ep // 2
    rows_step = 2 * cap
    pair = jnp.concatenate([normed, swap_core(normed)], axis=0)
    send = lax.dot_general(
        dispatch, pair, (((0,), (0,)), ((), ())), preferred_element_type=jnp.float32
    ).astype(jnp.bfloat16)
    pieces = [send[d * rows_step : (d + 1) * rows_step] for d in range(steps)]
    pieces = [pieces[0]] + [shift(pieces[d], "ep", 2 * d) for d in range(1, steps)]
    arrived = jnp.concatenate(pieces, axis=0)
    stacked = stack_blocks(
        gather_direct(arrived[:, : 2 * width], "tp")
        + gather_direct(arrived[:, 2 * width :], "etp")
    )

    far = ring_gather(stacked[:2], "etp") + ring_gather(stacked[2:], "tp")
    slots = experts * cap
    hidden = gate_weight.shape[2]
    early = lax.optimization_barrier([far[q][:3] for q in range(4)])
    sums = first_sums(early, gate_weight, up_weight)

    def last_sum(half, weight):
        return sum(
            jnp.dot(
                far[2 * half + k][3],
                weight[0, (2 * half + k) * width : (2 * half + k + 1) * width],
                preferred_element_type=jnp.float32,
            )
            for k in range(2)
        )

    def crossed(v):
        return jnp.swapaxes(v.reshape(4, 4, slots, hidden), 0, 1).reshape(4, 4 * slots, hidden)

    def whole(n, weight):
        parts = [
            jnp.concatenate(
                [sums[half, :, n * hidden : (n + 1) * hidden], last_sum(half, weight)], axis=0
            )
            for half in range(2)
        ]
        return parts[0].reshape(4, 4 * slots, hidden) + crossed(parts[1])

    inner = (jax.nn.silu(whole(0, gate_weight)) * whole(1, up_weight)).astype(jnp.bfloat16)
    inner_a, inner_b = inner, crossed(inner)
    over = down_terms([inner_a[3], inner_a[3], inner_b[3], inner_b[3]], down_weight)
    inner_a, inner_b, _ = lax.optimization_barrier((inner_a, inner_b, over))
    direct = down_terms([inner_a[1], inner_a[2], inner_b[1], inner_b[2]], down_weight)
    inner_a, inner_b, _ = lax.optimization_barrier((inner_a, inner_b, direct))
    passed = down_terms([inner_a[2], inner_a[1], inner_b[2], inner_b[1]], down_weight)
    kept_terms = down_terms([inner_a[0], inner_a[0], inner_b[0], inner_b[0]], down_weight)
    returned = []
    for half, (first, second) in enumerate((("tp", "etp"), ("etp", "tp"))):
        q0, q1 = 2 * half, 2 * half + 1
        over_lo, over_hi = shift(over[q0], second, 1), shift(over[q1], second, -1)
        got_lo, got_hi = shift(direct[q0], second, -1), shift(direct[q1], second, 1)
        last_lo = shift(add(passed[q0], over_lo), second, 1)
        last_hi = shift(add(passed[q1], over_hi), second, -1)
        blocks = merge_terms(
            (kept_terms[q0], got_lo, last_lo), (kept_terms[q1], got_hi, last_hi)
        )
        returned.append(
            add(blocks[0], *[shift(blocks[j], first, OFFSETS[j]) for j in range(1, 4)])
        )
    outs = jnp.concatenate(returned, axis=1)
    pieces = [outs[d * rows_step : (d + 1) * rows_step] for d in range(steps)]
    pieces = [pieces[0]] + [shift(pieces[d], "ep", -2 * d) for d in range(1, steps)]
    expert_rows = jnp.concatenate(pieces, axis=0)
    both = jnp.dot(hi, expert_rows, preferred_element_type=jnp.float32) + jnp.dot(
        lo, expert_rows, preferred_element_type=jnp.float32
    )
    theirs = swap_core(both[moe_rows:].astype(jnp.bfloat16))
    mixed = (state + both[:moe_rows] + theirs.astype(jnp.float32)).astype(jnp.bfloat16)
    return (attention, mixed.reshape(1, 1, moe_rows, model))


def solution(mesh):
    return jax.shard_map(
        shards,
        mesh=mesh,
        in_specs=(
            P(("ep", "etp"), "tp"),
            P(("ep", "etp"), "tp"),
            P(("ep", "etp"), "tp"),
            P(("ep", "etp"), "tp", None, None),
            P(),
            P("tp", "etp"),
            P("ep", None, ("tp", "etp")),
            P("ep", None, ("tp", "etp")),
            P("ep", ("tp", "etp"), None),
            P(("ep", "etp"), "tp", None, None),
            P(("ep", "etp"), "tp", None, None),
        ),
        out_specs=(P(("ep", "etp"), "tp"), P(("ep", "etp"), "tp", None, None)),
        check_vma=False,
    )
```

```python
import functools
import math

import jax
import jax.numpy as jnp
from jax import lax
from jax.experimental import pallas as pl
from jax.experimental.pallas import tpu as pltpu
from jax.sharding import PartitionSpec as P

HD = 128


def route_slots(ids, experts):
    tokens, top = ids.shape
    flat = ids.reshape(-1)
    hot = (flat[:, None] == jnp.arange(experts, dtype=jnp.int32)[None, :]).astype(jnp.int32)
    rank = jnp.cumsum(hot, axis=0) - hot
    return jnp.sum(rank * hot, axis=1).reshape(tokens, top)


def split_bf16(x):
    hi = x.astype(jnp.bfloat16)
    lo = (x - hi.astype(jnp.float32)).astype(jnp.bfloat16)
    return hi, lo


def shift(x, axis, by):
    n = lax.axis_size(axis)
    return lax.ppermute(x, axis, [(i, (i + by) % n) for i in range(n)])


def swap_core(x):
    n = lax.axis_size("ep")
    return lax.ppermute(x, "ep", [(i, i ^ 1) for i in range(n)])


def pair_places(ids, side, cap, experts):
    me = lax.axis_index("ep")
    chip = (ids // 2 - me // 2) % (experts // 2)
    place = chip * (2 * cap) + side * cap + route_slots(ids, experts)
    return jnp.where(ids % 2 == me % 2, place, -1)


def ring_gather(halves, axis):
    lo, hi = halves
    left_lo, right_hi = shift(lo, axis, 1), shift(hi, axis, -1)
    left_hi, right_lo = shift(hi, axis, 1), shift(lo, axis, -1)
    return (
        (lo, left_lo, right_lo, shift(left_lo, axis, 1)),
        (hi, left_hi, right_hi, shift(right_hi, axis, -1)),
    )


def add(*terms):
    return sum(t.astype(jnp.float32) for t in terms).astype(jnp.bfloat16)


def gather_direct(x, axis, step=1):
    return (
        x,
        shift(x, axis, step),
        shift(x, axis, -step),
        shift(x, axis, 2 * step),
    )


OFFSETS = (0, -1, 1, 2)


LIMIT = 48 * 2**20


def attend_kernel(scale, places_ref, q_ref, *refs):
    keys, vals = refs[:4], refs[4:8]
    out_ref, diff_ref, top_ref, sum_ref, acc_ref = refs[8:]
    depth, width = q_ref.shape
    rows = out_ref.shape[0]
    me = places_ref[32]
    top_ref[...] = jnp.full_like(top_ref, -1e20)
    sum_ref[...] = jnp.zeros_like(sum_ref)
    acc_ref[...] = jnp.zeros_like(acc_ref)
    diff_ref[...] = lax.broadcasted_iota(jnp.int32, (rows, width), 0) - (
        lax.broadcasted_iota(jnp.int32, (rows, width), 1) % rows
    )
    for i in range(4):
        for j in range(4):
            at = [places_ref[(i * 4 + j) * 2 + n] for n in range(2)]

            @pl.when(jnp.minimum(at[0], at[1]) <= me)
            def _(i=i, j=j, at=at):
                k = keys[i][j * 2 * rows : (j + 1) * 2 * rows, :]
                v = vals[j][i * depth : (i + 1) * depth, :]
                s = jnp.dot(k, q_ref[...], preferred_element_type=jnp.float32) * scale
                s = jnp.concatenate(
                    [
                        jnp.where(
                            diff_ref[...] <= (me - at[n]) * rows,
                            s[n * rows : (n + 1) * rows],
                            -1e30,
                        )
                        for n in range(2)
                    ],
                    axis=0,
                )
                old = top_ref[...]
                new = jnp.maximum(old, jnp.max(s, axis=0, keepdims=True))
                p = jnp.exp2(s - new)
                carry = jnp.exp2(old - new)
                top_ref[...] = new
                sum_ref[...] = sum_ref[...] * carry + jnp.sum(p, axis=0, keepdims=True)
                acc_ref[...] = acc_ref[...] * carry + jnp.dot(
                    v, p.astype(jnp.bfloat16), preferred_element_type=jnp.float32
                )

    done = acc_ref[...] / sum_ref[...]
    for h in range(width // rows):
        out_ref[:, h * depth : (h + 1) * depth] = (
            done[:, h * rows : (h + 1) * rows].T.astype(out_ref.dtype)
        )


def attend(places, q, keys, vals):
    depth = keys[0].shape[1]
    heads = q.shape[1] // depth
    rows = q.shape[0]
    turned = jnp.transpose(q.reshape(rows, heads, depth), (2, 1, 0)).reshape(depth, heads * rows)
    vmem = pl.BlockSpec(memory_space=pltpu.VMEM)
    return pl.pallas_call(
        functools.partial(attend_kernel, math.log2(math.e) / math.sqrt(depth)),
        out_shape=jax.ShapeDtypeStruct(q.shape, q.dtype),
        in_specs=[pl.BlockSpec(memory_space=pltpu.SMEM)] + [vmem] * 9,
        out_specs=vmem,
        scratch_shapes=[
            pltpu.VMEM((rows, heads * rows), jnp.int32),
            pltpu.VMEM((1, heads * rows), jnp.float32),
            pltpu.VMEM((1, heads * rows), jnp.float32),
            pltpu.VMEM((depth, heads * rows), jnp.float32),
        ],
        compiler_params=pltpu.CompilerParams(vmem_limit_bytes=LIMIT),
        cost_estimate=pl.CostEstimate(
            flops=4 * heads * rows * 32 * rows * depth,
            bytes_accessed=4 * 32 * rows * depth,
            transcendentals=heads * rows * 32 * rows,
        ),
    )(places, turned, *keys, *vals)


def stack_kernel(*refs):
    ins, outs = refs[:8], refs[8:]
    rows, cols = ins[0].shape
    for half in range(2):
        for j in range(4):
            for k in range(2):
                outs[2 * half + k][j * rows : (j + 1) * rows, :] = ins[4 * half + j][
                    :, k * (cols // 2) : (k + 1) * (cols // 2)
                ]


def stack_blocks(blocks):
    rows, cols = blocks[0].shape
    vmem = pl.BlockSpec(memory_space=pltpu.VMEM)
    return pl.pallas_call(
        stack_kernel,
        out_shape=[jax.ShapeDtypeStruct((4 * rows, cols // 2), blocks[0].dtype)] * 4,
        in_specs=[vmem] * 8,
        out_specs=[vmem] * 4,
        compiler_params=pltpu.CompilerParams(vmem_limit_bytes=LIMIT),
    )(*blocks)


def add_products(half, j, x, gate, up, out_ref):
    rows = x.shape[0]
    hidden = gate.shape[1]
    quarter = rows // 4
    for n, weight in enumerate((gate, up)):
        span = slice(n * hidden, (n + 1) * hidden)
        y = jnp.dot(x, weight, preferred_element_type=jnp.float32)
        if half == 0:
            out_ref[j * rows : (j + 1) * rows, span] += y
        else:
            for i in range(4):
                at = (i * 4 + j) * quarter
                out_ref[at : at + quarter, span] += y[i * quarter : (i + 1) * quarter]


def first_sums_kernel(*refs):
    blocks, (gate_ref, up_ref, out_ref) = refs[:12], refs[12:]
    step = pl.program_id(0)

    @pl.when(step == 0)
    def _():
        out_ref[...] = jnp.zeros_like(out_ref)

    for part in range(4):

        @pl.when(step // 2 == part)
        def _(part=part):
            for j in range(3):
                x = blocks[3 * part + j][...]
                add_products(part // 2, j, x, gate_ref[0], up_ref[0], out_ref)


def part_spec(part, rows, sub):
    return pl.BlockSpec((rows, sub), lambda g: (0, jnp.clip(g - 2 * part, 0, 1)))


def first_sums(blocks, gate, up):
    rows, width = blocks[0][0].shape
    hidden = gate.shape[2]
    sub = width // 2
    weight = pl.BlockSpec((1, sub, hidden), lambda g: (0, g, 0))
    return pl.pallas_call(
        first_sums_kernel,
        grid=(8,),
        out_shape=jax.ShapeDtypeStruct((4 * rows, 2 * hidden), jnp.float32),
        in_specs=[part_spec(part, rows, sub) for part in range(4) for _ in range(3)]
        + [weight, weight],
        out_specs=pl.BlockSpec((4 * rows, 2 * hidden), lambda g: (0, 0)),
        compiler_params=pltpu.CompilerParams(vmem_limit_bytes=LIMIT),
    )(*[x for part in blocks for x in part], gate, up)


def inner_kernel(*refs):
    blocks, (sums_ref, gate_ref, up_ref, out_ref, crossed_ref, total_ref) = refs[:4], refs[4:]
    step = pl.program_id(0)
    hidden = gate_ref.shape[-1]
    quarter = blocks[0].shape[0] // 4

    @pl.when(step == 0)
    def _():
        total_ref[...] = sums_ref[...]

    for part in range(4):

        @pl.when(step // 2 == part)
        def _(part=part):
            add_products(part // 2, 3, blocks[part][...], gate_ref[0], up_ref[0], total_ref)

    @pl.when(step == 7)
    def _():
        for i in range(4):
            for j in range(4):
                at, to = (4 * i + j) * quarter, (4 * j + i) * quarter
                gate_v = total_ref[at : at + quarter, :hidden]
                up_v = total_ref[at : at + quarter, hidden:]
                inner = (gate_v / (1.0 + jnp.exp(-gate_v)) * up_v).astype(out_ref.dtype)
                out_ref[at : at + quarter, :] = inner
                crossed_ref[to : to + quarter, :] = inner


def inner_rows(blocks, sums, gate, up):
    rows, width = blocks[0].shape
    hidden = gate.shape[2]
    sub = width // 2
    weight = pl.BlockSpec((1, sub, hidden), lambda g: (0, g, 0))
    whole = pl.BlockSpec((4 * rows, hidden), lambda g: (0, 0))
    return pl.pallas_call(
        inner_kernel,
        grid=(8,),
        out_shape=[jax.ShapeDtypeStruct((4 * rows, hidden), jnp.bfloat16)] * 2,
        in_specs=[part_spec(part, rows, sub) for part in range(4)]
        + [pl.BlockSpec((4 * rows, 2 * hidden), lambda g: (0, 0)), weight, weight],
        out_specs=[whole, whole],
        scratch_shapes=[pltpu.VMEM((4 * rows, 2 * hidden), jnp.float32)],
        compiler_params=pltpu.CompilerParams(vmem_limit_bytes=LIMIT),
    )(*blocks, sums, gate, up)


def down_kernel(*refs):
    xs, down_ref, outs = refs[:4], refs[4], refs[5:]
    for part in range(4):

        @pl.when(pl.program_id(0) == part)
        def _(part=part):
            outs[part][...] = jnp.dot(
                xs[part][...], down_ref[0], preferred_element_type=jnp.float32
            ).astype(outs[part].dtype)


def down_terms(xs, down):
    rows, hidden = xs[0].shape
    width = down.shape[2] // 4
    return pl.pallas_call(
        down_kernel,
        grid=(4,),
        out_shape=[jax.ShapeDtypeStruct((rows, width), jnp.bfloat16)] * 4,
        in_specs=[pl.BlockSpec((rows, hidden), lambda g: (0, 0))] * 4
        + [pl.BlockSpec((1, hidden, width), lambda g: (0, 0, g))],
        out_specs=[pl.BlockSpec((rows, width), lambda g: (0, 0))] * 4,
        compiler_params=pltpu.CompilerParams(vmem_limit_bytes=LIMIT),
    )(*xs, down)


def merge_kernel(*refs):
    terms, outs = refs[:6], refs[6:]
    rows, cols = outs[0].shape
    for k in range(2):
        for j in range(4):
            span = slice(j * rows, (j + 1) * rows)
            a, b, c = (terms[3 * k + n][span, :].astype(jnp.float32) for n in range(3))
            outs[j][:, k * (cols // 2) : (k + 1) * (cols // 2)] = (a + b + c).astype(
                outs[j].dtype
            )


def merge_terms(lo, hi):
    rows, width = lo[0].shape
    vmem = pl.BlockSpec(memory_space=pltpu.VMEM)
    return pl.pallas_call(
        merge_kernel,
        out_shape=[jax.ShapeDtypeStruct((rows // 4, 2 * width), jnp.bfloat16)] * 4,
        in_specs=[vmem] * 6,
        out_specs=[vmem] * 4,
        compiler_params=pltpu.CompilerParams(vmem_limit_bytes=LIMIT),
    )(*lo, *hi)


def shards(
    queries,
    keys,
    values,
    residual,
    norm_gain,
    out_weight,
    gate_weight,
    up_weight,
    down_weight,
    expert_ids,
    route_weights,
):
    n_tp = lax.axis_size("tp")
    n_ep = lax.axis_size("ep")
    n_etp = lax.axis_size("etp")
    tp, ep, etp = (lax.axis_index(name) for name in ("tp", "ep", "etp"))
    rows = queries.shape[0]
    chip, core = ep // 2, ep % 2
    half_q = queries.shape[1] // 2

    def halves(x):
        w = x.shape[1] // 2
        return jnp.where(core == 0, x[:, :w], x[:, w:]), jnp.where(core == 0, x[:, w:], x[:, :w])

    (own_k, other_k), (own_v, other_v), (own_q, other_q) = (
        halves(x) for x in (keys, values, queries)
    )
    swapped = swap_core(jnp.concatenate([other_k, other_v, other_q], axis=1))
    key_pair = jnp.concatenate([own_k, swapped[:, :HD]], axis=0)
    value_pair = jnp.concatenate([own_v, swapped[:, HD : 2 * HD]], axis=0).T
    other_q = swapped[:, 2 * HD :]
    tokens_dev = residual.shape[2]
    top = expert_ids.shape[-1]
    ids = expert_ids.reshape(tokens_dev, top)
    weights = route_weights.reshape(tokens_dev, top)
    routes = swap_core(jnp.concatenate([ids.astype(jnp.float32), weights], axis=1))
    key_pair, routes = lax.optimization_barrier((key_pair, routes))
    other_ids, other_weights = routes[:, :top].astype(jnp.int32), routes[:, top:]
    key_line = jnp.concatenate(gather_direct(key_pair, "etp"), axis=0)
    value_line = jnp.concatenate(gather_direct(value_pair, "ep", 2), axis=0)
    all_keys = gather_direct(key_line, "ep", 2)
    all_values = gather_direct(value_line, "etp")
    order = jnp.array(OFFSETS, jnp.int32)
    chips = (chip + order) % (n_ep // 2)
    depths = (etp + order) % n_etp
    cores = jnp.stack([core, 1 - core])
    places = (
        (2 * chips[:, None, None] + cores[None, None, :]) * n_etp + depths[None, :, None]
    ).reshape(-1)

    def for_block(block):
        return jnp.concatenate([places, block[None]]).astype(jnp.int32)

    me = ep * n_etp + etp
    far_block = (ep + 1 - 2 * core) * n_etp + etp
    lent = attend(for_block(far_block), other_q, all_keys, all_values)
    back = swap_core(lent)
    own_q, _ = lax.optimization_barrier((own_q, lent))
    kept = attend(for_block(me), own_q, all_keys, all_values)
    attention = jnp.concatenate(
        [jnp.where(core == 0, kept, back), jnp.where(core == 0, back, kept)], axis=1
    )
    near_weight = lax.dynamic_slice_in_dim(out_weight, core * half_q, half_q, 0)
    far_weight = lax.dynamic_slice_in_dim(out_weight, (1 - core) * half_q, half_q, 0)
    back_all = gather_direct(back, "etp")
    kept_all = gather_direct(kept, "etp")
    moe_rows = rows // n_tp
    cols = out_weight.shape[1]
    partial_proj = jnp.stack(
        [
            (
                jnp.dot(b, far_weight, preferred_element_type=jnp.float32)
                + jnp.dot(k, near_weight, preferred_element_type=jnp.float32)
            )
            .astype(jnp.bfloat16)
            .reshape(n_tp, moe_rows, cols)
            for b, k in zip(back_all, kept_all)
        ],
        axis=1,
    )

    def for_tp(by):
        at = (tp + by) % n_tp
        return lax.dynamic_slice_in_dim(partial_proj, at, 1, 0).reshape(n_etp * moe_rows, cols)

    summed = for_tp(0).astype(jnp.float32)
    for by in (1, -1, 2):
        summed = summed + shift(for_tp(by), "tp", by).astype(jnp.float32)
    summed = summed.astype(jnp.bfloat16).reshape(n_etp, moe_rows, cols)
    column_blocks = [summed[0]] + [
        shift(summed[j], "etp", OFFSETS[j]) for j in range(1, n_etp)
    ]
    sources = [(etp - OFFSETS[j]) % n_etp for j in range(n_etp)]
    projected = jnp.concatenate(
        [
            sum(
                jnp.where(sources[j] == q, column_blocks[j].astype(jnp.float32), 0.0)
                for j in range(n_etp)
            )
            for q in range(n_etp)
        ],
        axis=1,
    )
    model = n_etp * cols
    state = residual.reshape(moe_rows, model).astype(jnp.float32) + projected
    scale_rows = lax.rsqrt(jnp.mean(state * state, axis=-1, keepdims=True) + 1e-05)
    normed = (state * scale_rows * norm_gain).astype(jnp.bfloat16)
    experts = n_ep * gate_weight.shape[0]
    cap = max(2, min(moe_rows, 5 * moe_rows * top // (4 * experts)))
    place = jnp.concatenate(
        [pair_places(ids, 0, cap, experts), pair_places(other_ids, 1, cap, experts)], axis=0
    )
    match = place[:, :, None] == jnp.arange(experts * cap, dtype=jnp.int32)[None, None, :]
    dispatch = jnp.sum(match.astype(jnp.float32), axis=1).astype(jnp.bfloat16)
    pair_weights = jnp.concatenate([weights, other_weights], axis=0)
    combine = jnp.sum(jnp.where(match, pair_weights[:, :, None], 0.0), axis=1)
    hi, lo = split_bf16(combine)

    width = model // 4
    steps = n_ep // 2
    rows_step = 2 * cap
    pair = jnp.concatenate([normed, swap_core(normed)], axis=0)
    send = lax.dot_general(
        dispatch, pair, (((0,), (0,)), ((), ())), preferred_element_type=jnp.float32
    ).astype(jnp.bfloat16)
    pieces = [send[d * rows_step : (d + 1) * rows_step] for d in range(steps)]
    pieces = [pieces[0]] + [shift(pieces[d], "ep", 2 * d) for d in range(1, steps)]
    arrived = jnp.concatenate(pieces, axis=0)
    stacked = stack_blocks(
        gather_direct(arrived[:, : 2 * width], "tp")
        + gather_direct(arrived[:, 2 * width :], "etp")
    )

    far = ring_gather(stacked[:2], "etp") + ring_gather(stacked[2:], "tp")
    slots = experts * cap
    hidden = gate_weight.shape[2]
    early = lax.optimization_barrier([far[q][:3] for q in range(4)])
    sums = first_sums(early, gate_weight, up_weight)

    late = lax.optimization_barrier([far[q][3] for q in range(4)])
    inner_a, inner_b = inner_rows(late, sums, gate_weight, up_weight)
    inner_a = inner_a.reshape(4, 4 * slots, hidden)
    inner_b = inner_b.reshape(4, 4 * slots, hidden)
    over = down_terms([inner_a[3], inner_a[3], inner_b[3], inner_b[3]], down_weight)
    inner_a, inner_b, _ = lax.optimization_barrier((inner_a, inner_b, over))
    direct = down_terms([inner_a[1], inner_a[2], inner_b[1], inner_b[2]], down_weight)
    inner_a, inner_b, _ = lax.optimization_barrier((inner_a, inner_b, direct))
    passed = down_terms([inner_a[2], inner_a[1], inner_b[2], inner_b[1]], down_weight)
    kept_terms = down_terms([inner_a[0], inner_a[0], inner_b[0], inner_b[0]], down_weight)
    returned = []
    for half, (first, second) in enumerate((("tp", "etp"), ("etp", "tp"))):
        q0, q1 = 2 * half, 2 * half + 1
        over_lo, over_hi = shift(over[q0], second, 1), shift(over[q1], second, -1)
        far_sum_lo, far_sum_hi = add(passed[q0], over_lo), add(passed[q1], over_hi)
        next_lo, _ = lax.optimization_barrier((direct[q0], over_hi))
        next_hi, _ = lax.optimization_barrier((direct[q1], over_lo))
        got_lo, got_hi = shift(next_lo, second, -1), shift(next_hi, second, 1)
        last_lo = shift(far_sum_lo, second, 1)
        last_hi = shift(far_sum_hi, second, -1)
        blocks = merge_terms(
            (kept_terms[q0], got_lo, last_lo), (kept_terms[q1], got_hi, last_hi)
        )
        returned.append(
            add(blocks[0], *[shift(blocks[j], first, OFFSETS[j]) for j in range(1, 4)])
        )
    outs = jnp.concatenate(returned, axis=1)
    pieces = [outs[d * rows_step : (d + 1) * rows_step] for d in range(steps)]
    pieces = [pieces[0]] + [shift(pieces[d], "ep", -2 * d) for d in range(1, steps)]
    expert_rows = jnp.concatenate(pieces, axis=0)
    both = jnp.dot(hi, expert_rows, preferred_element_type=jnp.float32) + jnp.dot(
        lo, expert_rows, preferred_element_type=jnp.float32
    )
    theirs = swap_core(both[moe_rows:].astype(jnp.bfloat16))
    mixed = (state + both[:moe_rows] + theirs.astype(jnp.float32)).astype(jnp.bfloat16)
    return (attention, mixed.reshape(1, 1, moe_rows, model))


def solution(mesh):
    return jax.shard_map(
        shards,
        mesh=mesh,
        in_specs=(
            P(("ep", "etp"), "tp"),
            P(("ep", "etp"), "tp"),
            P(("ep", "etp"), "tp"),
            P(("ep", "etp"), "tp", None, None),
            P(),
            P("tp", "etp"),
            P("ep", None, ("tp", "etp")),
            P("ep", None, ("tp", "etp")),
            P("ep", ("tp", "etp"), None),
            P(("ep", "etp"), "tp", None, None),
            P(("ep", "etp"), "tp", None, None),
        ),
        out_specs=(P(("ep", "etp"), "tp"), P(("ep", "etp"), "tp", None, None)),
        check_vma=False,
    )
```

```python
import functools
import math

import jax
import jax.numpy as jnp
from jax import lax
from jax.experimental import pallas as pl
from jax.experimental.pallas import tpu as pltpu
from jax.sharding import PartitionSpec as P

HD = 128


def route_slots(ids, experts):
    tokens, top = ids.shape
    flat = ids.reshape(-1)
    hot = (flat[:, None] == jnp.arange(experts, dtype=jnp.int32)[None, :]).astype(jnp.int32)
    rank = jnp.cumsum(hot, axis=0) - hot
    return jnp.sum(rank * hot, axis=1).reshape(tokens, top)


def split_bf16(x):
    hi = x.astype(jnp.bfloat16)
    lo = (x - hi.astype(jnp.float32)).astype(jnp.bfloat16)
    return hi, lo


def shift(x, axis, by):
    n = lax.axis_size(axis)
    return lax.ppermute(x, axis, [(i, (i + by) % n) for i in range(n)])


def swap_core(x):
    n = lax.axis_size("ep")
    return lax.ppermute(x, "ep", [(i, i ^ 1) for i in range(n)])


def pair_places(ids, side, cap, experts):
    me = lax.axis_index("ep")
    chip = (ids // 2 - me // 2) % (experts // 2)
    place = chip * (2 * cap) + side * cap + route_slots(ids, experts)
    return jnp.where(ids % 2 == me % 2, place, -1)


def ring_gather(halves, axis):
    lo, hi = halves
    left_lo, right_hi = shift(lo, axis, 1), shift(hi, axis, -1)
    left_hi, right_lo = shift(hi, axis, 1), shift(lo, axis, -1)
    return (
        (lo, left_lo, right_lo, shift(left_lo, axis, 1)),
        (hi, left_hi, right_hi, shift(right_hi, axis, -1)),
    )


def add(*terms):
    return sum(t.astype(jnp.float32) for t in terms).astype(jnp.bfloat16)


def gather_direct(x, axis, step=1):
    return (
        x,
        shift(x, axis, step),
        shift(x, axis, -step),
        shift(x, axis, 2 * step),
    )


OFFSETS = (0, -1, 1, 2)


LIMIT = 52 * 2**20


def attend_kernel(scale, places_ref, q_ref, *refs):
    keys, vals = refs[:4], refs[4:8]
    out_ref, diff_ref, top_ref, sum_ref, acc_ref = refs[8:]
    depth, width = q_ref.shape
    rows = out_ref.shape[0]
    me = places_ref[32]
    top_ref[...] = jnp.full_like(top_ref, -1e20)
    sum_ref[...] = jnp.zeros_like(sum_ref)
    acc_ref[...] = jnp.zeros_like(acc_ref)
    diff_ref[...] = lax.broadcasted_iota(jnp.int32, (rows, width), 0) - (
        lax.broadcasted_iota(jnp.int32, (rows, width), 1) % rows
    )
    def line(i, masked):
        at = [places_ref[i * 8 + n] for n in range(8)]
        q = q_ref[...]
        scores = []
        for j in range(4):
            k = keys[i][j * 2 * rows : (j + 1) * 2 * rows, :]
            s = jnp.dot(k, q, preferred_element_type=jnp.float32) * scale
            if masked:
                s = jnp.concatenate(
                    [
                        jnp.where(
                            diff_ref[...] <= (me - at[2 * j + n]) * rows,
                            s[n * rows : (n + 1) * rows],
                            -1e30,
                        )
                        for n in range(2)
                    ],
                    axis=0,
                )
            scores.append(s)
        old = top_ref[...]
        new = old
        for s in scores:
            new = jnp.maximum(new, jnp.max(s, axis=0, keepdims=True))
        carry = jnp.exp2(old - new)
        total, acc = sum_ref[...] * carry, acc_ref[...] * carry
        for j, s in enumerate(scores):
            p = jnp.exp2(s - new)
            total += jnp.sum(p, axis=0, keepdims=True)
            acc += jnp.dot(
                vals[j][i * depth : (i + 1) * depth, :],
                p.astype(jnp.bfloat16),
                preferred_element_type=jnp.float32,
            )
        top_ref[...], sum_ref[...], acc_ref[...] = new, total, acc

    for i in range(4):
        least = most = places_ref[i * 8]
        for n in range(1, 8):
            least = jnp.minimum(least, places_ref[i * 8 + n])
            most = jnp.maximum(most, places_ref[i * 8 + n])
        pl.when(most < me)(functools.partial(line, i, False))
        pl.when(jnp.logical_and(most >= me, least <= me))(functools.partial(line, i, True))

    done = acc_ref[...] / sum_ref[...]
    for h in range(width // rows):
        out_ref[:, h * depth : (h + 1) * depth] = (
            done[:, h * rows : (h + 1) * rows].T.astype(out_ref.dtype)
        )


def attend(places, q, keys, vals):
    depth = keys[0].shape[1]
    heads = q.shape[1] // depth
    rows = q.shape[0]
    turned = jnp.transpose(q.reshape(rows, heads, depth), (2, 1, 0)).reshape(depth, heads * rows)
    vmem = pl.BlockSpec(memory_space=pltpu.VMEM)
    return pl.pallas_call(
        functools.partial(attend_kernel, math.log2(math.e) / math.sqrt(depth)),
        out_shape=jax.ShapeDtypeStruct(q.shape, q.dtype),
        in_specs=[pl.BlockSpec(memory_space=pltpu.SMEM)] + [vmem] * 9,
        out_specs=vmem,
        scratch_shapes=[
            pltpu.VMEM((rows, heads * rows), jnp.int32),
            pltpu.VMEM((1, heads * rows), jnp.float32),
            pltpu.VMEM((1, heads * rows), jnp.float32),
            pltpu.VMEM((depth, heads * rows), jnp.float32),
        ],
        compiler_params=pltpu.CompilerParams(vmem_limit_bytes=LIMIT),
        cost_estimate=pl.CostEstimate(
            flops=4 * heads * rows * 32 * rows * depth,
            bytes_accessed=4 * 32 * rows * depth,
            transcendentals=heads * rows * 32 * rows,
        ),
    )(places, turned, *keys, *vals)


def stack_kernel(*refs):
    ins, outs = refs[:8], refs[8:]
    rows, cols = ins[0].shape
    for half in range(2):
        for j in range(4):
            for k in range(2):
                outs[2 * half + k][j * rows : (j + 1) * rows, :] = ins[4 * half + j][
                    :, k * (cols // 2) : (k + 1) * (cols // 2)
                ]


def stack_blocks(blocks):
    rows, cols = blocks[0].shape
    vmem = pl.BlockSpec(memory_space=pltpu.VMEM)
    return pl.pallas_call(
        stack_kernel,
        out_shape=[jax.ShapeDtypeStruct((4 * rows, cols // 2), blocks[0].dtype)] * 4,
        in_specs=[vmem] * 8,
        out_specs=[vmem] * 4,
        compiler_params=pltpu.CompilerParams(vmem_limit_bytes=LIMIT),
    )(*blocks)


def swish_product(gate_v, up_v):
    return (gate_v / (1.0 + jnp.exp(-gate_v)) * up_v).astype(jnp.bfloat16)


def first_sums_kernel(*refs):
    blocks, (gate_ref, up_ref, rest_ref, in_a_ref, in_b_ref, total_ref) = refs[:12], refs[12:]
    step = pl.program_id(0)
    rows, hidden = blocks[0].shape[0], gate_ref.shape[-1]
    quarter = rows // 4

    @pl.when(step == 0)
    def _():
        total_ref[...] = jnp.zeros_like(total_ref)

    for part in range(4):

        @pl.when(step // 2 == part)
        def _(part=part):
            for j in range(3):
                x = blocks[3 * part + j][...]
                for n, weight in enumerate((gate_ref, up_ref)):
                    span = slice(n * hidden, (n + 1) * hidden)
                    y = jnp.dot(x, weight[0], preferred_element_type=jnp.float32)
                    if part < 2:
                        total_ref[j * rows : (j + 1) * rows, span] += y
                    else:
                        for i in range(4):
                            at = (i * 4 + j) * quarter
                            total_ref[at : at + quarter, span] += y[i * quarter : (i + 1) * quarter]

    @pl.when(step == 7)
    def _():
        in_a_ref[...] = jnp.zeros_like(in_a_ref)
        in_b_ref[...] = jnp.zeros_like(in_b_ref)
        rest_ref[:rows, :] = total_ref[3 * rows :, :]
        for i in range(3):
            at = (4 * i + 3) * quarter
            rest_ref[rows + i * quarter : rows + (i + 1) * quarter, :] = total_ref[
                at : at + quarter, :
            ]
            for j in range(3):
                at, to = (4 * i + j) * quarter, (4 * j + i) * quarter
                inner = swish_product(
                    total_ref[at : at + quarter, :hidden], total_ref[at : at + quarter, hidden:]
                )
                in_a_ref[at : at + quarter, :] = inner
                in_b_ref[to : to + quarter, :] = inner


def part_spec(part, rows, sub):
    return pl.BlockSpec((rows, sub), lambda g: (0, jnp.clip(g - 2 * part, 0, 1)))


def first_sums(blocks, gate, up):
    rows, width = blocks[0][0].shape
    hidden = gate.shape[2]
    sub = width // 2
    weight = pl.BlockSpec((1, sub, hidden), lambda g: (0, jnp.minimum(g, 7), 0))
    rest = 7 * rows // 4

    def fixed(r, c):
        return pl.BlockSpec((r, c), lambda g: (0, 0))

    return pl.pallas_call(
        first_sums_kernel,
        grid=(8,),
        out_shape=[
            jax.ShapeDtypeStruct((rest, 2 * hidden), jnp.float32),
            jax.ShapeDtypeStruct((3 * rows, hidden), jnp.bfloat16),
            jax.ShapeDtypeStruct((3 * rows, hidden), jnp.bfloat16),
        ],
        in_specs=[part_spec(part, rows, sub) for part in range(4) for _ in range(3)]
        + [weight, weight],
        out_specs=[fixed(rest, 2 * hidden), fixed(3 * rows, hidden), fixed(3 * rows, hidden)],
        scratch_shapes=[pltpu.VMEM((4 * rows, 2 * hidden), jnp.float32)],
        compiler_params=pltpu.CompilerParams(vmem_limit_bytes=LIMIT),
    )(*[x for part in blocks for x in part], gate, up)


def last_sums_kernel(*refs):
    blocks, refs = refs[:4], refs[4:]
    rest_ref, early_a_ref, early_b_ref, gate_ref, up_ref, down_ref = refs[:6]
    (in_a_ref, in_b_ref), outs = refs[6:8], refs[8:12]
    total_ref, far_a_ref, far_b_ref = refs[12:]
    step = pl.program_id(0)
    rows, hidden = blocks[0].shape[0], gate_ref.shape[-1]
    quarter = rows // 4

    @pl.when(step == 0)
    def _():
        total_ref[...] = rest_ref[...]
        in_a_ref[...] = early_a_ref[...]
        in_b_ref[...] = early_b_ref[...]

    for part in range(4):

        @pl.when(step // 2 == part)
        def _(part=part):
            x = blocks[part][...]
            for n, weight in enumerate((gate_ref, up_ref)):
                span = slice(n * hidden, (n + 1) * hidden)
                y = jnp.dot(x, weight[0], preferred_element_type=jnp.float32)
                if part < 2:
                    total_ref[:rows, span] += y
                else:
                    total_ref[rows:, span] += y[: 3 * quarter]
                    total_ref[3 * quarter : rows, span] += y[3 * quarter :]

    @pl.when(step == 7)
    def _():
        for i in range(7):
            at = i * quarter
            inner = swish_product(
                total_ref[at : at + quarter, :hidden], total_ref[at : at + quarter, hidden:]
            )
            if i < 4:
                far_a_ref[at : at + quarter, :] = inner
                if i < 3:
                    to = (4 * i + 3) * quarter
                    in_b_ref[to : to + quarter, :] = inner
                else:
                    far_b_ref[3 * quarter :, :] = inner
            else:
                to = (i - 4) * quarter
                far_b_ref[to : to + quarter, :] = inner
                to = (4 * (i - 4) + 3) * quarter
                in_a_ref[to : to + quarter, :] = inner

    for part in range(4):

        @pl.when(step == 8 + part)
        def _(part=part):
            x = (far_a_ref if part < 2 else far_b_ref)[...]
            outs[part][...] = jnp.dot(
                x, down_ref[0], preferred_element_type=jnp.float32
            ).astype(outs[part].dtype)


def last_sums(blocks, rest, early_a, early_b, gate, up, down):
    rows, width = blocks[0].shape
    hidden = gate.shape[2]
    sub = width // 2
    weight = pl.BlockSpec((1, sub, hidden), lambda g: (0, jnp.minimum(g, 7), 0))
    near = pl.BlockSpec((3 * rows, hidden), lambda g: (0, 0))
    term = pl.BlockSpec((rows, width), lambda g: (0, 0))
    outs = pl.pallas_call(
        last_sums_kernel,
        grid=(12,),
        out_shape=[jax.ShapeDtypeStruct((3 * rows, hidden), jnp.bfloat16)] * 2
        + [jax.ShapeDtypeStruct((rows, width), jnp.bfloat16)] * 4,
        in_specs=[part_spec(part, rows, sub) for part in range(4)]
        + [
            pl.BlockSpec(rest.shape, lambda g: (0, 0)),
            near,
            near,
            weight,
            weight,
            pl.BlockSpec((1, hidden, width), lambda g: (0, 0, jnp.clip(g - 8, 0, 3))),
        ],
        out_specs=[near, near] + [term] * 4,
        scratch_shapes=[
            pltpu.VMEM(rest.shape, jnp.float32),
            pltpu.VMEM((rows, hidden), jnp.bfloat16),
            pltpu.VMEM((rows, hidden), jnp.bfloat16),
        ],
        compiler_params=pltpu.CompilerParams(vmem_limit_bytes=LIMIT),
    )(*blocks, rest, early_a, early_b, gate, up, down)
    return outs[0].reshape(3, rows, hidden), outs[1].reshape(3, rows, hidden), outs[2:]


def down_kernel(*refs):
    xs, down_ref, outs = refs[:4], refs[4], refs[5:]
    for part in range(4):

        @pl.when(pl.program_id(0) == part)
        def _(part=part):
            outs[part][...] = jnp.dot(
                xs[part][...], down_ref[0], preferred_element_type=jnp.float32
            ).astype(outs[part].dtype)


def down_terms(xs, down):
    rows, hidden = xs[0].shape
    width = down.shape[2] // 4
    return pl.pallas_call(
        down_kernel,
        grid=(4,),
        out_shape=[jax.ShapeDtypeStruct((rows, width), jnp.bfloat16)] * 4,
        in_specs=[pl.BlockSpec((rows, hidden), lambda g: (0, 0))] * 4
        + [pl.BlockSpec((1, hidden, width), lambda g: (0, 0, g))],
        out_specs=[pl.BlockSpec((rows, width), lambda g: (0, 0))] * 4,
        compiler_params=pltpu.CompilerParams(vmem_limit_bytes=LIMIT),
    )(*xs, down)


def merge_kernel(*refs):
    terms, outs = refs[:6], refs[6:]
    rows, cols = outs[0].shape
    for k in range(2):
        for j in range(4):
            span = slice(j * rows, (j + 1) * rows)
            a, b, c = (terms[3 * k + n][span, :].astype(jnp.float32) for n in range(3))
            outs[j][:, k * (cols // 2) : (k + 1) * (cols // 2)] = (a + b + c).astype(
                outs[j].dtype
            )


def merge_terms(lo, hi):
    rows, width = lo[0].shape
    vmem = pl.BlockSpec(memory_space=pltpu.VMEM)
    return pl.pallas_call(
        merge_kernel,
        out_shape=[jax.ShapeDtypeStruct((rows // 4, 2 * width), jnp.bfloat16)] * 4,
        in_specs=[vmem] * 6,
        out_specs=[vmem] * 4,
        compiler_params=pltpu.CompilerParams(vmem_limit_bytes=LIMIT),
    )(*lo, *hi)


def shards(
    queries,
    keys,
    values,
    residual,
    norm_gain,
    out_weight,
    gate_weight,
    up_weight,
    down_weight,
    expert_ids,
    route_weights,
):
    n_tp = lax.axis_size("tp")
    n_ep = lax.axis_size("ep")
    n_etp = lax.axis_size("etp")
    tp, ep, etp = (lax.axis_index(name) for name in ("tp", "ep", "etp"))
    rows = queries.shape[0]
    chip, core = ep // 2, ep % 2
    half_q = queries.shape[1] // 2

    def halves(x):
        w = x.shape[1] // 2
        return jnp.where(core == 0, x[:, :w], x[:, w:]), jnp.where(core == 0, x[:, w:], x[:, :w])

    (own_k, other_k), (own_v, other_v), (own_q, other_q) = (
        halves(x) for x in (keys, values, queries)
    )
    swapped = swap_core(jnp.concatenate([other_k, other_v, other_q], axis=1))
    key_pair = jnp.concatenate([own_k, swapped[:, :HD]], axis=0)
    value_pair = jnp.concatenate([own_v, swapped[:, HD : 2 * HD]], axis=0).T
    other_q = swapped[:, 2 * HD :]
    tokens_dev = residual.shape[2]
    top = expert_ids.shape[-1]
    ids = expert_ids.reshape(tokens_dev, top)
    weights = route_weights.reshape(tokens_dev, top)
    routes = swap_core(jnp.concatenate([ids.astype(jnp.float32), weights], axis=1))
    key_pair, routes = lax.optimization_barrier((key_pair, routes))
    other_ids, other_weights = routes[:, :top].astype(jnp.int32), routes[:, top:]
    key_line = jnp.concatenate(gather_direct(key_pair, "etp"), axis=0)
    value_line = jnp.concatenate(gather_direct(value_pair, "ep", 2), axis=0)
    all_keys = gather_direct(key_line, "ep", 2)
    all_values = gather_direct(value_line, "etp")
    order = jnp.array(OFFSETS, jnp.int32)
    chips = (chip + order) % (n_ep // 2)
    depths = (etp + order) % n_etp
    cores = jnp.stack([core, 1 - core])
    places = (
        (2 * chips[:, None, None] + cores[None, None, :]) * n_etp + depths[None, :, None]
    ).reshape(-1)

    def for_block(block):
        return jnp.concatenate([places, block[None]]).astype(jnp.int32)

    me = ep * n_etp + etp
    far_block = (ep + 1 - 2 * core) * n_etp + etp
    lent = attend(for_block(far_block), other_q, all_keys, all_values)

    def to_other_core(by):
        pairs = [
            (e * n_etp + z, (e ^ 1) * n_etp + (z + by) % n_etp)
            for e in range(n_ep)
            for z in range(n_etp)
        ]
        return lax.ppermute(lent, ("ep", "etp"), pairs)

    back_all = [to_other_core(by) for by in (0, 1, -1, 2)]
    back = back_all[0]
    own_q, _ = lax.optimization_barrier((own_q, lent))
    kept = attend(for_block(me), own_q, all_keys, all_values)
    attention = jnp.concatenate(
        [jnp.where(core == 0, kept, back), jnp.where(core == 0, back, kept)], axis=1
    )
    near_weight = lax.dynamic_slice_in_dim(out_weight, core * half_q, half_q, 0)
    far_weight = lax.dynamic_slice_in_dim(out_weight, (1 - core) * half_q, half_q, 0)
    kept_all = gather_direct(kept, "etp")
    moe_rows = rows // n_tp
    cols = out_weight.shape[1]
    partial_proj = jnp.stack(
        [
            (
                jnp.dot(b, far_weight, preferred_element_type=jnp.float32)
                + jnp.dot(k, near_weight, preferred_element_type=jnp.float32)
            )
            .astype(jnp.bfloat16)
            .reshape(n_tp, moe_rows, cols)
            for b, k in zip(back_all, kept_all)
        ],
        axis=1,
    )

    def for_tp(by):
        at = (tp + by) % n_tp
        return lax.dynamic_slice_in_dim(partial_proj, at, 1, 0).reshape(n_etp * moe_rows, cols)

    summed = for_tp(0).astype(jnp.float32)
    for by in (1, -1, 2):
        summed = summed + shift(for_tp(by), "tp", by).astype(jnp.float32)
    summed = summed.astype(jnp.bfloat16).reshape(n_etp, moe_rows, cols)
    column_blocks = [summed[0]] + [
        shift(summed[j], "etp", OFFSETS[j]) for j in range(1, n_etp)
    ]
    sources = [(etp - OFFSETS[j]) % n_etp for j in range(n_etp)]
    projected = jnp.concatenate(
        [
            sum(
                jnp.where(sources[j] == q, column_blocks[j].astype(jnp.float32), 0.0)
                for j in range(n_etp)
            )
            for q in range(n_etp)
        ],
        axis=1,
    )
    model = n_etp * cols
    state = residual.reshape(moe_rows, model).astype(jnp.float32) + projected
    scale_rows = lax.rsqrt(jnp.mean(state * state, axis=-1, keepdims=True) + 1e-05)
    normed = (state * scale_rows * norm_gain).astype(jnp.bfloat16)
    experts = n_ep * gate_weight.shape[0]
    cap = max(2, min(moe_rows, 5 * moe_rows * top // (4 * experts)))
    place = jnp.concatenate(
        [pair_places(ids, 0, cap, experts), pair_places(other_ids, 1, cap, experts)], axis=0
    )
    match = place[:, :, None] == jnp.arange(experts * cap, dtype=jnp.int32)[None, None, :]
    dispatch = jnp.sum(match.astype(jnp.float32), axis=1).astype(jnp.bfloat16)
    pair_weights = jnp.concatenate([weights, other_weights], axis=0)
    combine = jnp.sum(jnp.where(match, pair_weights[:, :, None], 0.0), axis=1)
    hi, lo = split_bf16(combine)

    width = model // 4
    steps = n_ep // 2
    rows_step = 2 * cap
    pair = jnp.concatenate([normed, swap_core(normed)], axis=0)
    send = lax.dot_general(
        dispatch, pair, (((0,), (0,)), ((), ())), preferred_element_type=jnp.float32
    ).astype(jnp.bfloat16)
    pieces = [send[d * rows_step : (d + 1) * rows_step] for d in range(steps)]
    pieces = [pieces[0]] + [shift(pieces[d], "ep", 2 * d) for d in range(1, steps)]
    arrived = jnp.concatenate(pieces, axis=0)
    stacked = stack_blocks(
        gather_direct(arrived[:, : 2 * width], "tp")
        + gather_direct(arrived[:, 2 * width :], "etp")
    )

    far = ring_gather(stacked[:2], "etp") + ring_gather(stacked[2:], "tp")
    early = lax.optimization_barrier([far[q][:3] for q in range(4)])
    rest, early_a, early_b = first_sums(early, gate_weight, up_weight)
    late = lax.optimization_barrier([far[q][3] for q in range(4)])
    inner_a, inner_b, over = last_sums(
        late, rest, early_a, early_b, gate_weight, up_weight, down_weight
    )
    inner_a, inner_b, _ = lax.optimization_barrier((inner_a, inner_b, over))
    direct = down_terms([inner_a[1], inner_a[2], inner_b[1], inner_b[2]], down_weight)
    inner_a, inner_b, _ = lax.optimization_barrier((inner_a, inner_b, direct))
    passed = down_terms([inner_a[2], inner_a[1], inner_b[2], inner_b[1]], down_weight)
    kept_terms = down_terms([inner_a[0], inner_a[0], inner_b[0], inner_b[0]], down_weight)
    returned = []
    for half, (first, second) in enumerate((("tp", "etp"), ("etp", "tp"))):
        q0, q1 = 2 * half, 2 * half + 1
        over_lo, over_hi = shift(over[q0], second, 1), shift(over[q1], second, -1)
        far_sum_lo, far_sum_hi = add(passed[q0], over_lo), add(passed[q1], over_hi)
        next_lo, _ = lax.optimization_barrier((direct[q0], over_hi))
        next_hi, _ = lax.optimization_barrier((direct[q1], over_lo))
        got_lo, got_hi = shift(next_lo, second, -1), shift(next_hi, second, 1)
        last_lo = shift(far_sum_lo, second, 1)
        last_hi = shift(far_sum_hi, second, -1)
        blocks = merge_terms(
            (kept_terms[q0], got_lo, last_lo), (kept_terms[q1], got_hi, last_hi)
        )
        returned.append(
            add(blocks[0], *[shift(blocks[j], first, OFFSETS[j]) for j in range(1, 4)])
        )
    outs = jnp.concatenate(returned, axis=1)
    pieces = [outs[d * rows_step : (d + 1) * rows_step] for d in range(steps)]
    pieces = [pieces[0]] + [shift(pieces[d], "ep", -2 * d) for d in range(1, steps)]
    expert_rows = jnp.concatenate(pieces, axis=0)
    both = jnp.dot(hi, expert_rows, preferred_element_type=jnp.float32) + jnp.dot(
        lo, expert_rows, preferred_element_type=jnp.float32
    )
    theirs = swap_core(both[moe_rows:].astype(jnp.bfloat16))
    mixed = (state + both[:moe_rows] + theirs.astype(jnp.float32)).astype(jnp.bfloat16)
    return (attention, mixed.reshape(1, 1, moe_rows, model))


def solution(mesh):
    return jax.shard_map(
        shards,
        mesh=mesh,
        in_specs=(
            P(("ep", "etp"), "tp"),
            P(("ep", "etp"), "tp"),
            P(("ep", "etp"), "tp"),
            P(("ep", "etp"), "tp", None, None),
            P(),
            P("tp", "etp"),
            P("ep", None, ("tp", "etp")),
            P("ep", None, ("tp", "etp")),
            P("ep", ("tp", "etp"), None),
            P(("ep", "etp"), "tp", None, None),
            P(("ep", "etp"), "tp", None, None),
        ),
        out_specs=(P(("ep", "etp"), "tp"), P(("ep", "etp"), "tp", None, None)),
        check_vma=False,
    )
```

```python
import functools
import math

import jax
import jax.numpy as jnp
from jax import lax
from jax.experimental import pallas as pl
from jax.experimental.pallas import tpu as pltpu
from jax.sharding import PartitionSpec as P

HD = 128


def route_slots(ids, experts):
    tokens, top = ids.shape
    flat = ids.reshape(-1)
    hot = (flat[:, None] == jnp.arange(experts, dtype=jnp.int32)[None, :]).astype(jnp.int32)
    rank = jnp.cumsum(hot, axis=0) - hot
    return jnp.sum(rank * hot, axis=1).reshape(tokens, top)


def split_bf16(x):
    hi = x.astype(jnp.bfloat16)
    lo = (x - hi.astype(jnp.float32)).astype(jnp.bfloat16)
    return hi, lo


def shift(x, axis, by):
    n = lax.axis_size(axis)
    return lax.ppermute(x, axis, [(i, (i + by) % n) for i in range(n)])


def swap_core(x):
    n = lax.axis_size("ep")
    return lax.ppermute(x, "ep", [(i, i ^ 1) for i in range(n)])


def pair_places(ids, side, cap, experts):
    me = lax.axis_index("ep")
    chip = (ids // 2 - me // 2) % (experts // 2)
    place = chip * (2 * cap) + side * cap + route_slots(ids, experts)
    return jnp.where(ids % 2 == me % 2, place, -1)


def ring_gather(halves, axis):
    lo, hi = halves
    left_lo, right_hi = shift(lo, axis, 1), shift(hi, axis, -1)
    left_hi, right_lo = shift(hi, axis, 1), shift(lo, axis, -1)
    return (
        (lo, left_lo, right_lo, shift(left_lo, axis, 1)),
        (hi, left_hi, right_hi, shift(right_hi, axis, -1)),
    )


def add(*terms):
    return sum(t.astype(jnp.float32) for t in terms).astype(jnp.bfloat16)


def gather_direct(x, axis, step=1):
    return (
        x,
        shift(x, axis, step),
        shift(x, axis, -step),
        shift(x, axis, 2 * step),
    )


OFFSETS = (0, -1, 1, 2)


MIB = 2**20


def attend_kernel(scale, places_ref, q_ref, *refs):
    keys, vals = refs[:4], refs[4:8]
    outs, (diff_ref, top_ref, sum_ref, acc_ref) = refs[8:10], refs[10:]
    depth, width = q_ref.shape
    rows = outs[0].shape[0]
    half = width // 2
    mine, other = places_ref[32], places_ref[33]
    low, high = jnp.minimum(mine, other), jnp.maximum(mine, other)
    top_ref[...] = jnp.full_like(top_ref, -1e20)
    sum_ref[...] = jnp.zeros_like(sum_ref)
    acc_ref[...] = jnp.zeros_like(acc_ref)
    for n, block in enumerate((mine, other)):
        col = lax.broadcasted_iota(jnp.int32, (rows, half), 1) % rows
        row = lax.broadcasted_iota(jnp.int32, (rows, half), 0)
        diff_ref[:, n * half : (n + 1) * half] = row - col - block * rows

    def line(i, masked):
        at = [places_ref[i * 8 + n] for n in range(8)]
        q = q_ref[...]
        scores = []
        for j in range(4):
            k = keys[i][j * 2 * rows : (j + 1) * 2 * rows, :]
            s = jnp.dot(k, q, preferred_element_type=jnp.float32) * scale
            if masked:
                s = jnp.concatenate(
                    [
                        jnp.where(
                            diff_ref[...] <= -at[2 * j + n] * rows,
                            s[n * rows : (n + 1) * rows],
                            -1e30,
                        )
                        for n in range(2)
                    ],
                    axis=0,
                )
            scores.append(s)
        old = top_ref[...]
        new = old
        for s in scores:
            new = jnp.maximum(new, jnp.max(s, axis=0, keepdims=True))
        carry = jnp.exp2(old - new)
        total, acc = sum_ref[...] * carry, acc_ref[...] * carry
        for j, s in enumerate(scores):
            p = jnp.exp2(s - new)
            total += jnp.sum(p, axis=0, keepdims=True)
            acc += jnp.dot(
                vals[j][i * depth : (i + 1) * depth, :],
                p.astype(jnp.bfloat16),
                preferred_element_type=jnp.float32,
            )
        top_ref[...], sum_ref[...], acc_ref[...] = new, total, acc

    for i in range(4):
        least = most = places_ref[i * 8]
        for n in range(1, 8):
            least = jnp.minimum(least, places_ref[i * 8 + n])
            most = jnp.maximum(most, places_ref[i * 8 + n])
        pl.when(most < low)(functools.partial(line, i, False))
        pl.when(jnp.logical_and(most >= low, least <= high))(functools.partial(line, i, True))

    done = acc_ref[...] / sum_ref[...]
    for n in range(2):
        for h in range(half // rows):
            at = n * half + h * rows
            outs[n][:, h * depth : (h + 1) * depth] = done[:, at : at + rows].T.astype(
                outs[n].dtype
            )


def attend(places, queries, keys, vals):
    depth = keys[0].shape[1]
    rows, width = queries[0].shape
    heads = width // depth
    turned = jnp.concatenate(
        [
            jnp.transpose(q.reshape(rows, heads, depth), (2, 1, 0)).reshape(depth, heads * rows)
            for q in queries
        ],
        axis=1,
    )
    vmem = pl.BlockSpec(memory_space=pltpu.VMEM)
    columns = 2 * heads * rows
    return pl.pallas_call(
        functools.partial(attend_kernel, math.log2(math.e) / math.sqrt(depth)),
        out_shape=[jax.ShapeDtypeStruct(q.shape, q.dtype) for q in queries],
        in_specs=[pl.BlockSpec(memory_space=pltpu.SMEM)] + [vmem] * 9,
        out_specs=[vmem] * 2,
        scratch_shapes=[
            pltpu.VMEM((rows, columns), jnp.int32),
            pltpu.VMEM((1, columns), jnp.float32),
            pltpu.VMEM((1, columns), jnp.float32),
            pltpu.VMEM((depth, columns), jnp.float32),
        ],
        compiler_params=pltpu.CompilerParams(vmem_limit_bytes=40 * MIB),
        cost_estimate=pl.CostEstimate(
            flops=4 * columns * 32 * rows * depth,
            bytes_accessed=4 * 32 * rows * depth,
            transcendentals=columns * 32 * rows,
        ),
    )(places, turned, *keys, *vals)


def stack_kernel(*refs):
    ins, outs = refs[:8], refs[8:]
    rows, cols = ins[0].shape
    for half in range(2):
        for j in range(4):
            for k in range(2):
                outs[2 * half + k][j * rows : (j + 1) * rows, :] = ins[4 * half + j][
                    :, k * (cols // 2) : (k + 1) * (cols // 2)
                ]


def stack_blocks(blocks):
    rows, cols = blocks[0].shape
    vmem = pl.BlockSpec(memory_space=pltpu.VMEM)
    return pl.pallas_call(
        stack_kernel,
        out_shape=[jax.ShapeDtypeStruct((4 * rows, cols // 2), blocks[0].dtype)] * 4,
        in_specs=[vmem] * 8,
        out_specs=[vmem] * 4,
        compiler_params=pltpu.CompilerParams(vmem_limit_bytes=12 * MIB),
    )(*blocks)


def swish_product(gate_v, up_v):
    return (gate_v / (1.0 + jnp.exp(-gate_v)) * up_v).astype(jnp.bfloat16)


def first_sums_kernel(*refs):
    blocks, (gate_ref, up_ref, rest_ref, in_a_ref, in_b_ref, total_ref) = refs[:12], refs[12:]
    step = pl.program_id(0)
    rows, hidden = blocks[0].shape[0], gate_ref.shape[-1]
    quarter = rows // 4

    @pl.when(step == 0)
    def _():
        total_ref[...] = jnp.zeros_like(total_ref)

    for part in range(4):

        @pl.when(step // 2 == part)
        def _(part=part):
            for j in range(3):
                x = blocks[3 * part + j][...]
                for n, weight in enumerate((gate_ref, up_ref)):
                    span = slice(n * hidden, (n + 1) * hidden)
                    y = jnp.dot(x, weight[0], preferred_element_type=jnp.float32)
                    if part < 2:
                        total_ref[j * rows : (j + 1) * rows, span] += y
                    else:
                        for i in range(4):
                            at = (i * 4 + j) * quarter
                            total_ref[at : at + quarter, span] += y[i * quarter : (i + 1) * quarter]

    @pl.when(step == 7)
    def _():
        in_a_ref[...] = jnp.zeros_like(in_a_ref)
        in_b_ref[...] = jnp.zeros_like(in_b_ref)
        rest_ref[:rows, :] = total_ref[3 * rows :, :]
        for i in range(3):
            at = (4 * i + 3) * quarter
            rest_ref[rows + i * quarter : rows + (i + 1) * quarter, :] = total_ref[
                at : at + quarter, :
            ]
            for j in range(3):
                at, to = (4 * i + j) * quarter, (4 * j + i) * quarter
                inner = swish_product(
                    total_ref[at : at + quarter, :hidden], total_ref[at : at + quarter, hidden:]
                )
                in_a_ref[at : at + quarter, :] = inner
                in_b_ref[to : to + quarter, :] = inner


def part_spec(part, rows, sub):
    return pl.BlockSpec((rows, sub), lambda g: (0, jnp.clip(g - 2 * part, 0, 1)))


def first_sums(blocks, gate, up):
    rows, width = blocks[0][0].shape
    hidden = gate.shape[2]
    sub = width // 2
    weight = pl.BlockSpec((1, sub, hidden), lambda g: (0, jnp.minimum(g, 7), 0))
    rest = 7 * rows // 4

    def fixed(r, c):
        return pl.BlockSpec((r, c), lambda g: (0, 0))

    return pl.pallas_call(
        first_sums_kernel,
        grid=(8,),
        out_shape=[
            jax.ShapeDtypeStruct((rest, 2 * hidden), jnp.float32),
            jax.ShapeDtypeStruct((3 * rows, hidden), jnp.bfloat16),
            jax.ShapeDtypeStruct((3 * rows, hidden), jnp.bfloat16),
        ],
        in_specs=[part_spec(part, rows, sub) for part in range(4) for _ in range(3)]
        + [weight, weight],
        out_specs=[fixed(rest, 2 * hidden), fixed(3 * rows, hidden), fixed(3 * rows, hidden)],
        scratch_shapes=[pltpu.VMEM((4 * rows, 2 * hidden), jnp.float32)],
        compiler_params=pltpu.CompilerParams(vmem_limit_bytes=34 * MIB),
    )(*[x for part in blocks for x in part], gate, up)


def last_sums_kernel(*refs):
    blocks, refs = refs[:4], refs[4:]
    rest_ref, early_a_ref, early_b_ref, gate_ref, up_ref, down_ref = refs[:6]
    (in_a_ref, in_b_ref), outs = refs[6:8], refs[8:12]
    total_ref, far_a_ref, far_b_ref = refs[12:]
    step = pl.program_id(0)
    rows, hidden = blocks[0].shape[0], gate_ref.shape[-1]
    quarter = rows // 4

    @pl.when(step == 0)
    def _():
        total_ref[...] = rest_ref[...]
        in_a_ref[...] = early_a_ref[...]
        in_b_ref[...] = early_b_ref[...]

    for part in range(4):

        @pl.when(step // 2 == part)
        def _(part=part):
            x = blocks[part][...]
            for n, weight in enumerate((gate_ref, up_ref)):
                span = slice(n * hidden, (n + 1) * hidden)
                y = jnp.dot(x, weight[0], preferred_element_type=jnp.float32)
                if part < 2:
                    total_ref[:rows, span] += y
                else:
                    total_ref[rows:, span] += y[: 3 * quarter]
                    total_ref[3 * quarter : rows, span] += y[3 * quarter :]

    @pl.when(step == 7)
    def _():
        for i in range(7):
            at = i * quarter
            inner = swish_product(
                total_ref[at : at + quarter, :hidden], total_ref[at : at + quarter, hidden:]
            )
            if i < 4:
                far_a_ref[at : at + quarter, :] = inner
                if i < 3:
                    to = (4 * i + 3) * quarter
                    in_b_ref[to : to + quarter, :] = inner
                else:
                    far_b_ref[3 * quarter :, :] = inner
            else:
                to = (i - 4) * quarter
                far_b_ref[to : to + quarter, :] = inner
                to = (4 * (i - 4) + 3) * quarter
                in_a_ref[to : to + quarter, :] = inner

    for part in range(4):

        @pl.when(step == 8 + part)
        def _(part=part):
            x = (far_a_ref if part < 2 else far_b_ref)[...]
            outs[part][...] = jnp.dot(
                x, down_ref[0], preferred_element_type=jnp.float32
            ).astype(outs[part].dtype)


def last_sums(blocks, rest, early_a, early_b, gate, up, down):
    rows, width = blocks[0].shape
    hidden = gate.shape[2]
    sub = width // 2
    weight = pl.BlockSpec((1, sub, hidden), lambda g: (0, jnp.minimum(g, 7), 0))
    near = pl.BlockSpec((3 * rows, hidden), lambda g: (0, 0))
    term = pl.BlockSpec((rows, width), lambda g: (0, 0))
    outs = pl.pallas_call(
        last_sums_kernel,
        grid=(12,),
        out_shape=[jax.ShapeDtypeStruct((3 * rows, hidden), jnp.bfloat16)] * 2
        + [jax.ShapeDtypeStruct((rows, width), jnp.bfloat16)] * 4,
        in_specs=[part_spec(part, rows, sub) for part in range(4)]
        + [
            pl.BlockSpec(rest.shape, lambda g: (0, 0)),
            near,
            near,
            weight,
            weight,
            pl.BlockSpec((1, hidden, width), lambda g: (0, 0, jnp.clip(g - 8, 0, 3))),
        ],
        out_specs=[near, near] + [term] * 4,
        scratch_shapes=[
            pltpu.VMEM(rest.shape, jnp.float32),
            pltpu.VMEM((rows, hidden), jnp.bfloat16),
            pltpu.VMEM((rows, hidden), jnp.bfloat16),
        ],
        compiler_params=pltpu.CompilerParams(vmem_limit_bytes=34 * MIB),
    )(*blocks, rest, early_a, early_b, gate, up, down)
    return outs[0].reshape(3, rows, hidden), outs[1].reshape(3, rows, hidden), outs[2:]


def down_kernel(*refs):
    xs, down_ref, outs = refs[:4], refs[4], refs[5:]
    for part in range(4):

        @pl.when(pl.program_id(0) == part)
        def _(part=part):
            outs[part][...] = jnp.dot(
                xs[part][...], down_ref[0], preferred_element_type=jnp.float32
            ).astype(outs[part].dtype)


def down_terms(xs, down):
    rows, hidden = xs[0].shape
    width = down.shape[2] // 4
    return pl.pallas_call(
        down_kernel,
        grid=(4,),
        out_shape=[jax.ShapeDtypeStruct((rows, width), jnp.bfloat16)] * 4,
        in_specs=[pl.BlockSpec((rows, hidden), lambda g: (0, 0))] * 4
        + [pl.BlockSpec((1, hidden, width), lambda g: (0, 0, g))],
        out_specs=[pl.BlockSpec((rows, width), lambda g: (0, 0))] * 4,
        compiler_params=pltpu.CompilerParams(vmem_limit_bytes=18 * MIB),
    )(*xs, down)


def merge_kernel(*refs):
    terms, outs = refs[:6], refs[6:]
    rows, cols = outs[0].shape
    for k in range(2):
        for j in range(4):
            span = slice(j * rows, (j + 1) * rows)
            a, b, c = (terms[3 * k + n][span, :].astype(jnp.float32) for n in range(3))
            outs[j][:, k * (cols // 2) : (k + 1) * (cols // 2)] = (a + b + c).astype(
                outs[j].dtype
            )


def merge_terms(lo, hi):
    rows, width = lo[0].shape
    vmem = pl.BlockSpec(memory_space=pltpu.VMEM)
    return pl.pallas_call(
        merge_kernel,
        out_shape=[jax.ShapeDtypeStruct((rows // 4, 2 * width), jnp.bfloat16)] * 4,
        in_specs=[vmem] * 6,
        out_specs=[vmem] * 4,
        compiler_params=pltpu.CompilerParams(vmem_limit_bytes=12 * MIB),
    )(*lo, *hi)


def shards(
    queries,
    keys,
    values,
    residual,
    norm_gain,
    out_weight,
    gate_weight,
    up_weight,
    down_weight,
    expert_ids,
    route_weights,
):
    n_tp = lax.axis_size("tp")
    n_ep = lax.axis_size("ep")
    n_etp = lax.axis_size("etp")
    tp, ep, etp = (lax.axis_index(name) for name in ("tp", "ep", "etp"))
    rows = queries.shape[0]
    chip, core = ep // 2, ep % 2
    half_q = queries.shape[1] // 2

    def halves(x):
        w = x.shape[1] // 2
        return jnp.where(core == 0, x[:, :w], x[:, w:]), jnp.where(core == 0, x[:, w:], x[:, :w])

    (own_k, other_k), (own_v, other_v), (own_q, other_q) = (
        halves(x) for x in (keys, values, queries)
    )
    swapped = swap_core(jnp.concatenate([other_k, other_v, other_q], axis=1))
    key_pair = jnp.concatenate([own_k, swapped[:, :HD]], axis=0)
    value_pair = jnp.concatenate([own_v, swapped[:, HD : 2 * HD]], axis=0).T
    other_q = swapped[:, 2 * HD :]
    tokens_dev = residual.shape[2]
    top = expert_ids.shape[-1]
    ids = expert_ids.reshape(tokens_dev, top)
    weights = route_weights.reshape(tokens_dev, top)
    routes = swap_core(jnp.concatenate([ids.astype(jnp.float32), weights], axis=1))
    key_pair, routes = lax.optimization_barrier((key_pair, routes))
    other_ids, other_weights = routes[:, :top].astype(jnp.int32), routes[:, top:]
    key_line = jnp.concatenate(gather_direct(key_pair, "etp"), axis=0)
    value_line = jnp.concatenate(gather_direct(value_pair, "ep", 2), axis=0)
    all_keys = gather_direct(key_line, "ep", 2)
    all_values = gather_direct(value_line, "etp")
    order = jnp.array(OFFSETS, jnp.int32)
    chips = (chip + order) % (n_ep // 2)
    depths = (etp + order) % n_etp
    cores = jnp.stack([core, 1 - core])
    places = (
        (2 * chips[:, None, None] + cores[None, None, :]) * n_etp + depths[None, :, None]
    ).reshape(-1)

    me = ep * n_etp + etp
    far_block = (ep + 1 - 2 * core) * n_etp + etp
    places = jnp.concatenate([places, jnp.stack([me, far_block])]).astype(jnp.int32)
    kept, lent = attend(places, (own_q, other_q), all_keys, all_values)

    def to_other_core(by):
        pairs = [
            (e * n_etp + z, (e ^ 1) * n_etp + (z + by) % n_etp)
            for e in range(n_ep)
            for z in range(n_etp)
        ]
        return lax.ppermute(lent, ("ep", "etp"), pairs)

    back_all = [to_other_core(by) for by in (0, 1, -1, 2)]
    back = back_all[0]
    attention = jnp.concatenate(
        [jnp.where(core == 0, kept, back), jnp.where(core == 0, back, kept)], axis=1
    )
    near_weight = lax.dynamic_slice_in_dim(out_weight, core * half_q, half_q, 0)
    far_weight = lax.dynamic_slice_in_dim(out_weight, (1 - core) * half_q, half_q, 0)
    kept_all = gather_direct(kept, "etp")
    moe_rows = rows // n_tp
    cols = out_weight.shape[1]
    partial_proj = jnp.stack(
        [
            (
                jnp.dot(b, far_weight, preferred_element_type=jnp.float32)
                + jnp.dot(k, near_weight, preferred_element_type=jnp.float32)
            )
            .astype(jnp.bfloat16)
            .reshape(n_tp, moe_rows, cols)
            for b, k in zip(back_all, kept_all)
        ],
        axis=1,
    )

    def for_tp(by):
        at = (tp + by) % n_tp
        return lax.dynamic_slice_in_dim(partial_proj, at, 1, 0).reshape(n_etp * moe_rows, cols)

    summed = for_tp(0).astype(jnp.float32)
    for by in (1, -1, 2):
        summed = summed + shift(for_tp(by), "tp", by).astype(jnp.float32)
    summed = summed.astype(jnp.bfloat16).reshape(n_etp, moe_rows, cols)
    column_blocks = [summed[0]] + [
        shift(summed[j], "etp", OFFSETS[j]) for j in range(1, n_etp)
    ]
    sources = [(etp - OFFSETS[j]) % n_etp for j in range(n_etp)]
    projected = jnp.concatenate(
        [
            sum(
                jnp.where(sources[j] == q, column_blocks[j].astype(jnp.float32), 0.0)
                for j in range(n_etp)
            )
            for q in range(n_etp)
        ],
        axis=1,
    )
    model = n_etp * cols
    state = residual.reshape(moe_rows, model).astype(jnp.float32) + projected
    scale_rows = lax.rsqrt(jnp.mean(state * state, axis=-1, keepdims=True) + 1e-05)
    normed = (state * scale_rows * norm_gain).astype(jnp.bfloat16)
    experts = n_ep * gate_weight.shape[0]
    cap = max(2, min(moe_rows, 5 * moe_rows * top // (4 * experts)))
    place = jnp.concatenate(
        [pair_places(ids, 0, cap, experts), pair_places(other_ids, 1, cap, experts)], axis=0
    )
    match = place[:, :, None] == jnp.arange(experts * cap, dtype=jnp.int32)[None, None, :]
    dispatch = jnp.sum(match.astype(jnp.float32), axis=1).astype(jnp.bfloat16)
    pair_weights = jnp.concatenate([weights, other_weights], axis=0)
    combine = jnp.sum(jnp.where(match, pair_weights[:, :, None], 0.0), axis=1)
    hi, lo = split_bf16(combine)

    width = model // 4
    steps = n_ep // 2
    rows_step = 2 * cap
    pair = jnp.concatenate([normed, swap_core(normed)], axis=0)
    send = lax.dot_general(
        dispatch, pair, (((0,), (0,)), ((), ())), preferred_element_type=jnp.float32
    ).astype(jnp.bfloat16)
    pieces = [send[d * rows_step : (d + 1) * rows_step] for d in range(steps)]
    pieces = [pieces[0]] + [shift(pieces[d], "ep", 2 * d) for d in range(1, steps)]
    arrived = jnp.concatenate(pieces, axis=0)
    stacked = stack_blocks(
        gather_direct(arrived[:, : 2 * width], "tp")
        + gather_direct(arrived[:, 2 * width :], "etp")
    )

    far = ring_gather(stacked[:2], "etp") + ring_gather(stacked[2:], "tp")
    early = lax.optimization_barrier([far[q][:3] for q in range(4)])
    rest, early_a, early_b = first_sums(early, gate_weight, up_weight)
    late = lax.optimization_barrier([far[q][3] for q in range(4)])
    inner_a, inner_b, over = last_sums(
        late, rest, early_a, early_b, gate_weight, up_weight, down_weight
    )
    inner_a, inner_b, _ = lax.optimization_barrier((inner_a, inner_b, over))
    direct = down_terms([inner_a[1], inner_a[2], inner_b[1], inner_b[2]], down_weight)
    inner_a, inner_b, _ = lax.optimization_barrier((inner_a, inner_b, direct))
    passed = down_terms([inner_a[2], inner_a[1], inner_b[2], inner_b[1]], down_weight)
    kept_terms = down_terms([inner_a[0], inner_a[0], inner_b[0], inner_b[0]], down_weight)
    returned = []
    for half, (first, second) in enumerate((("tp", "etp"), ("etp", "tp"))):
        q0, q1 = 2 * half, 2 * half + 1
        over_lo, over_hi = shift(over[q0], second, 1), shift(over[q1], second, -1)
        far_sum_lo, far_sum_hi = add(passed[q0], over_lo), add(passed[q1], over_hi)
        next_lo, _ = lax.optimization_barrier((direct[q0], over_hi))
        next_hi, _ = lax.optimization_barrier((direct[q1], over_lo))
        got_lo, got_hi = shift(next_lo, second, -1), shift(next_hi, second, 1)
        last_lo = shift(far_sum_lo, second, 1)
        last_hi = shift(far_sum_hi, second, -1)
        blocks = merge_terms(
            (kept_terms[q0], got_lo, last_lo), (kept_terms[q1], got_hi, last_hi)
        )
        returned.append(
            add(blocks[0], *[shift(blocks[j], first, OFFSETS[j]) for j in range(1, 4)])
        )
    outs = jnp.concatenate(returned, axis=1)
    pieces = [outs[d * rows_step : (d + 1) * rows_step] for d in range(steps)]
    pieces = [pieces[0]] + [shift(pieces[d], "ep", -2 * d) for d in range(1, steps)]
    expert_rows = jnp.concatenate(pieces, axis=0)
    both = jnp.dot(hi, expert_rows, preferred_element_type=jnp.float32) + jnp.dot(
        lo, expert_rows, preferred_element_type=jnp.float32
    )
    theirs = swap_core(both[moe_rows:].astype(jnp.bfloat16))
    mixed = (state + both[:moe_rows] + theirs.astype(jnp.float32)).astype(jnp.bfloat16)
    return (attention, mixed.reshape(1, 1, moe_rows, model))


def solution(mesh):
    return jax.shard_map(
        shards,
        mesh=mesh,
        in_specs=(
            P(("ep", "etp"), "tp"),
            P(("ep", "etp"), "tp"),
            P(("ep", "etp"), "tp"),
            P(("ep", "etp"), "tp", None, None),
            P(),
            P("tp", "etp"),
            P("ep", None, ("tp", "etp")),
            P("ep", None, ("tp", "etp")),
            P("ep", ("tp", "etp"), None),
            P(("ep", "etp"), "tp", None, None),
            P(("ep", "etp"), "tp", None, None),
        ),
        out_specs=(P(("ep", "etp"), "tp"), P(("ep", "etp"), "tp", None, None)),
        check_vma=False,
    )
```

```python
import functools
import math

import jax
import jax.numpy as jnp
from jax import lax
from jax.experimental import pallas as pl
from jax.experimental.pallas import tpu as pltpu
from jax.sharding import PartitionSpec as P

HD = 128


def route_slots(ids, experts):
    tokens, top = ids.shape
    flat = ids.reshape(-1)
    hot = (flat[:, None] == jnp.arange(experts, dtype=jnp.int32)[None, :]).astype(jnp.int32)
    rank = jnp.cumsum(hot, axis=0) - hot
    return jnp.sum(rank * hot, axis=1).reshape(tokens, top)


def split_bf16(x):
    hi = x.astype(jnp.bfloat16)
    lo = (x - hi.astype(jnp.float32)).astype(jnp.bfloat16)
    return hi, lo


def shift(x, axis, by):
    n = lax.axis_size(axis)
    return lax.ppermute(x, axis, [(i, (i + by) % n) for i in range(n)])


def swap_core(x):
    n = lax.axis_size("ep")
    return lax.ppermute(x, "ep", [(i, i ^ 1) for i in range(n)])


def pair_places(ids, side, cap, experts):
    me = lax.axis_index("ep")
    chip = (ids // 2 - me // 2) % (experts // 2)
    place = chip * (2 * cap) + side * cap + route_slots(ids, experts)
    return jnp.where(ids % 2 == me % 2, place, -1)


def ring_gather(halves, axis):
    lo, hi = halves
    left_lo, right_hi = shift(lo, axis, 1), shift(hi, axis, -1)
    left_hi, right_lo = shift(hi, axis, 1), shift(lo, axis, -1)
    return (
        (lo, left_lo, right_lo, shift(left_lo, axis, 1)),
        (hi, left_hi, right_hi, shift(right_hi, axis, -1)),
    )


def add(*terms):
    return sum(t.astype(jnp.float32) for t in terms).astype(jnp.bfloat16)


def ring_sum(own, left, right, far, axis):
    half = own.shape[1] // 2
    over_lo = shift(far[:, :half], axis, 1)
    over_hi = shift(far[:, half:], axis, -1)
    to_right = jnp.concatenate([add(right[:, :half], over_lo), right[:, half:]], axis=1)
    to_left = jnp.concatenate([left[:, :half], add(left[:, half:], over_hi)], axis=1)
    terms = (own, shift(to_right, axis, 1), shift(to_left, axis, -1))
    return sum(t.astype(jnp.float32) for t in terms)


def ring_blocks(x, axis):
    half = x.shape[1] // 2
    left, right = shift(x, axis, 1), shift(x, axis, -1)
    return x, left, right, shift(left[:, :half], axis, 1), shift(right[:, half:], axis, -1)


def gather_direct(x, axis, step=1):
    return (
        x,
        shift(x, axis, step),
        shift(x, axis, -step),
        shift(x, axis, 2 * step),
    )


OFFSETS = (0, -1, 1, 2)


MIB = 2**20


def attend_kernel(scale, places_ref, q_ref, *refs):
    keys, vals = refs[:4], refs[4:8]
    outs, (diff_ref, top_ref, sum_ref, acc_ref) = refs[8:10], refs[10:]
    depth, width = q_ref.shape
    rows = outs[0].shape[0]
    half = width // 2
    mine, other = places_ref[32], places_ref[33]
    low, high = jnp.minimum(mine, other), jnp.maximum(mine, other)
    top_ref[...] = jnp.full_like(top_ref, -1e20)
    sum_ref[...] = jnp.zeros_like(sum_ref)
    acc_ref[...] = jnp.zeros_like(acc_ref)
    for n, block in enumerate((mine, other)):
        col = lax.broadcasted_iota(jnp.int32, (rows, half), 1) % rows
        row = lax.broadcasted_iota(jnp.int32, (rows, half), 0)
        diff_ref[:, n * half : (n + 1) * half] = row - col - block * rows

    def line(i, masked):
        at = [places_ref[i * 8 + n] for n in range(8)]
        q = q_ref[...]
        scores = []
        for j in range(4):
            k = keys[i][j * 2 * rows : (j + 1) * 2 * rows, :]
            s = jnp.dot(k, q, preferred_element_type=jnp.float32) * scale
            if masked:
                s = jnp.concatenate(
                    [
                        jnp.where(
                            diff_ref[...] <= -at[2 * j + n] * rows,
                            s[n * rows : (n + 1) * rows],
                            -1e30,
                        )
                        for n in range(2)
                    ],
                    axis=0,
                )
            scores.append(s)
        old = top_ref[...]
        new = old
        for s in scores:
            new = jnp.maximum(new, jnp.max(s, axis=0, keepdims=True))
        carry = jnp.exp2(old - new)
        total, acc = sum_ref[...] * carry, acc_ref[...] * carry
        for j, s in enumerate(scores):
            p = jnp.exp2(s - new)
            total += jnp.sum(p, axis=0, keepdims=True)
            acc += jnp.dot(
                vals[j][i * depth : (i + 1) * depth, :],
                p.astype(jnp.bfloat16),
                preferred_element_type=jnp.float32,
            )
        top_ref[...], sum_ref[...], acc_ref[...] = new, total, acc

    for i in range(4):
        least = most = places_ref[i * 8]
        for n in range(1, 8):
            least = jnp.minimum(least, places_ref[i * 8 + n])
            most = jnp.maximum(most, places_ref[i * 8 + n])
        pl.when(most < low)(functools.partial(line, i, False))
        pl.when(jnp.logical_and(most >= low, least <= high))(functools.partial(line, i, True))

    done = acc_ref[...] / sum_ref[...]
    for n in range(2):
        for h in range(half // rows):
            at = n * half + h * rows
            outs[n][:, h * depth : (h + 1) * depth] = done[:, at : at + rows].T.astype(
                outs[n].dtype
            )


def attend(places, queries, keys, vals):
    depth = keys[0].shape[1]
    rows, width = queries[0].shape
    heads = width // depth
    turned = jnp.concatenate(
        [
            jnp.transpose(q.reshape(rows, heads, depth), (2, 1, 0)).reshape(depth, heads * rows)
            for q in queries
        ],
        axis=1,
    )
    vmem = pl.BlockSpec(memory_space=pltpu.VMEM)
    columns = 2 * heads * rows
    return pl.pallas_call(
        functools.partial(attend_kernel, math.log2(math.e) / math.sqrt(depth)),
        out_shape=[jax.ShapeDtypeStruct(q.shape, q.dtype) for q in queries],
        in_specs=[pl.BlockSpec(memory_space=pltpu.SMEM)] + [vmem] * 9,
        out_specs=[vmem] * 2,
        scratch_shapes=[
            pltpu.VMEM((rows, columns), jnp.int32),
            pltpu.VMEM((1, columns), jnp.float32),
            pltpu.VMEM((1, columns), jnp.float32),
            pltpu.VMEM((depth, columns), jnp.float32),
        ],
        compiler_params=pltpu.CompilerParams(vmem_limit_bytes=40 * MIB),
        cost_estimate=pl.CostEstimate(
            flops=4 * columns * 32 * rows * depth,
            bytes_accessed=4 * 32 * rows * depth,
            transcendentals=columns * 32 * rows,
        ),
    )(places, turned, *keys, *vals)


def stack_kernel(*refs):
    ins, outs = refs[:10], refs[10:]
    rows, cols = ins[0].shape
    for half in range(2):
        blocks = ins[5 * half : 5 * half + 5]
        for k in range(2):
            out = outs[2 * half + k]
            for j in range(3):
                out[j * rows : (j + 1) * rows, :] = blocks[j][
                    :, k * (cols // 2) : (k + 1) * (cols // 2)
                ]
            out[3 * rows :, :] = blocks[3 + k][...]


def stack_blocks(blocks):
    rows, cols = blocks[0].shape
    vmem = pl.BlockSpec(memory_space=pltpu.VMEM)
    return pl.pallas_call(
        stack_kernel,
        out_shape=[jax.ShapeDtypeStruct((4 * rows, cols // 2), blocks[0].dtype)] * 4,
        in_specs=[vmem] * 10,
        out_specs=[vmem] * 4,
        compiler_params=pltpu.CompilerParams(vmem_limit_bytes=12 * MIB),
    )(*blocks)


def swish_product(gate_v, up_v):
    return (gate_v / (1.0 + jnp.exp(-gate_v)) * up_v).astype(jnp.bfloat16)


def first_sums_kernel(*refs):
    blocks, (gate_ref, up_ref, rest_ref, in_a_ref, in_b_ref, total_ref) = refs[:12], refs[12:]
    step = pl.program_id(0)
    rows, hidden = blocks[0].shape[0], gate_ref.shape[-1]
    quarter = rows // 4

    @pl.when(step == 0)
    def _():
        total_ref[...] = jnp.zeros_like(total_ref)

    for part in range(4):

        @pl.when(step // 2 == part)
        def _(part=part):
            for j in range(3):
                x = blocks[3 * part + j][...]
                for n, weight in enumerate((gate_ref, up_ref)):
                    span = slice(n * hidden, (n + 1) * hidden)
                    y = jnp.dot(x, weight[0], preferred_element_type=jnp.float32)
                    if part < 2:
                        total_ref[j * rows : (j + 1) * rows, span] += y
                    else:
                        for i in range(4):
                            at = (i * 4 + j) * quarter
                            total_ref[at : at + quarter, span] += y[i * quarter : (i + 1) * quarter]

    @pl.when(step == 7)
    def _():
        in_a_ref[...] = jnp.zeros_like(in_a_ref)
        in_b_ref[...] = jnp.zeros_like(in_b_ref)
        rest_ref[:rows, :] = total_ref[3 * rows :, :]
        for i in range(3):
            at = (4 * i + 3) * quarter
            rest_ref[rows + i * quarter : rows + (i + 1) * quarter, :] = total_ref[
                at : at + quarter, :
            ]
            for j in range(3):
                at, to = (4 * i + j) * quarter, (4 * j + i) * quarter
                inner = swish_product(
                    total_ref[at : at + quarter, :hidden], total_ref[at : at + quarter, hidden:]
                )
                in_a_ref[at : at + quarter, :] = inner
                in_b_ref[to : to + quarter, :] = inner


def part_spec(part, rows, sub):
    return pl.BlockSpec((rows, sub), lambda g: (0, jnp.clip(g - 2 * part, 0, 1)))


def first_sums(blocks, gate, up):
    rows, width = blocks[0][0].shape
    hidden = gate.shape[2]
    sub = width // 2
    weight = pl.BlockSpec((1, sub, hidden), lambda g: (0, jnp.minimum(g, 7), 0))
    rest = 7 * rows // 4

    def fixed(r, c):
        return pl.BlockSpec((r, c), lambda g: (0, 0))

    return pl.pallas_call(
        first_sums_kernel,
        grid=(8,),
        out_shape=[
            jax.ShapeDtypeStruct((rest, 2 * hidden), jnp.float32),
            jax.ShapeDtypeStruct((3 * rows, hidden), jnp.bfloat16),
            jax.ShapeDtypeStruct((3 * rows, hidden), jnp.bfloat16),
        ],
        in_specs=[part_spec(part, rows, sub) for part in range(4) for _ in range(3)]
        + [weight, weight],
        out_specs=[fixed(rest, 2 * hidden), fixed(3 * rows, hidden), fixed(3 * rows, hidden)],
        scratch_shapes=[pltpu.VMEM((4 * rows, 2 * hidden), jnp.float32)],
        compiler_params=pltpu.CompilerParams(vmem_limit_bytes=56 * MIB),
    )(*[x for part in blocks for x in part], gate, up)


def last_sums_kernel(*refs):
    blocks, refs = refs[:4], refs[4:]
    rest_ref, early_a_ref, early_b_ref, gate_ref, up_ref, down_ref = refs[:6]
    (in_a_ref, in_b_ref), outs = refs[6:8], refs[8:12]
    total_ref, far_a_ref, far_b_ref = refs[12:]
    step = pl.program_id(0)
    rows, hidden = blocks[0].shape[0], gate_ref.shape[-1]
    quarter = rows // 4

    @pl.when(step == 0)
    def _():
        total_ref[...] = rest_ref[...]
        in_a_ref[...] = early_a_ref[...]
        in_b_ref[...] = early_b_ref[...]

    for part in range(4):

        @pl.when(step // 2 == part)
        def _(part=part):
            x = blocks[part][...]
            for n, weight in enumerate((gate_ref, up_ref)):
                span = slice(n * hidden, (n + 1) * hidden)
                y = jnp.dot(x, weight[0], preferred_element_type=jnp.float32)
                if part < 2:
                    total_ref[:rows, span] += y
                else:
                    total_ref[rows:, span] += y[: 3 * quarter]
                    total_ref[3 * quarter : rows, span] += y[3 * quarter :]

    @pl.when(step == 7)
    def _():
        for i in range(7):
            at = i * quarter
            inner = swish_product(
                total_ref[at : at + quarter, :hidden], total_ref[at : at + quarter, hidden:]
            )
            if i < 4:
                far_a_ref[at : at + quarter, :] = inner
                if i < 3:
                    to = (4 * i + 3) * quarter
                    in_b_ref[to : to + quarter, :] = inner
                else:
                    far_b_ref[3 * quarter :, :] = inner
            else:
                to = (i - 4) * quarter
                far_b_ref[to : to + quarter, :] = inner
                to = (4 * (i - 4) + 3) * quarter
                in_a_ref[to : to + quarter, :] = inner

    for part in range(4):

        @pl.when(step == 8 + part)
        def _(part=part):
            x = (far_a_ref if part < 2 else far_b_ref)[...]
            outs[part][...] = jnp.dot(
                x, down_ref[0], preferred_element_type=jnp.float32
            ).astype(outs[part].dtype)


def last_sums(blocks, rest, early_a, early_b, gate, up, down):
    rows, width = blocks[0].shape
    hidden = gate.shape[2]
    sub = width // 2
    weight = pl.BlockSpec((1, sub, hidden), lambda g: (0, jnp.minimum(g, 7), 0))
    near = pl.BlockSpec((3 * rows, hidden), lambda g: (0, 0))
    term = pl.BlockSpec((rows, width), lambda g: (0, 0))
    outs = pl.pallas_call(
        last_sums_kernel,
        grid=(12,),
        out_shape=[jax.ShapeDtypeStruct((3 * rows, hidden), jnp.bfloat16)] * 2
        + [jax.ShapeDtypeStruct((rows, width), jnp.bfloat16)] * 4,
        in_specs=[part_spec(part, rows, sub) for part in range(4)]
        + [
            pl.BlockSpec(rest.shape, lambda g: (0, 0)),
            near,
            near,
            weight,
            weight,
            pl.BlockSpec((1, hidden, width), lambda g: (0, 0, jnp.clip(g - 8, 0, 3))),
        ],
        out_specs=[near, near] + [term] * 4,
        scratch_shapes=[
            pltpu.VMEM(rest.shape, jnp.float32),
            pltpu.VMEM((rows, hidden), jnp.bfloat16),
            pltpu.VMEM((rows, hidden), jnp.bfloat16),
        ],
        compiler_params=pltpu.CompilerParams(vmem_limit_bytes=58 * MIB),
    )(*blocks, rest, early_a, early_b, gate, up, down)
    return outs[0].reshape(3, rows, hidden), outs[1].reshape(3, rows, hidden), outs[2:]


def down_kernel(*refs):
    xs, down_ref, outs = refs[:4], refs[4], refs[5:]
    for part in range(4):

        @pl.when(pl.program_id(0) == part)
        def _(part=part):
            outs[part][...] = jnp.dot(
                xs[part][...], down_ref[0], preferred_element_type=jnp.float32
            ).astype(outs[part].dtype)


def down_terms(xs, down):
    rows, hidden = xs[0].shape
    width = down.shape[2] // 4
    return pl.pallas_call(
        down_kernel,
        grid=(4,),
        out_shape=[jax.ShapeDtypeStruct((rows, width), jnp.bfloat16)] * 4,
        in_specs=[pl.BlockSpec((rows, hidden), lambda g: (0, 0))] * 4
        + [pl.BlockSpec((1, hidden, width), lambda g: (0, 0, g))],
        out_specs=[pl.BlockSpec((rows, width), lambda g: (0, 0))] * 4,
        compiler_params=pltpu.CompilerParams(vmem_limit_bytes=18 * MIB),
    )(*xs, down)


def merge_kernel(*refs):
    terms, outs = refs[:6], refs[6:]
    rows, cols = outs[0].shape
    for k in range(2):
        for j in range(4):
            span = slice(j * rows, (j + 1) * rows)
            a, b, c = (terms[3 * k + n][span, :].astype(jnp.float32) for n in range(3))
            outs[j][:, k * (cols // 2) : (k + 1) * (cols // 2)] = (a + b + c).astype(
                outs[j].dtype
            )


def merge_terms(lo, hi):
    rows, width = lo[0].shape
    vmem = pl.BlockSpec(memory_space=pltpu.VMEM)
    return pl.pallas_call(
        merge_kernel,
        out_shape=[jax.ShapeDtypeStruct((rows // 4, 2 * width), jnp.bfloat16)] * 4,
        in_specs=[vmem] * 6,
        out_specs=[vmem] * 4,
        compiler_params=pltpu.CompilerParams(vmem_limit_bytes=12 * MIB),
    )(*lo, *hi)


def shards(
    queries,
    keys,
    values,
    residual,
    norm_gain,
    out_weight,
    gate_weight,
    up_weight,
    down_weight,
    expert_ids,
    route_weights,
):
    n_tp = lax.axis_size("tp")
    n_ep = lax.axis_size("ep")
    n_etp = lax.axis_size("etp")
    tp, ep, etp = (lax.axis_index(name) for name in ("tp", "ep", "etp"))
    rows = queries.shape[0]
    chip, core = ep // 2, ep % 2
    half_q = queries.shape[1] // 2

    def halves(x):
        w = x.shape[1] // 2
        return jnp.where(core == 0, x[:, :w], x[:, w:]), jnp.where(core == 0, x[:, w:], x[:, :w])

    (own_k, other_k), (own_v, other_v), (own_q, other_q) = (
        halves(x) for x in (keys, values, queries)
    )
    swapped = swap_core(jnp.concatenate([other_k, other_v, other_q], axis=1))
    key_pair = jnp.concatenate([own_k, swapped[:, :HD]], axis=0)
    value_pair = jnp.concatenate([own_v, swapped[:, HD : 2 * HD]], axis=0).T
    other_q = swapped[:, 2 * HD :]
    tokens_dev = residual.shape[2]
    top = expert_ids.shape[-1]
    ids = expert_ids.reshape(tokens_dev, top)
    weights = route_weights.reshape(tokens_dev, top)
    routes = swap_core(jnp.concatenate([ids.astype(jnp.float32), weights], axis=1))
    key_pair, routes = lax.optimization_barrier((key_pair, routes))
    other_ids, other_weights = routes[:, :top].astype(jnp.int32), routes[:, top:]
    key_line = jnp.concatenate(gather_direct(key_pair, "etp"), axis=0)
    value_line = jnp.concatenate(gather_direct(value_pair, "ep", 2), axis=0)
    all_keys = gather_direct(key_line, "ep", 2)
    all_values = gather_direct(value_line, "etp")
    order = jnp.array(OFFSETS, jnp.int32)
    chips = (chip + order) % (n_ep // 2)
    depths = (etp + order) % n_etp
    cores = jnp.stack([core, 1 - core])
    places = (
        (2 * chips[:, None, None] + cores[None, None, :]) * n_etp + depths[None, :, None]
    ).reshape(-1)

    me = ep * n_etp + etp
    far_block = (ep + 1 - 2 * core) * n_etp + etp
    places = jnp.concatenate([places, jnp.stack([me, far_block])]).astype(jnp.int32)
    kept, lent = attend(places, (own_q, other_q), all_keys, all_values)

    def to_other_core(by):
        pairs = [
            (e * n_etp + z, (e ^ 1) * n_etp + (z + by) % n_etp)
            for e in range(n_ep)
            for z in range(n_etp)
        ]
        return lax.ppermute(lent, ("ep", "etp"), pairs)

    back, back_left, back_right = (to_other_core(by) for by in (0, 1, -1))
    back_all = (back, back_left, back_right, shift(back_right, "etp", -1))
    attention = jnp.concatenate(
        [jnp.where(core == 0, kept, back), jnp.where(core == 0, back, kept)], axis=1
    )
    near_weight = lax.dynamic_slice_in_dim(out_weight, core * half_q, half_q, 0)
    far_weight = lax.dynamic_slice_in_dim(out_weight, (1 - core) * half_q, half_q, 0)
    kept_left, kept_right = shift(kept, "etp", 1), shift(kept, "etp", -1)
    kept_all = (kept, kept_left, kept_right, shift(kept_left, "etp", 1))
    moe_rows = rows // n_tp
    cols = out_weight.shape[1]
    partial_proj = jnp.stack(
        [
            (
                jnp.dot(b, far_weight, preferred_element_type=jnp.float32)
                + jnp.dot(k, near_weight, preferred_element_type=jnp.float32)
            )
            .astype(jnp.bfloat16)
            .reshape(n_tp, moe_rows, cols)
            for b, k in zip(back_all, kept_all)
        ],
        axis=1,
    )

    def for_tp(by):
        at = (tp + by) % n_tp
        return lax.dynamic_slice_in_dim(partial_proj, at, 1, 0).reshape(n_etp * moe_rows, cols)

    summed = ring_sum(for_tp(0), for_tp(-1), for_tp(1), for_tp(2), "tp")
    summed = summed.astype(jnp.bfloat16).reshape(n_etp, moe_rows, cols)
    column_blocks = [summed[0]] + [
        shift(summed[j], "etp", OFFSETS[j]) for j in range(1, n_etp)
    ]
    sources = [(etp - OFFSETS[j]) % n_etp for j in range(n_etp)]
    projected = jnp.concatenate(
        [
            sum(
                jnp.where(sources[j] == q, column_blocks[j].astype(jnp.float32), 0.0)
                for j in range(n_etp)
            )
            for q in range(n_etp)
        ],
        axis=1,
    )
    model = n_etp * cols
    state = residual.reshape(moe_rows, model).astype(jnp.float32) + projected
    scale_rows = lax.rsqrt(jnp.mean(state * state, axis=-1, keepdims=True) + 1e-05)
    normed = (state * scale_rows * norm_gain).astype(jnp.bfloat16)
    experts = n_ep * gate_weight.shape[0]
    cap = max(2, min(moe_rows, 5 * moe_rows * top // (4 * experts)))
    place = jnp.concatenate(
        [pair_places(ids, 0, cap, experts), pair_places(other_ids, 1, cap, experts)], axis=0
    )
    match = place[:, :, None] == jnp.arange(experts * cap, dtype=jnp.int32)[None, None, :]
    dispatch = jnp.sum(match.astype(jnp.float32), axis=1).astype(jnp.bfloat16)
    pair_weights = jnp.concatenate([weights, other_weights], axis=0)
    combine = jnp.sum(jnp.where(match, pair_weights[:, :, None], 0.0), axis=1)
    hi, lo = split_bf16(combine)

    width = model // 4
    steps = n_ep // 2
    rows_step = 2 * cap
    pair = jnp.concatenate([normed, swap_core(normed)], axis=0)
    send = lax.dot_general(
        dispatch, pair, (((0,), (0,)), ((), ())), preferred_element_type=jnp.float32
    ).astype(jnp.bfloat16)
    pieces = [send[d * rows_step : (d + 1) * rows_step] for d in range(steps)]
    pieces = [pieces[0]] + [shift(pieces[d], "ep", 2 * d) for d in range(1, steps)]
    arrived = jnp.concatenate(pieces, axis=0)
    stacked = stack_blocks(
        ring_blocks(arrived[:, : 2 * width], "tp") + ring_blocks(arrived[:, 2 * width :], "etp")
    )

    far = ring_gather(stacked[:2], "etp") + ring_gather(stacked[2:], "tp")
    early = lax.optimization_barrier([far[q][:3] for q in range(4)])
    rest, early_a, early_b = first_sums(early, gate_weight, up_weight)
    late = lax.optimization_barrier([far[q][3] for q in range(4)])
    inner_a, inner_b, over = last_sums(
        late, rest, early_a, early_b, gate_weight, up_weight, down_weight
    )
    inner_a, inner_b, _ = lax.optimization_barrier((inner_a, inner_b, over))
    direct = down_terms([inner_a[1], inner_a[2], inner_b[1], inner_b[2]], down_weight)
    inner_a, inner_b, _ = lax.optimization_barrier((inner_a, inner_b, direct))
    passed = down_terms([inner_a[2], inner_a[1], inner_b[2], inner_b[1]], down_weight)
    kept_terms = down_terms([inner_a[0], inner_a[0], inner_b[0], inner_b[0]], down_weight)
    returned = []
    for half, (first, second) in enumerate((("tp", "etp"), ("etp", "tp"))):
        q0, q1 = 2 * half, 2 * half + 1
        over_lo, over_hi = shift(over[q0], second, 1), shift(over[q1], second, -1)
        far_sum_lo, far_sum_hi = add(passed[q0], over_lo), add(passed[q1], over_hi)
        next_lo, _ = lax.optimization_barrier((direct[q0], over_hi))
        next_hi, _ = lax.optimization_barrier((direct[q1], over_lo))
        got_lo, got_hi = shift(next_lo, second, -1), shift(next_hi, second, 1)
        last_lo = shift(far_sum_lo, second, 1)
        last_hi = shift(far_sum_hi, second, -1)
        blocks = merge_terms(
            (kept_terms[q0], got_lo, last_lo), (kept_terms[q1], got_hi, last_hi)
        )
        returned.append(ring_sum(*blocks, first).astype(jnp.bfloat16))
    outs = jnp.concatenate(returned, axis=1)
    pieces = [outs[d * rows_step : (d + 1) * rows_step] for d in range(steps)]
    pieces = [pieces[0]] + [shift(pieces[d], "ep", -2 * d) for d in range(1, steps)]
    expert_rows = jnp.concatenate(pieces, axis=0)
    both = jnp.dot(hi, expert_rows, preferred_element_type=jnp.float32) + jnp.dot(
        lo, expert_rows, preferred_element_type=jnp.float32
    )
    theirs = swap_core(both[moe_rows:].astype(jnp.bfloat16))
    mixed = (state + both[:moe_rows] + theirs.astype(jnp.float32)).astype(jnp.bfloat16)
    return (attention, mixed.reshape(1, 1, moe_rows, model))


def solution(mesh):
    return jax.shard_map(
        shards,
        mesh=mesh,
        in_specs=(
            P(("ep", "etp"), "tp"),
            P(("ep", "etp"), "tp"),
            P(("ep", "etp"), "tp"),
            P(("ep", "etp"), "tp", None, None),
            P(),
            P("tp", "etp"),
            P("ep", None, ("tp", "etp")),
            P("ep", None, ("tp", "etp")),
            P("ep", ("tp", "etp"), None),
            P(("ep", "etp"), "tp", None, None),
            P(("ep", "etp"), "tp", None, None),
        ),
        out_specs=(P(("ep", "etp"), "tp"), P(("ep", "etp"), "tp", None, None)),
        check_vma=False,
    )
```

```python
import functools
import math

import jax
import jax.numpy as jnp
from jax import lax
from jax.experimental import pallas as pl
from jax.experimental.pallas import tpu as pltpu
from jax.sharding import PartitionSpec as P

HD = 128


def route_slots(ids, experts):
    tokens, top = ids.shape
    flat = ids.reshape(-1)
    hot = (flat[:, None] == jnp.arange(experts, dtype=jnp.int32)[None, :]).astype(jnp.int32)
    rank = jnp.cumsum(hot, axis=0) - hot
    return jnp.sum(rank * hot, axis=1).reshape(tokens, top)


def split_bf16(x):
    hi = x.astype(jnp.bfloat16)
    lo = (x - hi.astype(jnp.float32)).astype(jnp.bfloat16)
    return hi, lo


def shift(x, axis, by):
    n = lax.axis_size(axis)
    return lax.ppermute(x, axis, [(i, (i + by) % n) for i in range(n)])


def swap_core(x):
    n = lax.axis_size("ep")
    return lax.ppermute(x, "ep", [(i, i ^ 1) for i in range(n)])


def pair_places(ids, side, cap, experts):
    me = lax.axis_index("ep")
    chip = (ids // 2 - me // 2) % (experts // 2)
    place = chip * (2 * cap) + side * cap + route_slots(ids, experts)
    return jnp.where(ids % 2 == me % 2, place, -1)


def ring_gather(halves, axis):
    lo, hi = halves
    left_lo, right_hi = shift(lo, axis, 1), shift(hi, axis, -1)
    left_hi, right_lo = shift(hi, axis, 1), shift(lo, axis, -1)
    return (
        (lo, left_lo, right_lo, shift(left_lo, axis, 1)),
        (hi, left_hi, right_hi, shift(right_hi, axis, -1)),
    )


def add(*terms):
    return sum(t.astype(jnp.float32) for t in terms).astype(jnp.bfloat16)


def ring_sum(own, left, right, far, axis):
    half = own.shape[1] // 2
    over_lo = shift(far[:, :half], axis, 1)
    over_hi = shift(far[:, half:], axis, -1)
    to_right = jnp.concatenate([add(right[:, :half], over_lo), right[:, half:]], axis=1)
    to_left = jnp.concatenate([left[:, :half], add(left[:, half:], over_hi)], axis=1)
    terms = (own, shift(to_right, axis, 1), shift(to_left, axis, -1))
    return sum(t.astype(jnp.float32) for t in terms)


def ring_blocks(x, axis):
    half = x.shape[1] // 2
    left, right = shift(x, axis, 1), shift(x, axis, -1)
    return x, left, right, shift(left[:, :half], axis, 1), shift(right[:, half:], axis, -1)


def gather_direct(x, axis, step=1):
    return (
        x,
        shift(x, axis, step),
        shift(x, axis, -step),
        shift(x, axis, 2 * step),
    )


OFFSETS = (0, -1, 1, 2)


MIB = 2**20


def attend_kernel(scale, places_ref, q_ref, *refs):
    keys, vals = refs[:4], refs[4:8]
    outs, (diff_ref, top_ref, sum_ref, acc_ref) = refs[8:10], refs[10:]
    depth, width = q_ref.shape
    rows = outs[0].shape[0]
    half = width // 2
    mine, other = places_ref[32], places_ref[33]
    low, high = jnp.minimum(mine, other), jnp.maximum(mine, other)
    top_ref[...] = jnp.full_like(top_ref, -1e20)
    sum_ref[...] = jnp.zeros_like(sum_ref)
    acc_ref[...] = jnp.zeros_like(acc_ref)
    for n, block in enumerate((mine, other)):
        col = lax.broadcasted_iota(jnp.int32, (rows, half), 1) % rows
        row = lax.broadcasted_iota(jnp.int32, (rows, half), 0)
        diff_ref[:, n * half : (n + 1) * half] = row - col - block * rows

    def line(i, masked):
        at = [places_ref[i * 8 + n] for n in range(8)]
        q = q_ref[...]
        scores = []
        for j in range(4):
            k = keys[i][j * 2 * rows : (j + 1) * 2 * rows, :]
            s = jnp.dot(k, q, preferred_element_type=jnp.float32) * scale
            if masked:
                s = jnp.concatenate(
                    [
                        jnp.where(
                            diff_ref[...] <= -at[2 * j + n] * rows,
                            s[n * rows : (n + 1) * rows],
                            -1e30,
                        )
                        for n in range(2)
                    ],
                    axis=0,
                )
            scores.append(s)
        old = top_ref[...]
        new = old
        for s in scores:
            new = jnp.maximum(new, jnp.max(s, axis=0, keepdims=True))
        carry = jnp.exp2(old - new)
        total, acc = sum_ref[...] * carry, acc_ref[...] * carry
        for j, s in enumerate(scores):
            p = jnp.exp2(s - new)
            total += jnp.sum(p, axis=0, keepdims=True)
            acc += jnp.dot(
                vals[j][i * depth : (i + 1) * depth, :],
                p.astype(jnp.bfloat16),
                preferred_element_type=jnp.float32,
            )
        top_ref[...], sum_ref[...], acc_ref[...] = new, total, acc

    for i in range(4):
        least = most = places_ref[i * 8]
        for n in range(1, 8):
            least = jnp.minimum(least, places_ref[i * 8 + n])
            most = jnp.maximum(most, places_ref[i * 8 + n])
        pl.when(most < low)(functools.partial(line, i, False))
        pl.when(jnp.logical_and(most >= low, least <= high))(functools.partial(line, i, True))

    done = acc_ref[...] / sum_ref[...]
    for n in range(2):
        for h in range(half // rows):
            at = n * half + h * rows
            outs[n][:, h * depth : (h + 1) * depth] = done[:, at : at + rows].T.astype(
                outs[n].dtype
            )


def attend(places, queries, keys, vals):
    depth = keys[0].shape[1]
    rows, width = queries[0].shape
    heads = width // depth
    turned = jnp.concatenate(
        [
            jnp.transpose(q.reshape(rows, heads, depth), (2, 1, 0)).reshape(depth, heads * rows)
            for q in queries
        ],
        axis=1,
    )
    vmem = pl.BlockSpec(memory_space=pltpu.VMEM)
    columns = 2 * heads * rows
    return pl.pallas_call(
        functools.partial(attend_kernel, math.log2(math.e) / math.sqrt(depth)),
        out_shape=[jax.ShapeDtypeStruct(q.shape, q.dtype) for q in queries],
        in_specs=[pl.BlockSpec(memory_space=pltpu.SMEM)] + [vmem] * 9,
        out_specs=[vmem] * 2,
        scratch_shapes=[
            pltpu.VMEM((rows, columns), jnp.int32),
            pltpu.VMEM((1, columns), jnp.float32),
            pltpu.VMEM((1, columns), jnp.float32),
            pltpu.VMEM((depth, columns), jnp.float32),
        ],
        compiler_params=pltpu.CompilerParams(vmem_limit_bytes=40 * MIB),
        cost_estimate=pl.CostEstimate(
            flops=4 * columns * 32 * rows * depth,
            bytes_accessed=4 * 32 * rows * depth,
            transcendentals=columns * 32 * rows,
        ),
    )(places, turned, *keys, *vals)


def stack_kernel(*refs):
    ins, outs = refs[:10], refs[10:]
    rows, cols = ins[0].shape
    for half in range(2):
        blocks = ins[5 * half : 5 * half + 5]
        for k in range(2):
            out = outs[2 * half + k]
            for j in range(3):
                out[j * rows : (j + 1) * rows, :] = blocks[j][
                    :, k * (cols // 2) : (k + 1) * (cols // 2)
                ]
            out[3 * rows :, :] = blocks[3 + k][...]


def stack_blocks(blocks):
    rows, cols = blocks[0].shape
    vmem = pl.BlockSpec(memory_space=pltpu.VMEM)
    return pl.pallas_call(
        stack_kernel,
        out_shape=[jax.ShapeDtypeStruct((4 * rows, cols // 2), blocks[0].dtype)] * 4,
        in_specs=[vmem] * 10,
        out_specs=[vmem] * 4,
        compiler_params=pltpu.CompilerParams(vmem_limit_bytes=12 * MIB),
    )(*blocks)


def swish_product(gate_v, up_v):
    return (gate_v / (1.0 + jnp.exp(-gate_v)) * up_v).astype(jnp.bfloat16)


def first_sums_kernel(*refs):
    blocks, (gate_ref, up_ref, rest_ref, in_a_ref, in_b_ref, total_ref) = refs[:12], refs[12:]
    step = pl.program_id(0)
    rows, hidden = blocks[0].shape[0], gate_ref.shape[-1]
    quarter = rows // 4

    @pl.when(step == 0)
    def _():
        total_ref[...] = jnp.zeros_like(total_ref)

    for part in range(4):

        @pl.when(step // 2 == part)
        def _(part=part):
            for j in range(3):
                x = blocks[3 * part + j][...]
                for n, weight in enumerate((gate_ref, up_ref)):
                    span = slice(n * hidden, (n + 1) * hidden)
                    y = jnp.dot(x, weight[0], preferred_element_type=jnp.float32)
                    if part < 2:
                        total_ref[j * rows : (j + 1) * rows, span] += y
                    else:
                        for i in range(4):
                            at = (i * 4 + j) * quarter
                            total_ref[at : at + quarter, span] += y[i * quarter : (i + 1) * quarter]

    @pl.when(step == 7)
    def _():
        in_a_ref[...] = jnp.zeros_like(in_a_ref)
        in_b_ref[...] = jnp.zeros_like(in_b_ref)
        rest_ref[:rows, :] = total_ref[3 * rows :, :]
        for i in range(3):
            at = (4 * i + 3) * quarter
            rest_ref[rows + i * quarter : rows + (i + 1) * quarter, :] = total_ref[
                at : at + quarter, :
            ]
            for j in range(3):
                at, to = (4 * i + j) * quarter, (4 * j + i) * quarter
                inner = swish_product(
                    total_ref[at : at + quarter, :hidden], total_ref[at : at + quarter, hidden:]
                )
                in_a_ref[at : at + quarter, :] = inner
                in_b_ref[to : to + quarter, :] = inner


def part_spec(part, rows, sub):
    return pl.BlockSpec((rows, sub), lambda g: (0, jnp.clip(g - 2 * part, 0, 1)))


def first_sums(blocks, gate, up):
    rows, width = blocks[0][0].shape
    hidden = gate.shape[2]
    sub = width // 2
    weight = pl.BlockSpec((1, sub, hidden), lambda g: (0, jnp.minimum(g, 7), 0))
    rest = 7 * rows // 4

    def fixed(r, c):
        return pl.BlockSpec((r, c), lambda g: (0, 0))

    return pl.pallas_call(
        first_sums_kernel,
        grid=(8,),
        out_shape=[
            jax.ShapeDtypeStruct((rest, 2 * hidden), jnp.float32),
            jax.ShapeDtypeStruct((3 * rows, hidden), jnp.bfloat16),
            jax.ShapeDtypeStruct((3 * rows, hidden), jnp.bfloat16),
        ],
        in_specs=[part_spec(part, rows, sub) for part in range(4) for _ in range(3)]
        + [weight, weight],
        out_specs=[fixed(rest, 2 * hidden), fixed(3 * rows, hidden), fixed(3 * rows, hidden)],
        scratch_shapes=[pltpu.VMEM((4 * rows, 2 * hidden), jnp.float32)],
        compiler_params=pltpu.CompilerParams(vmem_limit_bytes=56 * MIB),
    )(*[x for part in blocks for x in part], gate, up)


def last_sums_kernel(*refs):
    blocks, refs = refs[:4], refs[4:]
    rest_ref, gate_ref, up_ref, down_ref, late_ref = refs[:5]
    outs, (total_ref, far_a_ref, far_b_ref) = refs[5:9], refs[9:]
    step = pl.program_id(0)
    rows, hidden = blocks[0].shape[0], gate_ref.shape[-1]
    quarter = rows // 4

    @pl.when(step == 0)
    def _():
        total_ref[...] = rest_ref[...]

    for part in range(4):

        @pl.when(step // 2 == part)
        def _(part=part):
            x = blocks[part][...]
            for n, weight in enumerate((gate_ref, up_ref)):
                span = slice(n * hidden, (n + 1) * hidden)
                y = jnp.dot(x, weight[0], preferred_element_type=jnp.float32)
                if part < 2:
                    total_ref[:rows, span] += y
                else:
                    total_ref[rows:, span] += y[: 3 * quarter]
                    total_ref[3 * quarter : rows, span] += y[3 * quarter :]

    @pl.when(step == 7)
    def _():
        for i in range(7):
            at = i * quarter
            inner = swish_product(
                total_ref[at : at + quarter, :hidden], total_ref[at : at + quarter, hidden:]
            )
            late_ref[at : at + quarter, :] = inner
            if i < 4:
                far_a_ref[at : at + quarter, :] = inner
            if i > 2:
                to = (i - 4) % 4 * quarter
                far_b_ref[to : to + quarter, :] = inner

    for part in range(4):

        @pl.when(step == 8 + part)
        def _(part=part):
            x = (far_a_ref if part < 2 else far_b_ref)[...]
            outs[part][...] = jnp.dot(
                x, down_ref[0], preferred_element_type=jnp.float32
            ).astype(outs[part].dtype)


def last_sums(blocks, rest, gate, up, down):
    rows, width = blocks[0].shape
    hidden = gate.shape[2]
    sub = width // 2
    weight = pl.BlockSpec((1, sub, hidden), lambda g: (0, jnp.minimum(g, 7), 0))
    term = pl.BlockSpec((rows, width), lambda g: (0, 0))
    outs = pl.pallas_call(
        last_sums_kernel,
        grid=(12,),
        out_shape=[jax.ShapeDtypeStruct((rest.shape[0], hidden), jnp.bfloat16)]
        + [jax.ShapeDtypeStruct((rows, width), jnp.bfloat16)] * 4,
        in_specs=[part_spec(part, rows, sub) for part in range(4)]
        + [
            pl.BlockSpec(rest.shape, lambda g: (0, 0)),
            weight,
            weight,
            pl.BlockSpec((1, hidden, width), lambda g: (0, 0, jnp.clip(g - 8, 0, 3))),
        ],
        out_specs=[pl.BlockSpec((rest.shape[0], hidden), lambda g: (0, 0))] + [term] * 4,
        scratch_shapes=[
            pltpu.VMEM(rest.shape, jnp.float32),
            pltpu.VMEM((rows, hidden), jnp.bfloat16),
            pltpu.VMEM((rows, hidden), jnp.bfloat16),
        ],
        compiler_params=pltpu.CompilerParams(vmem_limit_bytes=58 * MIB),
    )(*blocks, rest, gate, up, down)
    return outs[0], outs[1:]


def down_kernel(*refs):
    xs, down_ref, outs = refs[:4], refs[4], refs[5:]
    for part in range(4):

        @pl.when(pl.program_id(0) == part)
        def _(part=part):
            outs[part][...] = jnp.dot(
                xs[part][...], down_ref[0], preferred_element_type=jnp.float32
            ).astype(outs[part].dtype)


def down_terms(xs, down):
    rows, hidden = xs[0].shape
    width = down.shape[2] // 4
    return pl.pallas_call(
        down_kernel,
        grid=(4,),
        out_shape=[jax.ShapeDtypeStruct((rows, width), jnp.bfloat16)] * 4,
        in_specs=[pl.BlockSpec((rows, hidden), lambda g: (0, 0))] * 4
        + [pl.BlockSpec((1, hidden, width), lambda g: (0, 0, g))],
        out_specs=[pl.BlockSpec((rows, width), lambda g: (0, 0))] * 4,
        compiler_params=pltpu.CompilerParams(vmem_limit_bytes=18 * MIB),
    )(*xs, down)


def merge_kernel(*refs):
    terms, outs = refs[:6], refs[6:]
    rows, cols = outs[0].shape
    for k in range(2):
        for j in range(4):
            span = slice(j * rows, (j + 1) * rows)
            a, b, c = (terms[3 * k + n][span, :].astype(jnp.float32) for n in range(3))
            outs[j][:, k * (cols // 2) : (k + 1) * (cols // 2)] = (a + b + c).astype(
                outs[j].dtype
            )


def merge_terms(lo, hi):
    rows, width = lo[0].shape
    vmem = pl.BlockSpec(memory_space=pltpu.VMEM)
    return pl.pallas_call(
        merge_kernel,
        out_shape=[jax.ShapeDtypeStruct((rows // 4, 2 * width), jnp.bfloat16)] * 4,
        in_specs=[vmem] * 6,
        out_specs=[vmem] * 4,
        compiler_params=pltpu.CompilerParams(vmem_limit_bytes=12 * MIB),
    )(*lo, *hi)


def shards(
    queries,
    keys,
    values,
    residual,
    norm_gain,
    out_weight,
    gate_weight,
    up_weight,
    down_weight,
    expert_ids,
    route_weights,
):
    n_tp = lax.axis_size("tp")
    n_ep = lax.axis_size("ep")
    n_etp = lax.axis_size("etp")
    tp, ep, etp = (lax.axis_index(name) for name in ("tp", "ep", "etp"))
    rows = queries.shape[0]
    chip, core = ep // 2, ep % 2
    half_q = queries.shape[1] // 2

    def halves(x):
        w = x.shape[1] // 2
        return jnp.where(core == 0, x[:, :w], x[:, w:]), jnp.where(core == 0, x[:, w:], x[:, :w])

    (own_k, other_k), (own_v, other_v), (own_q, other_q) = (
        halves(x) for x in (keys, values, queries)
    )
    swapped = swap_core(jnp.concatenate([other_k, other_v, other_q], axis=1))
    key_pair = jnp.concatenate([own_k, swapped[:, :HD]], axis=0)
    value_pair = jnp.concatenate([own_v, swapped[:, HD : 2 * HD]], axis=0).T
    other_q = swapped[:, 2 * HD :]
    tokens_dev = residual.shape[2]
    top = expert_ids.shape[-1]
    ids = expert_ids.reshape(tokens_dev, top)
    weights = route_weights.reshape(tokens_dev, top)
    routes = swap_core(jnp.concatenate([ids.astype(jnp.float32), weights], axis=1))
    key_pair, routes = lax.optimization_barrier((key_pair, routes))
    other_ids, other_weights = routes[:, :top].astype(jnp.int32), routes[:, top:]
    key_line = jnp.concatenate(gather_direct(key_pair, "etp"), axis=0)
    value_line = jnp.concatenate(gather_direct(value_pair, "ep", 2), axis=0)
    all_keys = gather_direct(key_line, "ep", 2)
    all_values = gather_direct(value_line, "etp")
    order = jnp.array(OFFSETS, jnp.int32)
    chips = (chip + order) % (n_ep // 2)
    depths = (etp + order) % n_etp
    cores = jnp.stack([core, 1 - core])
    places = (
        (2 * chips[:, None, None] + cores[None, None, :]) * n_etp + depths[None, :, None]
    ).reshape(-1)

    me = ep * n_etp + etp
    far_block = (ep + 1 - 2 * core) * n_etp + etp
    places = jnp.concatenate([places, jnp.stack([me, far_block])]).astype(jnp.int32)
    kept, lent = attend(places, (own_q, other_q), all_keys, all_values)

    def to_other_core(by):
        pairs = [
            (e * n_etp + z, (e ^ 1) * n_etp + (z + by) % n_etp)
            for e in range(n_ep)
            for z in range(n_etp)
        ]
        return lax.ppermute(lent, ("ep", "etp"), pairs)

    back, back_left, back_right = (to_other_core(by) for by in (0, 1, -1))
    back_all = (back, back_left, back_right, shift(back_right, "etp", -1))
    attention = jnp.concatenate(
        [jnp.where(core == 0, kept, back), jnp.where(core == 0, back, kept)], axis=1
    )
    near_weight = lax.dynamic_slice_in_dim(out_weight, core * half_q, half_q, 0)
    far_weight = lax.dynamic_slice_in_dim(out_weight, (1 - core) * half_q, half_q, 0)
    kept_left, kept_right = shift(kept, "etp", 1), shift(kept, "etp", -1)
    kept_all = (kept, kept_left, kept_right, shift(kept_left, "etp", 1))
    moe_rows = rows // n_tp
    cols = out_weight.shape[1]
    partial_proj = jnp.stack(
        [
            (
                jnp.dot(b, far_weight, preferred_element_type=jnp.float32)
                + jnp.dot(k, near_weight, preferred_element_type=jnp.float32)
            )
            .astype(jnp.bfloat16)
            .reshape(n_tp, moe_rows, cols)
            for b, k in zip(back_all, kept_all)
        ],
        axis=1,
    )

    def for_tp(by):
        at = (tp + by) % n_tp
        return lax.dynamic_slice_in_dim(partial_proj, at, 1, 0).reshape(n_etp * moe_rows, cols)

    summed = ring_sum(for_tp(0), for_tp(-1), for_tp(1), for_tp(2), "tp")
    summed = summed.astype(jnp.bfloat16).reshape(n_etp, moe_rows, cols)
    column_blocks = [summed[0]] + [
        shift(summed[j], "etp", OFFSETS[j]) for j in range(1, n_etp)
    ]
    sources = [(etp - OFFSETS[j]) % n_etp for j in range(n_etp)]
    projected = jnp.concatenate(
        [
            sum(
                jnp.where(sources[j] == q, column_blocks[j].astype(jnp.float32), 0.0)
                for j in range(n_etp)
            )
            for q in range(n_etp)
        ],
        axis=1,
    )
    model = n_etp * cols
    state = residual.reshape(moe_rows, model).astype(jnp.float32) + projected
    scale_rows = lax.rsqrt(jnp.mean(state * state, axis=-1, keepdims=True) + 1e-05)
    normed = (state * scale_rows * norm_gain).astype(jnp.bfloat16)
    experts = n_ep * gate_weight.shape[0]
    cap = max(2, min(moe_rows, 5 * moe_rows * top // (4 * experts)))
    place = jnp.concatenate(
        [pair_places(ids, 0, cap, experts), pair_places(other_ids, 1, cap, experts)], axis=0
    )
    match = place[:, :, None] == jnp.arange(experts * cap, dtype=jnp.int32)[None, None, :]
    dispatch = jnp.sum(match.astype(jnp.float32), axis=1).astype(jnp.bfloat16)
    pair_weights = jnp.concatenate([weights, other_weights], axis=0)
    combine = jnp.sum(jnp.where(match, pair_weights[:, :, None], 0.0), axis=1)
    hi, lo = split_bf16(combine)

    width = model // 4
    steps = n_ep // 2
    rows_step = 2 * cap
    pair = jnp.concatenate([normed, swap_core(normed)], axis=0)
    send = lax.dot_general(
        dispatch, pair, (((0,), (0,)), ((), ())), preferred_element_type=jnp.float32
    ).astype(jnp.bfloat16)
    pieces = [send[d * rows_step : (d + 1) * rows_step] for d in range(steps)]
    pieces = [pieces[0]] + [shift(pieces[d], "ep", 2 * d) for d in range(1, steps)]
    arrived = jnp.concatenate(pieces, axis=0)
    stacked = stack_blocks(
        ring_blocks(arrived[:, : 2 * width], "tp") + ring_blocks(arrived[:, 2 * width :], "etp")
    )

    far = ring_gather(stacked[:2], "etp") + ring_gather(stacked[2:], "tp")
    early = lax.optimization_barrier([far[q][:3] for q in range(4)])
    rest, early_a, early_b = first_sums(early, gate_weight, up_weight)
    late = lax.optimization_barrier([far[q][3] for q in range(4)])
    late_rows, over = last_sums(late, rest, gate_weight, up_weight, down_weight)
    slots, hidden = experts * cap, gate_weight.shape[2]
    ends = late_rows.reshape(7, slots, hidden)

    def with_ends(rows_in, at):
        blocks = rows_in.reshape(3, 4, slots, hidden)
        return [
            jnp.concatenate([blocks[j, :3], ends[at + j][None]], axis=0).reshape(
                4 * slots, hidden
            )
            for j in range(3)
        ]

    inner_a, inner_b = with_ends(early_a, 4), with_ends(early_b, 0)
    inner_a, inner_b, _ = lax.optimization_barrier((inner_a, inner_b, over))
    direct = down_terms([inner_a[1], inner_a[2], inner_b[1], inner_b[2]], down_weight)
    inner_a, inner_b, _ = lax.optimization_barrier((inner_a, inner_b, direct))
    passed = down_terms([inner_a[2], inner_a[1], inner_b[2], inner_b[1]], down_weight)
    kept_terms = down_terms([inner_a[0], inner_a[0], inner_b[0], inner_b[0]], down_weight)
    returned = []
    for half, (first, second) in enumerate((("tp", "etp"), ("etp", "tp"))):
        q0, q1 = 2 * half, 2 * half + 1
        over_lo, over_hi = shift(over[q0], second, 1), shift(over[q1], second, -1)
        far_sum_lo, far_sum_hi = add(passed[q0], over_lo), add(passed[q1], over_hi)
        next_lo, _ = lax.optimization_barrier((direct[q0], over_hi))
        next_hi, _ = lax.optimization_barrier((direct[q1], over_lo))
        got_lo, got_hi = shift(next_lo, second, -1), shift(next_hi, second, 1)
        far_sum_lo, _ = lax.optimization_barrier((far_sum_lo, got_hi))
        far_sum_hi, _ = lax.optimization_barrier((far_sum_hi, got_lo))
        last_lo = shift(far_sum_lo, second, 1)
        last_hi = shift(far_sum_hi, second, -1)
        blocks = merge_terms(
            (kept_terms[q0], got_lo, last_lo), (kept_terms[q1], got_hi, last_hi)
        )
        returned.append(ring_sum(*blocks, first).astype(jnp.bfloat16))
    outs = jnp.concatenate(returned, axis=1)
    pieces = [outs[d * rows_step : (d + 1) * rows_step] for d in range(steps)]
    pieces = [pieces[0]] + [shift(pieces[d], "ep", -2 * d) for d in range(1, steps)]
    expert_rows = jnp.concatenate(pieces, axis=0)
    both = jnp.dot(hi, expert_rows, preferred_element_type=jnp.float32) + jnp.dot(
        lo, expert_rows, preferred_element_type=jnp.float32
    )
    theirs = swap_core(both[moe_rows:].astype(jnp.bfloat16))
    mixed = (state + both[:moe_rows] + theirs.astype(jnp.float32)).astype(jnp.bfloat16)
    return (attention, mixed.reshape(1, 1, moe_rows, model))


def solution(mesh):
    return jax.shard_map(
        shards,
        mesh=mesh,
        in_specs=(
            P(("ep", "etp"), "tp"),
            P(("ep", "etp"), "tp"),
            P(("ep", "etp"), "tp"),
            P(("ep", "etp"), "tp", None, None),
            P(),
            P("tp", "etp"),
            P("ep", None, ("tp", "etp")),
            P("ep", None, ("tp", "etp")),
            P("ep", ("tp", "etp"), None),
            P(("ep", "etp"), "tp", None, None),
            P(("ep", "etp"), "tp", None, None),
        ),
        out_specs=(P(("ep", "etp"), "tp"), P(("ep", "etp"), "tp", None, None)),
        check_vma=False,
    )
```

```python
import functools
import math

import jax
import jax.numpy as jnp
from jax import lax
from jax.experimental import pallas as pl
from jax.experimental.pallas import tpu as pltpu
from jax.sharding import PartitionSpec as P

HD = 128


def route_slots(ids, experts):
    tokens, top = ids.shape
    flat = ids.reshape(-1)
    hot = (flat[:, None] == jnp.arange(experts, dtype=jnp.int32)[None, :]).astype(jnp.int32)
    rank = jnp.cumsum(hot, axis=0) - hot
    return jnp.sum(rank * hot, axis=1).reshape(tokens, top)


def split_bf16(x):
    hi = x.astype(jnp.bfloat16)
    lo = (x - hi.astype(jnp.float32)).astype(jnp.bfloat16)
    return hi, lo


def shift(x, axis, by):
    n = lax.axis_size(axis)
    return lax.ppermute(x, axis, [(i, (i + by) % n) for i in range(n)])


def swap_core(x):
    n = lax.axis_size("ep")
    return lax.ppermute(x, "ep", [(i, i ^ 1) for i in range(n)])


def pair_places(ids, side, cap, experts):
    me = lax.axis_index("ep")
    chip = (ids // 2 - me // 2) % (experts // 2)
    place = chip * (2 * cap) + side * cap + route_slots(ids, experts)
    return jnp.where(ids % 2 == me % 2, place, -1)


def after(x, earlier):
    return lax.optimization_barrier((x, earlier))[0]


def ring_gather(halves, axis):
    lo, hi = halves
    left_lo, right_hi = shift(lo, axis, 1), shift(hi, axis, -1)
    left_hi, right_lo = shift(after(hi, left_lo), axis, 1), shift(after(lo, right_hi), axis, -1)
    far_lo = shift(after(left_lo, left_hi), axis, 1)
    far_hi = shift(after(right_hi, right_lo), axis, -1)
    return (lo, left_lo, right_lo, far_lo), (hi, left_hi, right_hi, far_hi)


def add(*terms):
    return sum(t.astype(jnp.float32) for t in terms).astype(jnp.bfloat16)


def ring_sum(own, left, right, far, axis):
    half = own.shape[1] // 2
    over_lo = shift(far[:, :half], axis, 1)
    over_hi = shift(far[:, half:], axis, -1)
    to_right = jnp.concatenate([add(right[:, :half], over_lo), right[:, half:]], axis=1)
    to_left = jnp.concatenate([left[:, :half], add(left[:, half:], over_hi)], axis=1)
    terms = (own, shift(to_right, axis, 1), shift(to_left, axis, -1))
    return sum(t.astype(jnp.float32) for t in terms)


def ring_blocks(x, axis):
    half = x.shape[1] // 2
    left, right = shift(x, axis, 1), shift(x, axis, -1)
    return x, left, right, shift(left[:, :half], axis, 1), shift(right[:, half:], axis, -1)


def gather_direct(x, axis, step=1):
    return (
        x,
        shift(x, axis, step),
        shift(x, axis, -step),
        shift(x, axis, 2 * step),
    )


OFFSETS = (0, -1, 1, 2)


MIB = 2**20


def attend_kernel(scale, places_ref, q_ref, *refs):
    keys, vals = refs[:4], refs[4:8]
    outs, (diff_ref, top_ref, sum_ref, acc_ref) = refs[8:10], refs[10:]
    depth, width = q_ref.shape
    rows = outs[0].shape[0]
    half = width // 2
    mine, other = places_ref[32], places_ref[33]
    low, high = jnp.minimum(mine, other), jnp.maximum(mine, other)
    top_ref[...] = jnp.full_like(top_ref, -1e20)
    sum_ref[...] = jnp.zeros_like(sum_ref)
    acc_ref[...] = jnp.zeros_like(acc_ref)
    for n, block in enumerate((mine, other)):
        col = lax.broadcasted_iota(jnp.int32, (rows, half), 1) % rows
        row = lax.broadcasted_iota(jnp.int32, (rows, half), 0)
        diff_ref[:, n * half : (n + 1) * half] = row - col - block * rows

    def line(i, masked):
        at = [places_ref[i * 8 + n] for n in range(8)]
        q = q_ref[...]
        scores = []
        for j in range(4):
            k = keys[i][j * 2 * rows : (j + 1) * 2 * rows, :]
            s = jnp.dot(k, q, preferred_element_type=jnp.float32) * scale
            if masked:
                s = jnp.concatenate(
                    [
                        jnp.where(
                            diff_ref[...] <= -at[2 * j + n] * rows,
                            s[n * rows : (n + 1) * rows],
                            -1e30,
                        )
                        for n in range(2)
                    ],
                    axis=0,
                )
            scores.append(s)
        old = top_ref[...]
        new = old
        for s in scores:
            new = jnp.maximum(new, jnp.max(s, axis=0, keepdims=True))
        carry = jnp.exp2(old - new)
        total, acc = sum_ref[...] * carry, acc_ref[...] * carry
        for j, s in enumerate(scores):
            p = jnp.exp2(s - new)
            total += jnp.sum(p, axis=0, keepdims=True)
            acc += jnp.dot(
                vals[j][i * depth : (i + 1) * depth, :],
                p.astype(jnp.bfloat16),
                preferred_element_type=jnp.float32,
            )
        top_ref[...], sum_ref[...], acc_ref[...] = new, total, acc

    for i in range(4):
        least = most = places_ref[i * 8]
        for n in range(1, 8):
            least = jnp.minimum(least, places_ref[i * 8 + n])
            most = jnp.maximum(most, places_ref[i * 8 + n])
        pl.when(most < low)(functools.partial(line, i, False))
        pl.when(jnp.logical_and(most >= low, least <= high))(functools.partial(line, i, True))

    done = acc_ref[...] / sum_ref[...]
    for n in range(2):
        for h in range(half // rows):
            at = n * half + h * rows
            outs[n][:, h * depth : (h + 1) * depth] = done[:, at : at + rows].T.astype(
                outs[n].dtype
            )


def attend(places, queries, keys, vals):
    depth = keys[0].shape[1]
    rows, width = queries[0].shape
    heads = width // depth
    turned = jnp.concatenate(
        [
            jnp.transpose(q.reshape(rows, heads, depth), (2, 1, 0)).reshape(depth, heads * rows)
            for q in queries
        ],
        axis=1,
    )
    vmem = pl.BlockSpec(memory_space=pltpu.VMEM)
    columns = 2 * heads * rows
    return pl.pallas_call(
        functools.partial(attend_kernel, math.log2(math.e) / math.sqrt(depth)),
        out_shape=[jax.ShapeDtypeStruct(q.shape, q.dtype) for q in queries],
        in_specs=[pl.BlockSpec(memory_space=pltpu.SMEM)] + [vmem] * 9,
        out_specs=[vmem] * 2,
        scratch_shapes=[
            pltpu.VMEM((rows, columns), jnp.int32),
            pltpu.VMEM((1, columns), jnp.float32),
            pltpu.VMEM((1, columns), jnp.float32),
            pltpu.VMEM((depth, columns), jnp.float32),
        ],
        compiler_params=pltpu.CompilerParams(vmem_limit_bytes=40 * MIB),
        cost_estimate=pl.CostEstimate(
            flops=4 * columns * 32 * rows * depth,
            bytes_accessed=4 * 32 * rows * depth,
            transcendentals=columns * 32 * rows,
        ),
    )(places, turned, *keys, *vals)


def stack_kernel(*refs):
    ins, outs = refs[:10], refs[10:]
    rows, cols = ins[0].shape
    for half in range(2):
        blocks = ins[5 * half : 5 * half + 5]
        for k in range(2):
            out = outs[2 * half + k]
            for j in range(3):
                out[j * rows : (j + 1) * rows, :] = blocks[j][
                    :, k * (cols // 2) : (k + 1) * (cols // 2)
                ]
            out[3 * rows :, :] = blocks[3 + k][...]


def stack_blocks(blocks):
    rows, cols = blocks[0].shape
    vmem = pl.BlockSpec(memory_space=pltpu.VMEM)
    return pl.pallas_call(
        stack_kernel,
        out_shape=[jax.ShapeDtypeStruct((4 * rows, cols // 2), blocks[0].dtype)] * 4,
        in_specs=[vmem] * 10,
        out_specs=[vmem] * 4,
        compiler_params=pltpu.CompilerParams(vmem_limit_bytes=12 * MIB),
    )(*blocks)


def swish_product(gate_v, up_v):
    return (gate_v / (1.0 + jnp.exp(-gate_v)) * up_v).astype(jnp.bfloat16)


def first_sums_kernel(*refs):
    blocks, (gate_ref, up_ref, rest_ref, in_a_ref, in_b_ref, total_ref) = refs[:12], refs[12:]
    step = pl.program_id(0)
    rows, hidden = blocks[0].shape[0], gate_ref.shape[-1]
    quarter = rows // 4

    @pl.when(step == 0)
    def _():
        total_ref[...] = jnp.zeros_like(total_ref)

    for part in range(4):

        @pl.when(step // 2 == part)
        def _(part=part):
            for j in range(3):
                x = blocks[3 * part + j][...]
                for n, weight in enumerate((gate_ref, up_ref)):
                    span = slice(n * hidden, (n + 1) * hidden)
                    y = jnp.dot(x, weight[0], preferred_element_type=jnp.float32)
                    if part < 2:
                        total_ref[j * rows : (j + 1) * rows, span] += y
                    else:
                        for i in range(4):
                            at = (i * 4 + j) * quarter
                            total_ref[at : at + quarter, span] += y[i * quarter : (i + 1) * quarter]

    @pl.when(step == 7)
    def _():
        in_a_ref[...] = jnp.zeros_like(in_a_ref)
        in_b_ref[...] = jnp.zeros_like(in_b_ref)
        rest_ref[:rows, :] = total_ref[3 * rows :, :]
        for i in range(3):
            at = (4 * i + 3) * quarter
            rest_ref[rows + i * quarter : rows + (i + 1) * quarter, :] = total_ref[
                at : at + quarter, :
            ]
            for j in range(3):
                at, to = (4 * i + j) * quarter, (4 * j + i) * quarter
                inner = swish_product(
                    total_ref[at : at + quarter, :hidden], total_ref[at : at + quarter, hidden:]
                )
                in_a_ref[at : at + quarter, :] = inner
                in_b_ref[to : to + quarter, :] = inner


def part_spec(part, rows, sub):
    return pl.BlockSpec((rows, sub), lambda g: (0, jnp.clip(g - 2 * part, 0, 1)))


def first_sums(blocks, gate, up):
    rows, width = blocks[0][0].shape
    hidden = gate.shape[2]
    sub = width // 2
    weight = pl.BlockSpec((1, sub, hidden), lambda g: (0, jnp.minimum(g, 7), 0))
    rest = 7 * rows // 4

    def fixed(r, c):
        return pl.BlockSpec((r, c), lambda g: (0, 0))

    return pl.pallas_call(
        first_sums_kernel,
        grid=(8,),
        out_shape=[
            jax.ShapeDtypeStruct((rest, 2 * hidden), jnp.float32),
            jax.ShapeDtypeStruct((3 * rows, hidden), jnp.bfloat16),
            jax.ShapeDtypeStruct((3 * rows, hidden), jnp.bfloat16),
        ],
        in_specs=[part_spec(part, rows, sub) for part in range(4) for _ in range(3)]
        + [weight, weight],
        out_specs=[fixed(rest, 2 * hidden), fixed(3 * rows, hidden), fixed(3 * rows, hidden)],
        scratch_shapes=[pltpu.VMEM((4 * rows, 2 * hidden), jnp.float32)],
        compiler_params=pltpu.CompilerParams(vmem_limit_bytes=56 * MIB),
    )(*[x for part in blocks for x in part], gate, up)


def last_sums_kernel(*refs):
    blocks, refs = refs[:4], refs[4:]
    rest_ref, gate_ref, up_ref, down_ref, late_ref = refs[:5]
    outs, (total_ref, far_a_ref, far_b_ref) = refs[5:9], refs[9:]
    step = pl.program_id(0)
    rows, hidden = blocks[0].shape[0], gate_ref.shape[-1]
    quarter = rows // 4

    @pl.when(step == 0)
    def _():
        total_ref[...] = rest_ref[...]

    for part in range(4):

        @pl.when(step // 2 == part)
        def _(part=part):
            x = blocks[part][...]
            for n, weight in enumerate((gate_ref, up_ref)):
                span = slice(n * hidden, (n + 1) * hidden)
                y = jnp.dot(x, weight[0], preferred_element_type=jnp.float32)
                if part < 2:
                    total_ref[:rows, span] += y
                else:
                    total_ref[rows:, span] += y[: 3 * quarter]
                    total_ref[3 * quarter : rows, span] += y[3 * quarter :]

    @pl.when(step == 7)
    def _():
        for i in range(7):
            at = i * quarter
            inner = swish_product(
                total_ref[at : at + quarter, :hidden], total_ref[at : at + quarter, hidden:]
            )
            late_ref[at : at + quarter, :] = inner
            if i < 4:
                far_a_ref[at : at + quarter, :] = inner
            if i > 2:
                to = (i - 4) % 4 * quarter
                far_b_ref[to : to + quarter, :] = inner

    for part in range(4):

        @pl.when(step == 8 + part)
        def _(part=part):
            x = (far_a_ref if part < 2 else far_b_ref)[...]
            outs[part][...] = jnp.dot(
                x, down_ref[0], preferred_element_type=jnp.float32
            ).astype(outs[part].dtype)


def last_sums(blocks, rest, gate, up, down):
    rows, width = blocks[0].shape
    hidden = gate.shape[2]
    sub = width // 2
    weight = pl.BlockSpec((1, sub, hidden), lambda g: (0, jnp.minimum(g, 7), 0))
    term = pl.BlockSpec((rows, width), lambda g: (0, 0))
    outs = pl.pallas_call(
        last_sums_kernel,
        grid=(12,),
        out_shape=[jax.ShapeDtypeStruct((rest.shape[0], hidden), jnp.bfloat16)]
        + [jax.ShapeDtypeStruct((rows, width), jnp.bfloat16)] * 4,
        in_specs=[part_spec(part, rows, sub) for part in range(4)]
        + [
            pl.BlockSpec(rest.shape, lambda g: (0, 0)),
            weight,
            weight,
            pl.BlockSpec((1, hidden, width), lambda g: (0, 0, jnp.clip(g - 8, 0, 3))),
        ],
        out_specs=[pl.BlockSpec((rest.shape[0], hidden), lambda g: (0, 0))] + [term] * 4,
        scratch_shapes=[
            pltpu.VMEM(rest.shape, jnp.float32),
            pltpu.VMEM((rows, hidden), jnp.bfloat16),
            pltpu.VMEM((rows, hidden), jnp.bfloat16),
        ],
        compiler_params=pltpu.CompilerParams(vmem_limit_bytes=58 * MIB),
    )(*blocks, rest, gate, up, down)
    return outs[0], outs[1:]


def down_kernel(*refs):
    xs, down_ref, outs = refs[:4], refs[4], refs[5:]
    for part in range(4):

        @pl.when(pl.program_id(0) == part)
        def _(part=part):
            outs[part][...] = jnp.dot(
                xs[part][...], down_ref[0], preferred_element_type=jnp.float32
            ).astype(outs[part].dtype)


def down_terms(xs, down):
    rows, hidden = xs[0].shape
    width = down.shape[2] // 4
    return pl.pallas_call(
        down_kernel,
        grid=(4,),
        out_shape=[jax.ShapeDtypeStruct((rows, width), jnp.bfloat16)] * 4,
        in_specs=[pl.BlockSpec((rows, hidden), lambda g: (0, 0))] * 4
        + [pl.BlockSpec((1, hidden, width), lambda g: (0, 0, g))],
        out_specs=[pl.BlockSpec((rows, width), lambda g: (0, 0))] * 4,
        compiler_params=pltpu.CompilerParams(vmem_limit_bytes=18 * MIB),
    )(*xs, down)


def merge_kernel(*refs):
    terms, outs = refs[:6], refs[6:]
    rows, cols = outs[0].shape
    for k in range(2):
        for j in range(4):
            span = slice(j * rows, (j + 1) * rows)
            a, b, c = (terms[3 * k + n][span, :].astype(jnp.float32) for n in range(3))
            outs[j][:, k * (cols // 2) : (k + 1) * (cols // 2)] = (a + b + c).astype(
                outs[j].dtype
            )


def merge_terms(lo, hi):
    rows, width = lo[0].shape
    vmem = pl.BlockSpec(memory_space=pltpu.VMEM)
    return pl.pallas_call(
        merge_kernel,
        out_shape=[jax.ShapeDtypeStruct((rows // 4, 2 * width), jnp.bfloat16)] * 4,
        in_specs=[vmem] * 6,
        out_specs=[vmem] * 4,
        compiler_params=pltpu.CompilerParams(vmem_limit_bytes=12 * MIB),
    )(*lo, *hi)


def shards(
    queries,
    keys,
    values,
    residual,
    norm_gain,
    out_weight,
    gate_weight,
    up_weight,
    down_weight,
    expert_ids,
    route_weights,
):
    n_tp = lax.axis_size("tp")
    n_ep = lax.axis_size("ep")
    n_etp = lax.axis_size("etp")
    tp, ep, etp = (lax.axis_index(name) for name in ("tp", "ep", "etp"))
    rows = queries.shape[0]
    chip, core = ep // 2, ep % 2
    half_q = queries.shape[1] // 2

    def halves(x):
        w = x.shape[1] // 2
        return jnp.where(core == 0, x[:, :w], x[:, w:]), jnp.where(core == 0, x[:, w:], x[:, :w])

    (own_k, other_k), (own_v, other_v), (own_q, other_q) = (
        halves(x) for x in (keys, values, queries)
    )
    swapped = swap_core(jnp.concatenate([other_k, other_v, other_q], axis=1))
    key_pair = jnp.concatenate([own_k, swapped[:, :HD]], axis=0)
    value_pair = jnp.concatenate([own_v, swapped[:, HD : 2 * HD]], axis=0).T
    other_q = swapped[:, 2 * HD :]
    tokens_dev = residual.shape[2]
    top = expert_ids.shape[-1]
    ids = expert_ids.reshape(tokens_dev, top)
    weights = route_weights.reshape(tokens_dev, top)
    routes = swap_core(jnp.concatenate([ids.astype(jnp.float32), weights], axis=1))
    key_pair, routes = lax.optimization_barrier((key_pair, routes))
    other_ids, other_weights = routes[:, :top].astype(jnp.int32), routes[:, top:]
    key_line = jnp.concatenate(gather_direct(key_pair, "etp"), axis=0)
    value_line = jnp.concatenate(gather_direct(value_pair, "ep", 2), axis=0)
    all_keys = gather_direct(key_line, "ep", 2)
    all_values = gather_direct(value_line, "etp")
    order = jnp.array(OFFSETS, jnp.int32)
    chips = (chip + order) % (n_ep // 2)
    depths = (etp + order) % n_etp
    cores = jnp.stack([core, 1 - core])
    places = (
        (2 * chips[:, None, None] + cores[None, None, :]) * n_etp + depths[None, :, None]
    ).reshape(-1)

    me = ep * n_etp + etp
    far_block = (ep + 1 - 2 * core) * n_etp + etp
    places = jnp.concatenate([places, jnp.stack([me, far_block])]).astype(jnp.int32)
    kept, lent = attend(places, (own_q, other_q), all_keys, all_values)

    def to_other_core(by):
        pairs = [
            (e * n_etp + z, (e ^ 1) * n_etp + (z + by) % n_etp)
            for e in range(n_ep)
            for z in range(n_etp)
        ]
        return lax.ppermute(lent, ("ep", "etp"), pairs)

    back, back_left, back_right = (to_other_core(by) for by in (0, 1, -1))
    back_all = (back, back_left, back_right, shift(back_right, "etp", -1))
    attention = jnp.concatenate(
        [jnp.where(core == 0, kept, back), jnp.where(core == 0, back, kept)], axis=1
    )
    near_weight = lax.dynamic_slice_in_dim(out_weight, core * half_q, half_q, 0)
    far_weight = lax.dynamic_slice_in_dim(out_weight, (1 - core) * half_q, half_q, 0)
    kept_left, kept_right = shift(kept, "etp", 1), shift(kept, "etp", -1)
    kept_all = (kept, kept_left, kept_right, shift(kept_left, "etp", 1))
    moe_rows = rows // n_tp
    cols = out_weight.shape[1]
    partial_proj = jnp.stack(
        [
            (
                jnp.dot(b, far_weight, preferred_element_type=jnp.float32)
                + jnp.dot(k, near_weight, preferred_element_type=jnp.float32)
            )
            .astype(jnp.bfloat16)
            .reshape(n_tp, moe_rows, cols)
            for b, k in zip(back_all, kept_all)
        ],
        axis=1,
    )

    def for_tp(by):
        at = (tp + by) % n_tp
        return lax.dynamic_slice_in_dim(partial_proj, at, 1, 0).reshape(n_etp * moe_rows, cols)

    summed = ring_sum(for_tp(0), for_tp(-1), for_tp(1), for_tp(2), "tp")
    summed = summed.astype(jnp.bfloat16).reshape(n_etp, moe_rows, cols)
    column_blocks = [summed[0]] + [
        shift(summed[j], "etp", OFFSETS[j]) for j in range(1, n_etp)
    ]
    sources = [(etp - OFFSETS[j]) % n_etp for j in range(n_etp)]
    projected = jnp.concatenate(
        [
            sum(
                jnp.where(sources[j] == q, column_blocks[j].astype(jnp.float32), 0.0)
                for j in range(n_etp)
            )
            for q in range(n_etp)
        ],
        axis=1,
    )
    model = n_etp * cols
    state = residual.reshape(moe_rows, model).astype(jnp.float32) + projected
    scale_rows = lax.rsqrt(jnp.mean(state * state, axis=-1, keepdims=True) + 1e-05)
    normed = (state * scale_rows * norm_gain).astype(jnp.bfloat16)
    experts = n_ep * gate_weight.shape[0]
    cap = max(2, min(moe_rows, 5 * moe_rows * top // (4 * experts)))
    place = jnp.concatenate(
        [pair_places(ids, 0, cap, experts), pair_places(other_ids, 1, cap, experts)], axis=0
    )
    match = place[:, :, None] == jnp.arange(experts * cap, dtype=jnp.int32)[None, None, :]
    dispatch = jnp.sum(match.astype(jnp.float32), axis=1).astype(jnp.bfloat16)
    pair_weights = jnp.concatenate([weights, other_weights], axis=0)
    combine = jnp.sum(jnp.where(match, pair_weights[:, :, None], 0.0), axis=1)
    hi, lo = split_bf16(combine)

    width = model // 4
    steps = n_ep // 2
    rows_step = 2 * cap
    pair = jnp.concatenate([normed, swap_core(normed)], axis=0)
    send = lax.dot_general(
        dispatch, pair, (((0,), (0,)), ((), ())), preferred_element_type=jnp.float32
    ).astype(jnp.bfloat16)
    pieces = [send[d * rows_step : (d + 1) * rows_step] for d in range(steps)]
    pieces = [pieces[0]] + [shift(pieces[d], "ep", 2 * d) for d in range(1, steps)]
    arrived = jnp.concatenate(pieces, axis=0)
    stacked = stack_blocks(
        ring_blocks(arrived[:, : 2 * width], "tp") + ring_blocks(arrived[:, 2 * width :], "etp")
    )

    far = ring_gather(stacked[:2], "etp") + ring_gather(stacked[2:], "tp")
    early = lax.optimization_barrier([far[q][:3] for q in range(4)])
    rest, early_a, early_b = first_sums(early, gate_weight, up_weight)
    late = lax.optimization_barrier([far[q][3] for q in range(4)])
    late_rows, over = last_sums(late, rest, gate_weight, up_weight, down_weight)
    early_a, early_b, _ = lax.optimization_barrier((early_a, early_b, late_rows))
    slots, hidden = experts * cap, gate_weight.shape[2]
    ends = late_rows.reshape(7, slots, hidden)

    def with_ends(rows_in, at):
        blocks = rows_in.reshape(3, 4, slots, hidden)
        return [
            jnp.concatenate([blocks[j, :3], ends[at + j][None]], axis=0).reshape(
                4 * slots, hidden
            )
            for j in range(3)
        ]

    inner_a, inner_b = with_ends(early_a, 4), with_ends(early_b, 0)
    inner_a, inner_b, _ = lax.optimization_barrier((inner_a, inner_b, over))
    direct = down_terms([inner_a[1], inner_a[2], inner_b[1], inner_b[2]], down_weight)
    inner_a, inner_b, _ = lax.optimization_barrier((inner_a, inner_b, direct))
    passed = down_terms([inner_a[2], inner_a[1], inner_b[2], inner_b[1]], down_weight)
    kept_terms = down_terms([inner_a[0], inner_a[0], inner_b[0], inner_b[0]], down_weight)
    returned = []
    for half, (first, second) in enumerate((("tp", "etp"), ("etp", "tp"))):
        q0, q1 = 2 * half, 2 * half + 1
        over_lo, over_hi = shift(over[q0], second, 1), shift(over[q1], second, -1)
        far_sum_lo, far_sum_hi = add(passed[q0], over_lo), add(passed[q1], over_hi)
        next_lo, _ = lax.optimization_barrier((direct[q0], over_hi))
        next_hi, _ = lax.optimization_barrier((direct[q1], over_lo))
        got_lo, got_hi = shift(next_lo, second, -1), shift(next_hi, second, 1)
        far_sum_lo, _ = lax.optimization_barrier((far_sum_lo, got_hi))
        far_sum_hi, _ = lax.optimization_barrier((far_sum_hi, got_lo))
        last_lo = shift(far_sum_lo, second, 1)
        last_hi = shift(far_sum_hi, second, -1)
        blocks = merge_terms(
            (kept_terms[q0], got_lo, last_lo), (kept_terms[q1], got_hi, last_hi)
        )
        returned.append(ring_sum(*blocks, first).astype(jnp.bfloat16))
    outs = jnp.concatenate(returned, axis=1)
    pieces = [outs[d * rows_step : (d + 1) * rows_step] for d in range(steps)]
    pieces = [pieces[0]] + [shift(pieces[d], "ep", -2 * d) for d in range(1, steps)]
    expert_rows = jnp.concatenate(pieces, axis=0)
    both = jnp.dot(hi, expert_rows, preferred_element_type=jnp.float32) + jnp.dot(
        lo, expert_rows, preferred_element_type=jnp.float32
    )
    theirs = swap_core(both[moe_rows:].astype(jnp.bfloat16))
    mixed = (state + both[:moe_rows] + theirs.astype(jnp.float32)).astype(jnp.bfloat16)
    return (attention, mixed.reshape(1, 1, moe_rows, model))


def solution(mesh):
    return jax.shard_map(
        shards,
        mesh=mesh,
        in_specs=(
            P(("ep", "etp"), "tp"),
            P(("ep", "etp"), "tp"),
            P(("ep", "etp"), "tp"),
            P(("ep", "etp"), "tp", None, None),
            P(),
            P("tp", "etp"),
            P("ep", None, ("tp", "etp")),
            P("ep", None, ("tp", "etp")),
            P("ep", ("tp", "etp"), None),
            P(("ep", "etp"), "tp", None, None),
            P(("ep", "etp"), "tp", None, None),
        ),
        out_specs=(P(("ep", "etp"), "tp"), P(("ep", "etp"), "tp", None, None)),
        check_vma=False,
    )
```

```python
import functools
import math

import jax
import jax.numpy as jnp
from jax import lax
from jax.experimental import pallas as pl
from jax.experimental.pallas import tpu as pltpu
from jax.sharding import PartitionSpec as P

HD = 128


def route_slots(ids, experts):
    tokens, top = ids.shape
    flat = ids.reshape(-1)
    hot = (flat[:, None] == jnp.arange(experts, dtype=jnp.int32)[None, :]).astype(jnp.int32)
    rank = jnp.cumsum(hot, axis=0) - hot
    return jnp.sum(rank * hot, axis=1).reshape(tokens, top)


def split_bf16(x):
    hi = x.astype(jnp.bfloat16)
    lo = (x - hi.astype(jnp.float32)).astype(jnp.bfloat16)
    return hi, lo


def shift(x, axis, by):
    n = lax.axis_size(axis)
    return lax.ppermute(x, axis, [(i, (i + by) % n) for i in range(n)])


def swap_core(x):
    n = lax.axis_size("ep")
    return lax.ppermute(x, "ep", [(i, i ^ 1) for i in range(n)])


def pair_places(ids, side, cap, experts):
    me = lax.axis_index("ep")
    chip = (ids // 2 - me // 2) % (experts // 2)
    place = chip * (2 * cap) + side * cap + route_slots(ids, experts)
    return jnp.where(ids % 2 == me % 2, place, -1)


def after(x, earlier):
    return lax.optimization_barrier((x, earlier))[0]


def ring_gather(halves, axis):
    lo, hi = halves
    left_lo, right_hi = shift(lo, axis, 1), shift(hi, axis, -1)
    left_hi, right_lo = shift(after(hi, left_lo), axis, 1), shift(after(lo, right_hi), axis, -1)
    far_lo = shift(after(left_lo, left_hi), axis, 1)
    far_hi = shift(after(right_hi, right_lo), axis, -1)
    return (lo, left_lo, right_lo, far_lo), (hi, left_hi, right_hi, far_hi)


def add(*terms):
    return sum(t.astype(jnp.float32) for t in terms).astype(jnp.bfloat16)


def ring_sum(own, left, right, far, axis):
    half = own.shape[1] // 2
    over_lo = shift(far[:, :half], axis, 1)
    over_hi = shift(far[:, half:], axis, -1)
    to_right = jnp.concatenate([add(right[:, :half], over_lo), right[:, half:]], axis=1)
    to_left = jnp.concatenate([left[:, :half], add(left[:, half:], over_hi)], axis=1)
    terms = (own, shift(to_right, axis, 1), shift(to_left, axis, -1))
    return sum(t.astype(jnp.float32) for t in terms)


def ring_blocks(x, axis):
    half = x.shape[1] // 2
    left, right = shift(x, axis, 1), shift(x, axis, -1)
    return x, left, right, shift(left[:, :half], axis, 1), shift(right[:, half:], axis, -1)


def gather_direct(x, axis, step=1):
    return (
        x,
        shift(x, axis, step),
        shift(x, axis, -step),
        shift(x, axis, 2 * step),
    )


OFFSETS = (0, -1, 1, 2)


MIB = 2**20


def attend_kernel(scale, places_ref, q_ref, *refs):
    keys, vals = refs[:4], refs[4:8]
    outs, (diff_ref, top_ref, sum_ref, acc_ref) = refs[8:10], refs[10:]
    depth, width = q_ref.shape
    rows = outs[0].shape[0]
    half = width // 2
    mine, other = places_ref[32], places_ref[33]
    low, high = jnp.minimum(mine, other), jnp.maximum(mine, other)
    top_ref[...] = jnp.full_like(top_ref, -1e20)
    sum_ref[...] = jnp.zeros_like(sum_ref)
    acc_ref[...] = jnp.zeros_like(acc_ref)
    for n, block in enumerate((mine, other)):
        col = lax.broadcasted_iota(jnp.int32, (rows, half), 1) % rows
        row = lax.broadcasted_iota(jnp.int32, (rows, half), 0)
        diff_ref[:, n * half : (n + 1) * half] = row - col - block * rows

    def line(i, masked):
        at = [places_ref[i * 8 + n] for n in range(8)]
        q = q_ref[...]
        scores = []
        for j in range(4):
            k = keys[i][j * 2 * rows : (j + 1) * 2 * rows, :]
            s = jnp.dot(k, q, preferred_element_type=jnp.float32) * scale
            if masked:
                s = jnp.concatenate(
                    [
                        jnp.where(
                            diff_ref[...] <= -at[2 * j + n] * rows,
                            s[n * rows : (n + 1) * rows],
                            -1e30,
                        )
                        for n in range(2)
                    ],
                    axis=0,
                )
            scores.append(s)
        old = top_ref[...]
        new = old
        for s in scores:
            new = jnp.maximum(new, jnp.max(s, axis=0, keepdims=True))
        carry = jnp.exp2(old - new)
        total, acc = sum_ref[...] * carry, acc_ref[...] * carry
        for j, s in enumerate(scores):
            p = jnp.exp2(s - new)
            total += jnp.sum(p, axis=0, keepdims=True)
            acc += jnp.dot(
                vals[j][i * depth : (i + 1) * depth, :],
                p.astype(jnp.bfloat16),
                preferred_element_type=jnp.float32,
            )
        top_ref[...], sum_ref[...], acc_ref[...] = new, total, acc

    for i in range(4):
        least = most = places_ref[i * 8]
        for n in range(1, 8):
            least = jnp.minimum(least, places_ref[i * 8 + n])
            most = jnp.maximum(most, places_ref[i * 8 + n])
        pl.when(most < low)(functools.partial(line, i, False))
        pl.when(jnp.logical_and(most >= low, least <= high))(functools.partial(line, i, True))

    done = acc_ref[...] / sum_ref[...]
    for n in range(2):
        for h in range(half // rows):
            at = n * half + h * rows
            outs[n][:, h * depth : (h + 1) * depth] = done[:, at : at + rows].T.astype(
                outs[n].dtype
            )


def attend(places, queries, keys, vals):
    depth = keys[0].shape[1]
    rows, width = queries[0].shape
    heads = width // depth
    turned = jnp.concatenate(
        [
            jnp.transpose(q.reshape(rows, heads, depth), (2, 1, 0)).reshape(depth, heads * rows)
            for q in queries
        ],
        axis=1,
    )
    vmem = pl.BlockSpec(memory_space=pltpu.VMEM)
    columns = 2 * heads * rows
    return pl.pallas_call(
        functools.partial(attend_kernel, math.log2(math.e) / math.sqrt(depth)),
        out_shape=[jax.ShapeDtypeStruct(q.shape, q.dtype) for q in queries],
        in_specs=[pl.BlockSpec(memory_space=pltpu.SMEM)] + [vmem] * 9,
        out_specs=[vmem] * 2,
        scratch_shapes=[
            pltpu.VMEM((rows, columns), jnp.int32),
            pltpu.VMEM((1, columns), jnp.float32),
            pltpu.VMEM((1, columns), jnp.float32),
            pltpu.VMEM((depth, columns), jnp.float32),
        ],
        compiler_params=pltpu.CompilerParams(vmem_limit_bytes=40 * MIB),
        cost_estimate=pl.CostEstimate(
            flops=4 * columns * 32 * rows * depth,
            bytes_accessed=4 * 32 * rows * depth,
            transcendentals=columns * 32 * rows,
        ),
    )(places, turned, *keys, *vals)


def stack_kernel(*refs):
    ins, outs = refs[:10], refs[10:]
    rows, cols = ins[0].shape
    for half in range(2):
        blocks = ins[5 * half : 5 * half + 5]
        for k in range(2):
            out = outs[2 * half + k]
            for j in range(3):
                out[j * rows : (j + 1) * rows, :] = blocks[j][
                    :, k * (cols // 2) : (k + 1) * (cols // 2)
                ]
            out[3 * rows :, :] = blocks[3 + k][...]


def stack_blocks(blocks):
    rows, cols = blocks[0].shape
    vmem = pl.BlockSpec(memory_space=pltpu.VMEM)
    return pl.pallas_call(
        stack_kernel,
        out_shape=[jax.ShapeDtypeStruct((4 * rows, cols // 2), blocks[0].dtype)] * 4,
        in_specs=[vmem] * 10,
        out_specs=[vmem] * 4,
        compiler_params=pltpu.CompilerParams(vmem_limit_bytes=12 * MIB),
    )(*blocks)


def swish_product(gate_v, up_v):
    return (gate_v / (1.0 + jnp.exp(-gate_v)) * up_v).astype(jnp.bfloat16)


def first_sums_kernel(*refs):
    blocks, (gate_ref, up_ref, rest_ref, in_a_ref, in_b_ref, total_ref) = refs[:12], refs[12:]
    step = pl.program_id(0)
    rows, hidden = blocks[0].shape[0], gate_ref.shape[-1]
    quarter = rows // 4

    @pl.when(step == 0)
    def _():
        total_ref[...] = jnp.zeros_like(total_ref)

    for part in range(4):

        @pl.when(step // 2 == part)
        def _(part=part):
            for j in range(3):
                x = blocks[3 * part + j][...]
                for n, weight in enumerate((gate_ref, up_ref)):
                    span = slice(n * hidden, (n + 1) * hidden)
                    y = jnp.dot(x, weight[0], preferred_element_type=jnp.float32)
                    if part < 2:
                        total_ref[j * rows : (j + 1) * rows, span] += y
                    else:
                        for i in range(4):
                            at = (i * 4 + j) * quarter
                            total_ref[at : at + quarter, span] += y[i * quarter : (i + 1) * quarter]

    @pl.when(step == 7)
    def _():
        in_a_ref[...] = jnp.zeros_like(in_a_ref)
        in_b_ref[...] = jnp.zeros_like(in_b_ref)
        rest_ref[:rows, :] = total_ref[3 * rows :, :]
        for i in range(3):
            at = (4 * i + 3) * quarter
            rest_ref[rows + i * quarter : rows + (i + 1) * quarter, :] = total_ref[
                at : at + quarter, :
            ]
            for j in range(3):
                at, to = (4 * i + j) * quarter, (4 * j + i) * quarter
                inner = swish_product(
                    total_ref[at : at + quarter, :hidden], total_ref[at : at + quarter, hidden:]
                )
                in_a_ref[at : at + quarter, :] = inner
                in_b_ref[to : to + quarter, :] = inner


def part_spec(part, rows, sub):
    return pl.BlockSpec((rows, sub), lambda g: (0, jnp.clip(g - 2 * part, 0, 1)))


def first_sums(blocks, gate, up):
    rows, width = blocks[0][0].shape
    hidden = gate.shape[2]
    sub = width // 2
    weight = pl.BlockSpec((1, sub, hidden), lambda g: (0, jnp.minimum(g, 7), 0))
    rest = 7 * rows // 4

    def fixed(r, c):
        return pl.BlockSpec((r, c), lambda g: (0, 0))

    return pl.pallas_call(
        first_sums_kernel,
        grid=(8,),
        out_shape=[
            jax.ShapeDtypeStruct((rest, 2 * hidden), jnp.float32),
            jax.ShapeDtypeStruct((3 * rows, hidden), jnp.bfloat16),
            jax.ShapeDtypeStruct((3 * rows, hidden), jnp.bfloat16),
        ],
        in_specs=[part_spec(part, rows, sub) for part in range(4) for _ in range(3)]
        + [weight, weight],
        out_specs=[fixed(rest, 2 * hidden), fixed(3 * rows, hidden), fixed(3 * rows, hidden)],
        scratch_shapes=[pltpu.VMEM((4 * rows, 2 * hidden), jnp.float32)],
        compiler_params=pltpu.CompilerParams(vmem_limit_bytes=56 * MIB),
    )(*[x for part in blocks for x in part], gate, up)


def last_sums_kernel(*refs):
    blocks, refs = refs[:4], refs[4:]
    rest_ref, gate_ref, up_ref, down_ref, late_ref = refs[:5]
    outs, (total_ref, far_a_ref, far_b_ref) = refs[5:9], refs[9:]
    step = pl.program_id(0)
    rows, hidden = blocks[0].shape[0], gate_ref.shape[-1]
    quarter = rows // 4

    @pl.when(step == 0)
    def _():
        total_ref[...] = rest_ref[...]

    for part in range(4):

        @pl.when(step // 2 == part)
        def _(part=part):
            x = blocks[part][...]
            for n, weight in enumerate((gate_ref, up_ref)):
                span = slice(n * hidden, (n + 1) * hidden)
                y = jnp.dot(x, weight[0], preferred_element_type=jnp.float32)
                if part < 2:
                    total_ref[:rows, span] += y
                else:
                    total_ref[rows:, span] += y[: 3 * quarter]
                    total_ref[3 * quarter : rows, span] += y[3 * quarter :]

    @pl.when(step == 7)
    def _():
        for i in range(7):
            at = i * quarter
            inner = swish_product(
                total_ref[at : at + quarter, :hidden], total_ref[at : at + quarter, hidden:]
            )
            late_ref[at : at + quarter, :] = inner
            if i < 4:
                far_a_ref[at : at + quarter, :] = inner
            if i > 2:
                to = (i - 4) % 4 * quarter
                far_b_ref[to : to + quarter, :] = inner

    for part in range(4):

        @pl.when(step == 8 + part)
        def _(part=part):
            x = (far_a_ref if part < 2 else far_b_ref)[...]
            outs[part][...] = jnp.dot(
                x, down_ref[0], preferred_element_type=jnp.float32
            ).astype(outs[part].dtype)


def last_sums(blocks, rest, gate, up, down):
    rows, width = blocks[0].shape
    hidden = gate.shape[2]
    sub = width // 2
    weight = pl.BlockSpec((1, sub, hidden), lambda g: (0, jnp.minimum(g, 7), 0))
    term = pl.BlockSpec((rows, width), lambda g: (0, 0))
    outs = pl.pallas_call(
        last_sums_kernel,
        grid=(12,),
        out_shape=[jax.ShapeDtypeStruct((rest.shape[0], hidden), jnp.bfloat16)]
        + [jax.ShapeDtypeStruct((rows, width), jnp.bfloat16)] * 4,
        in_specs=[part_spec(part, rows, sub) for part in range(4)]
        + [
            pl.BlockSpec(rest.shape, lambda g: (0, 0)),
            weight,
            weight,
            pl.BlockSpec((1, hidden, width), lambda g: (0, 0, jnp.clip(g - 8, 0, 3))),
        ],
        out_specs=[pl.BlockSpec((rest.shape[0], hidden), lambda g: (0, 0))] + [term] * 4,
        scratch_shapes=[
            pltpu.VMEM(rest.shape, jnp.float32),
            pltpu.VMEM((rows, hidden), jnp.bfloat16),
            pltpu.VMEM((rows, hidden), jnp.bfloat16),
        ],
        compiler_params=pltpu.CompilerParams(vmem_limit_bytes=58 * MIB),
    )(*blocks, rest, gate, up, down)
    return outs[0], outs[1:]


def down_kernel(*refs):
    xs, down_ref, outs = refs[:4], refs[4], refs[5:]
    for part in range(4):

        @pl.when(pl.program_id(0) == part)
        def _(part=part):
            outs[part][...] = jnp.dot(
                xs[part][...], down_ref[0], preferred_element_type=jnp.float32
            ).astype(outs[part].dtype)


def down_terms(xs, down):
    rows, hidden = xs[0].shape
    width = down.shape[2] // 4
    return pl.pallas_call(
        down_kernel,
        grid=(4,),
        out_shape=[jax.ShapeDtypeStruct((rows, width), jnp.bfloat16)] * 4,
        in_specs=[pl.BlockSpec((rows, hidden), lambda g: (0, 0))] * 4
        + [pl.BlockSpec((1, hidden, width), lambda g: (0, 0, g))],
        out_specs=[pl.BlockSpec((rows, width), lambda g: (0, 0))] * 4,
        compiler_params=pltpu.CompilerParams(vmem_limit_bytes=18 * MIB),
    )(*xs, down)


def merge_kernel(*refs):
    terms, outs = refs[:6], refs[6:]
    rows, cols = outs[0].shape
    for k in range(2):
        for j in range(4):
            span = slice(j * rows, (j + 1) * rows)
            a, b, c = (terms[3 * k + n][span, :].astype(jnp.float32) for n in range(3))
            outs[j][:, k * (cols // 2) : (k + 1) * (cols // 2)] = (a + b + c).astype(
                outs[j].dtype
            )


def merge_terms(lo, hi):
    rows, width = lo[0].shape
    vmem = pl.BlockSpec(memory_space=pltpu.VMEM)
    return pl.pallas_call(
        merge_kernel,
        out_shape=[jax.ShapeDtypeStruct((rows // 4, 2 * width), jnp.bfloat16)] * 4,
        in_specs=[vmem] * 6,
        out_specs=[vmem] * 4,
        compiler_params=pltpu.CompilerParams(vmem_limit_bytes=12 * MIB),
    )(*lo, *hi)


def shards(
    queries,
    keys,
    values,
    residual,
    norm_gain,
    out_weight,
    gate_weight,
    up_weight,
    down_weight,
    expert_ids,
    route_weights,
):
    n_tp = lax.axis_size("tp")
    n_ep = lax.axis_size("ep")
    n_etp = lax.axis_size("etp")
    tp, ep, etp = (lax.axis_index(name) for name in ("tp", "ep", "etp"))
    rows = queries.shape[0]
    chip, core = ep // 2, ep % 2
    half_q = queries.shape[1] // 2

    def halves(x):
        w = x.shape[1] // 2
        return jnp.where(core == 0, x[:, :w], x[:, w:]), jnp.where(core == 0, x[:, w:], x[:, :w])

    (own_k, other_k), (own_v, other_v), (own_q, other_q) = (
        halves(x) for x in (keys, values, queries)
    )
    swapped = swap_core(jnp.concatenate([other_k, other_v, other_q], axis=1))
    key_pair = jnp.concatenate([own_k, swapped[:, :HD]], axis=0)
    value_pair = jnp.concatenate([own_v, swapped[:, HD : 2 * HD]], axis=0).T
    other_q = swapped[:, 2 * HD :]
    tokens_dev = residual.shape[2]
    top = expert_ids.shape[-1]
    ids = expert_ids.reshape(tokens_dev, top)
    weights = route_weights.reshape(tokens_dev, top)
    routes = swap_core(jnp.concatenate([ids.astype(jnp.float32), weights], axis=1))
    key_pair, routes = lax.optimization_barrier((key_pair, routes))
    other_ids, other_weights = routes[:, :top].astype(jnp.int32), routes[:, top:]
    key_line = jnp.concatenate(gather_direct(key_pair, "etp"), axis=0)
    value_line = jnp.concatenate(gather_direct(value_pair, "ep", 2), axis=0)
    all_keys = gather_direct(key_line, "ep", 2)
    all_values = gather_direct(value_line, "etp")
    order = jnp.array(OFFSETS, jnp.int32)
    chips = (chip + order) % (n_ep // 2)
    depths = (etp + order) % n_etp
    cores = jnp.stack([core, 1 - core])
    places = (
        (2 * chips[:, None, None] + cores[None, None, :]) * n_etp + depths[None, :, None]
    ).reshape(-1)

    me = ep * n_etp + etp
    far_block = (ep + 1 - 2 * core) * n_etp + etp
    places = jnp.concatenate([places, jnp.stack([me, far_block])]).astype(jnp.int32)
    kept, lent = attend(places, (own_q, other_q), all_keys, all_values)

    def to_other_core(by):
        pairs = [
            (e * n_etp + z, (e ^ 1) * n_etp + (z + by) % n_etp)
            for e in range(n_ep)
            for z in range(n_etp)
        ]
        return lax.ppermute(lent, ("ep", "etp"), pairs)

    back, back_left, back_right = (to_other_core(by) for by in (0, 1, -1))
    back_all = (back, back_left, back_right, shift(back_right, "etp", -1))
    attention = jnp.concatenate(
        [jnp.where(core == 0, kept, back), jnp.where(core == 0, back, kept)], axis=1
    )
    near_weight = lax.dynamic_slice_in_dim(out_weight, core * half_q, half_q, 0)
    far_weight = lax.dynamic_slice_in_dim(out_weight, (1 - core) * half_q, half_q, 0)
    kept_left, kept_right = shift(kept, "etp", 1), shift(kept, "etp", -1)
    kept_all = (kept, kept_left, kept_right, shift(kept_left, "etp", 1))
    moe_rows = rows // n_tp
    cols = out_weight.shape[1]
    partial_proj = jnp.stack(
        [
            (
                jnp.dot(b, far_weight, preferred_element_type=jnp.float32)
                + jnp.dot(k, near_weight, preferred_element_type=jnp.float32)
            )
            .astype(jnp.bfloat16)
            .reshape(n_tp, moe_rows, cols)
            for b, k in zip(back_all, kept_all)
        ],
        axis=1,
    )

    def for_tp(by):
        at = (tp + by) % n_tp
        return lax.dynamic_slice_in_dim(partial_proj, at, 1, 0).reshape(n_etp * moe_rows, cols)

    summed = ring_sum(for_tp(0), for_tp(-1), for_tp(1), for_tp(2), "tp")
    summed = summed.astype(jnp.bfloat16).reshape(n_etp, moe_rows, cols)
    column_blocks = [summed[0]] + [
        shift(summed[j], "etp", OFFSETS[j]) for j in range(1, n_etp)
    ]
    sources = [(etp - OFFSETS[j]) % n_etp for j in range(n_etp)]
    projected = jnp.concatenate(
        [
            sum(
                jnp.where(sources[j] == q, column_blocks[j].astype(jnp.float32), 0.0)
                for j in range(n_etp)
            )
            for q in range(n_etp)
        ],
        axis=1,
    )
    model = n_etp * cols
    state = residual.reshape(moe_rows, model).astype(jnp.float32) + projected
    scale_rows = lax.rsqrt(jnp.mean(state * state, axis=-1, keepdims=True) + 1e-05)
    normed = (state * scale_rows * norm_gain).astype(jnp.bfloat16)
    experts = n_ep * gate_weight.shape[0]
    cap = max(2, min(moe_rows, 5 * moe_rows * top // (4 * experts)))
    place = jnp.concatenate(
        [pair_places(ids, 0, cap, experts), pair_places(other_ids, 1, cap, experts)], axis=0
    )
    match = place[:, :, None] == jnp.arange(experts * cap, dtype=jnp.int32)[None, None, :]
    dispatch = jnp.sum(match.astype(jnp.float32), axis=1).astype(jnp.bfloat16)
    pair_weights = jnp.concatenate([weights, other_weights], axis=0)
    combine = jnp.sum(jnp.where(match, pair_weights[:, :, None], 0.0), axis=1)
    hi, lo = split_bf16(combine)

    width = model // 4
    steps = n_ep // 2
    rows_step = 2 * cap
    pair = jnp.concatenate([normed, swap_core(normed)], axis=0)
    send = lax.dot_general(
        dispatch, pair, (((0,), (0,)), ((), ())), preferred_element_type=jnp.float32
    ).astype(jnp.bfloat16)
    pieces = [send[d * rows_step : (d + 1) * rows_step] for d in range(steps)]
    pieces = [pieces[0]] + [shift(pieces[d], "ep", 2 * d) for d in range(1, steps)]
    arrived = jnp.concatenate(pieces, axis=0)
    stacked = stack_blocks(
        ring_blocks(arrived[:, : 2 * width], "tp") + ring_blocks(arrived[:, 2 * width :], "etp")
    )

    far = ring_gather(stacked[:2], "etp") + ring_gather(stacked[2:], "tp")
    early = lax.optimization_barrier([far[q][:3] for q in range(4)])
    rest, early_a, early_b = first_sums(early, gate_weight, up_weight)
    late = lax.optimization_barrier([far[q][3] for q in range(4)])
    late_rows, over = last_sums(late, rest, gate_weight, up_weight, down_weight)
    early_a, early_b, _ = lax.optimization_barrier((early_a, early_b, late_rows))
    slots, hidden = experts * cap, gate_weight.shape[2]
    ends = late_rows.reshape(7, slots, hidden)

    def with_ends(rows_in, at):
        blocks = rows_in.reshape(3, 4, slots, hidden)
        return [
            jnp.concatenate([blocks[j, :3], ends[at + j][None]], axis=0).reshape(
                4 * slots, hidden
            )
            for j in range(3)
        ]

    inner_a, inner_b = with_ends(early_a, 4), with_ends(early_b, 0)
    inner_a, inner_b, _ = lax.optimization_barrier((inner_a, inner_b, over))
    direct = down_terms([inner_a[1], inner_a[2], inner_b[1], inner_b[2]], down_weight)
    inner_a, inner_b, _ = lax.optimization_barrier((inner_a, inner_b, direct))
    passed = down_terms([inner_a[2], inner_a[1], inner_b[2], inner_b[1]], down_weight)
    kept_terms = down_terms([inner_a[0], inner_a[0], inner_b[0], inner_b[0]], down_weight)
    returned = []
    for half, (first, second) in enumerate((("tp", "etp"), ("etp", "tp"))):
        q0, q1 = 2 * half, 2 * half + 1
        over_lo, over_hi = shift(over[q0], second, 1), shift(over[q1], second, -1)
        far_sum_lo, far_sum_hi = add(passed[q0], over_lo), add(passed[q1], over_hi)
        next_lo, _ = lax.optimization_barrier((direct[q0], over_hi))
        next_hi, _ = lax.optimization_barrier((direct[q1], over_lo))
        got_lo, got_hi = shift(next_lo, second, -1), shift(next_hi, second, 1)
        far_sum_lo, _ = lax.optimization_barrier((far_sum_lo, got_hi))
        far_sum_hi, _ = lax.optimization_barrier((far_sum_hi, got_lo))
        last_lo = shift(far_sum_lo, second, 1)
        last_hi = shift(far_sum_hi, second, -1)
        blocks = merge_terms(
            (kept_terms[q0], got_lo, last_lo), (kept_terms[q1], got_hi, last_hi)
        )
        returned.append(ring_sum(*blocks, first).astype(jnp.bfloat16))
    outs = jnp.concatenate(returned, axis=1)
    pieces = [outs[d * rows_step : (d + 1) * rows_step] for d in range(steps)]
    pieces = [pieces[0]] + [shift(pieces[d], "ep", -2 * d) for d in range(1, steps)]
    expert_rows = jnp.concatenate(pieces, axis=0)
    def weighted(rows_of):
        parts = jnp.concatenate([hi[rows_of], lo[rows_of]], axis=0)
        sums = jnp.dot(parts, expert_rows, preferred_element_type=jnp.float32)
        return sums[:moe_rows] + sums[moe_rows:]

    theirs = swap_core(weighted(slice(moe_rows, None)).astype(jnp.bfloat16))
    own_sums = weighted(slice(None, moe_rows))
    mixed = (state + own_sums + theirs.astype(jnp.float32)).astype(jnp.bfloat16)
    return (attention, mixed.reshape(1, 1, moe_rows, model))


def solution(mesh):
    return jax.shard_map(
        shards,
        mesh=mesh,
        in_specs=(
            P(("ep", "etp"), "tp"),
            P(("ep", "etp"), "tp"),
            P(("ep", "etp"), "tp"),
            P(("ep", "etp"), "tp", None, None),
            P(),
            P("tp", "etp"),
            P("ep", None, ("tp", "etp")),
            P("ep", None, ("tp", "etp")),
            P("ep", ("tp", "etp"), None),
            P(("ep", "etp"), "tp", None, None),
            P(("ep", "etp"), "tp", None, None),
        ),
        out_specs=(P(("ep", "etp"), "tp"), P(("ep", "etp"), "tp", None, None)),
        check_vma=False,
    )
```
